256 devices in a mesh: src: 8 (over y, core), tgt: 32 (over x, z).
Axes of the slice: x: 4, y: 4, z: 8, core: 2. Of those that a mesh axis runs over, the one named last changes fastest.
Arguments:
- source_features: bfloat16 [8192, 128], P('src'), may hold values from -20 to 20
- target_features: bfloat16 [32768, 128], P('tgt'), may hold values from -20 to 20
- source_logmass: float32 [8192], P('src'), may hold values from -1 to 1
- target_logmass: float32 [32768], P('tgt'), may hold values from -1 to 1
- teacher_rows: bfloat16 [32768, 1536], P('tgt'), may hold values from -6 to 6
Outputs:
- projected: bfloat16 [8192, 1536], P(('src', 'tgt'))
- source_potential: float32 [8192], P('src')
- target_potential: float32 [32768], P('tgt')
The draws below stay inside these ranges and needn't reach their ends.
All inputs are finite; a program needn't handle non-finite values.
Results may differ from the reference program's by a relative error of at most 0.0049.
Values sent between devices are 32-bit elements; how exact they have to be, the bound alone decides.
A program may use at most 64 MiB of HBM per device.

```python
import jax
import jax.numpy as jnp
from jax import lax

FEAT = 128
WIDTH = 1536
SRC_DEV = 1024
ITERS = 3
NS = 8192
NT = 32768


def feature_draw(key, rows):
    base = jnp.clip(jax.random.normal(key, (rows, FEAT), jnp.float32), -4.0, 4.0)
    return base


def draw_source_features(key, part):
    key = jax.random.fold_in(key, 1)
    return feature_draw(key, NS).astype(jnp.bfloat16)


def draw_target_features(key, part):
    key = jax.random.fold_in(key, 2)
    return feature_draw(key, NT).astype(jnp.bfloat16)


def steps_of(key, extent, shards, low, high):
    def one(axis_at, blocks):
        draws = jax.random.uniform(jax.random.fold_in(jax.random.fold_in(key, 6), axis_at), (blocks,), jnp.float32, low / len(shards), high / len(shards))
        return jnp.repeat(jnp.exp(draws), extent[axis_at] // blocks).reshape((-1,) + (1,) * (len(extent) - axis_at - 1))

    gain = one(*shards[0])
    for cut in shards[1:]:
        gain = gain * one(*cut)
    return gain


def gaussian(stream_key, extent, width, limit, pieces=(), dtype=jnp.bfloat16):
    loudness = steps_of(stream_key, extent, pieces, -0.22, 0.18) if pieces else 1.0
    array = jax.random.normal(stream_key, extent, jnp.float32) * width * loudness
    return jnp.minimum(jnp.maximum(array, -limit), limit).astype(dtype)


def setup_inputs(seed: int = 0) -> dict:
    splits = jax.random.split(jax.random.key(seed), 6)
    return {
        "source_features": draw_source_features(jax.random.fold_in(splits[5], 71), 0),
        "target_features": draw_target_features(jax.random.fold_in(splits[5], 71), 0),
        "source_logmass": jnp.clip(jax.random.uniform(splits[2], (NS,), jnp.float32, -1.0, 1.0) * steps_of(splits[2], (NS,), ((0, 8),), -0.4, 0.0), -1.0, 1.0),
        "target_logmass": jnp.clip(jax.random.uniform(splits[3], (NT,), jnp.float32, -1.0, 1.0) * steps_of(splits[3], (NT,), ((0, 32),), -0.4, 0.0), -1.0, 1.0),
        "teacher_rows": gaussian(splits[4], (NT, WIDTH), 1.0, 6.0, ((0, 32),)),
    }


EPS = 0.1


def costs(xs, ys):
    dots = jnp.dot(xs, ys.T, preferred_element_type=jnp.float32)
    xf = xs.astype(jnp.float32)
    yf = ys.astype(jnp.float32)
    nx = jnp.sum(xf * xf, axis=1)
    ny = jnp.sum(yf * yf, axis=1)
    return (nx[:, None] + ny[None, :] - 2.0 * dots) / FEAT


def reference(source_features, target_features, source_logmass, target_logmass, teacher_rows):
    blocks = NS // SRC_DEV
    feat_blocks = source_features.reshape(blocks, SRC_DEV, FEAT)
    mass_blocks = source_logmass.reshape(blocks, SRC_DEV)

    def row_lse(potential):
        def one(feats):
            scores = target_logmass[None, :] + (potential[None, :] - costs(feats, target_features)) / EPS
            peak = jnp.max(scores, axis=1)
            return peak + jnp.log(jnp.sum(jnp.exp(scores - peak[:, None]), axis=1))
        return lax.map(one, feat_blocks).reshape(NS)

    def col_lse(source_pot):
        pot_blocks = source_pot.reshape(blocks, SRC_DEV)

        def step(carry, items):
            peak, total = carry
            feats, mass, pot = items
            scores = mass[:, None] + (pot[:, None] - costs(feats, target_features)) / EPS
            local_peak = jnp.max(scores, axis=0)
            local_total = jnp.sum(jnp.exp(scores - local_peak[None, :]), axis=0)
            new_peak = jnp.maximum(peak, local_peak)
            total = total * jnp.exp(peak - new_peak) + local_total * jnp.exp(local_peak - new_peak)
            return (new_peak, total), None

        start = (jnp.full((NT,), -jnp.inf, jnp.float32), jnp.zeros((NT,), jnp.float32))
        (peak, total), _ = lax.scan(step, start, (feat_blocks, mass_blocks, pot_blocks))
        return peak + jnp.log(total)

    target_pot = jnp.zeros((NT,), jnp.float32)
    source_pot = jnp.zeros((NS,), jnp.float32)
    for step_index in range(ITERS):
        source_pot = -EPS * row_lse(target_pot)
        target_pot = -EPS * col_lse(source_pot)
    final_total = row_lse(target_pot).reshape(blocks, SRC_DEV)

    def project(items):
        feats, lse = items
        scores = target_logmass[None, :] + (target_pot[None, :] - costs(feats, target_features)) / EPS
        weights = jnp.exp(scores - lse[:, None]).astype(jnp.bfloat16)
        return jnp.dot(weights, teacher_rows, preferred_element_type=jnp.float32).astype(jnp.bfloat16)

    projected = lax.map(project, (feat_blocks, final_total)).reshape(NS, WIDTH)
    return projected, source_pot, target_pot
```

```python
import functools
import math

import jax
import jax.numpy as jnp
from jax import lax
from jax.experimental import pallas as pl
from jax.experimental.pallas import tpu as pltpu
from jax.sharding import PartitionSpec as P

MESH = pl.DeviceIdType.MESH
EPS = 0.1
LOG2E = math.log2(math.e)
LN2 = math.log(2.0)
NX, NY, NZ = 4, 4, 8
LANES = 128
TILE = 1024
BLK = TILE // LANES
ROWS = 32
CHUNKS = 12
A_CHUNKS = (0, 1, 2, 3, 4, 5, 6)
B_CHUNKS = (8, 9, 10, 11, 7)
PAIRS = (0, 8, 2, 10, 4, 6)


def kernel(feat, xs, ys, slm, tlm, rows_hbm, out, f_out, g_out,
           score, hcol, weights, teach, part, rbuf, cbuf, vec, tmp4, qbuf,
           xfar, xnear, asum, zfar, znear, bfar, bnear, bsum, bx, fin, rcol,
           load_sem, rs_sem, rr_sem, cs_sem, cr_sem, qs_sem, qr_sem,
           as_sem, ar_sem, zs_sem, zr_sem, bs_sem, br_sem, bxs_sem, bxr_sem):
    src = lax.axis_index("src")
    tgt = lax.axis_index("tgt")
    y, c = lax.div(src, 2), lax.rem(src, 2)
    x, z = lax.div(tgt, NZ), lax.rem(tgt, NZ)
    xi = [lax.rem(x + d, NX) for d in range(NX)]
    zi = [lax.rem(z + d, NZ) for d in range(NZ)]

    def at_tgt(dx, dz):
        return (src, xi[dx % NX] * NZ + zi[dz % NZ])

    def at_src(dy, dc):
        return (lax.rem(y + dy, NY) * 2 + lax.rem(c + dc, 2), tgt)

    def hops(d, n):
        return min(d, n - d)

    tgt_peers = sorted([(dx, dz) for dx in range(NX) for dz in range(NZ) if dx or dz],
                       key=lambda o: -hops(o[0], NX) - hops(o[1], NZ))
    src_peers = sorted([(dy, dc) for dy in range(NY) for dc in range(2) if dy or dc],
                       key=lambda o: -hops(o[0], NY) - 0.1 * o[1])

    load = pltpu.make_async_copy(rows_hbm, teach, load_sem)
    load.start()
    barrier = pltpu.get_barrier_semaphore()
    for o in tgt_peers:
        pl.semaphore_signal(barrier, inc=1, device_id=at_tgt(*o), device_id_type=MESH)
    for o in src_peers:
        pl.semaphore_signal(barrier, inc=1, device_id=at_src(*o), device_id_type=MESH)

    def remote(a, b, ssem, rsem, dev):
        pltpu.make_async_remote_copy(src_ref=a, dst_ref=b, send_sem=ssem, recv_sem=rsem,
                                     device_id=dev, device_id_type=MESH).start()

    def arrive(ref, sem):
        pltpu.make_async_copy(ref, ref, sem).wait()

    def row_exchange(e, value):
        rbuf[e, tgt] = value
        for o in tgt_peers:
            remote(rbuf.at[e, tgt], rbuf.at[e, tgt], rs_sem.at[e], rr_sem.at[e], at_tgt(*o))
        arrive(rbuf.at[e, pl.ds(0, 31)], rr_sem.at[e])
        return rbuf[e]

    def col_exchange(e, value):
        cbuf[e, src] = value
        for o in src_peers:
            remote(cbuf.at[e, src], cbuf.at[e, src], cs_sem.at[e], cr_sem.at[e], at_src(*o))
        arrive(cbuf.at[e, pl.ds(0, 7)], cr_sem.at[e])
        return cbuf[e]

    def lse2(parts):
        peak = jnp.max(parts, axis=0)
        return peak + jnp.log(jnp.sum(jnp.exp2(parts - peak), axis=0)) * LOG2E

    def col_form(row):
        return jnp.broadcast_to(row, (LANES, LANES)).T

    def lanes(k):
        return slice(k * LANES, (k + 1) * LANES)

    def fold(t):
        return t.reshape(LANES // 8, 8, LANES)

    slm2 = slm[...] * LOG2E
    tlm2 = tlm[...] * LOG2E
    norm_scale = LOG2E / (feat * EPS)
    for a in range(BLK):
        xf = xs[pl.ds(a * LANES, LANES), :].astype(jnp.float32)
        yf = ys[pl.ds(a * LANES, LANES), :].astype(jnp.float32)
        vec[0, pl.ds(a, 1), :] = jnp.sum((xf * xf).T, axis=0, keepdims=True)
        vec[1, pl.ds(a, 1), :] = jnp.sum((yf * yf).T, axis=0, keepdims=True)
    nx2 = vec[0] * norm_scale
    ny2 = vec[1] * norm_scale
    bias = tlm2 - ny2

    for a in range(BLK):
        d = lax.dot_general(xs[pl.ds(a * LANES, LANES), :], ys[...], (((1,), (1,)), ((), ())),
                            preferred_element_type=jnp.float32)
        e = d * (2.0 * norm_scale)
        score[a] = e
        t = [e[:, lanes(k)] + bias[k:k + 1, :] for k in range(BLK)]
        m = functools.reduce(jnp.maximum, t)
        m = jnp.max(m, axis=1, keepdims=True)
        s = functools.reduce(jnp.add, [jnp.exp2(v - m) for v in t])
        s = jnp.sum(s, axis=1, keepdims=True)
        lse = m + jnp.log(s) * LOG2E
        vec[2, pl.ds(a, 1), :] = jnp.broadcast_to(lse, (LANES, LANES)).T[0:1, :]
    pl.semaphore_wait(barrier, len(tgt_peers) + len(src_peers))
    row2 = lse2(row_exchange(0, vec[2]))

    h = slm2 - row2
    peaks = [jnp.full((8, LANES), -jnp.inf, jnp.float32)] * BLK
    for a in range(BLK):
        hc = col_form(h[a:a + 1, :])
        hcol[a] = hc
        for k in range(BLK):
            peaks[k] = jnp.maximum(peaks[k], jnp.max(fold(score[a, :, lanes(k)] + hc), axis=0))
    peaks = [jnp.max(p, axis=0, keepdims=True) for p in peaks]
    sums = [jnp.zeros((8, LANES), jnp.float32)] * BLK
    for a in range(BLK):
        hc = hcol[a]
        for k in range(BLK):
            sums[k] = sums[k] + jnp.sum(fold(jnp.exp2(score[a, :, lanes(k)] + hc - peaks[k])), axis=0)
    for k in range(BLK):
        total = jnp.sum(sums[k], axis=0, keepdims=True)
        vec[3, pl.ds(k, 1), :] = peaks[k] + jnp.log(total) * LOG2E
    col2 = lse2(col_exchange(0, vec[3]))

    tmass = jnp.exp(tlm[...])
    smass = jnp.exp(slm[...])
    for a in range(BLK):
        lc = col_form(row2[a:a + 1, :])
        acc = None
        for k in range(BLK):
            q = jnp.exp2(score[a, :, lanes(k)] - lc - col2[k:k + 1, :])
            score[a, :, lanes(k)] = q
            q = q * tmass[k:k + 1, :]
            acc = q if acc is None else acc + q
        vec[4, pl.ds(a, 1), :] = jnp.sum(acc.T, axis=0, keepdims=True)

    def row_step(v):
        for a in range(BLK):
            acc = None
            for k in range(BLK):
                q = score[a, :, lanes(k)] * v[k:k + 1, :]
                acc = q if acc is None else acc + q
            vec[4, pl.ds(a, 1), :] = jnp.sum(acc.T, axis=0, keepdims=True)

    def col_step(u):
        acc = [jnp.zeros((8, LANES), jnp.float32)] * BLK
        for a in range(BLK):
            uc = col_form(u[a:a + 1, :])
            for k in range(BLK):
                acc[k] = acc[k] + jnp.sum(fold(score[a, :, lanes(k)] * uc), axis=0)
        for k in range(BLK):
            vec[5, pl.ds(k, 1), :] = jnp.sum(acc[k], axis=0, keepdims=True)

    r = jnp.sum(row_exchange(1, vec[4]), axis=0)
    col_step(smass / r)
    cs = jnp.sum(col_exchange(1, vec[5]), axis=0)
    row_step(tmass / cs)
    r = jnp.sum(row_exchange(2, vec[4]), axis=0)
    f_out[...] = (nx2 - row2) * (EPS * LN2) - EPS * jnp.log(r)
    col_step(smass / r)
    cs = jnp.sum(col_exchange(2, vec[5]), axis=0)
    g_out[...] = (ny2 - col2) * (EPS * LN2) - EPS * jnp.log(cs)

    v = tmass / cs
    for a in range(BLK):
        acc = None
        for k in range(BLK):
            q = (score[a, :, lanes(k)] * v[k:k + 1, :]).astype(jnp.bfloat16)
            weights[pl.ds(a * LANES, LANES), lanes(k)] = q
            q = q.astype(jnp.float32)
            acc = q if acc is None else acc + q
        tmp4[a // 2, pl.ds(a % 2, 1), :] = jnp.sum(acc.T, axis=0, keepdims=True)
    load.wait()

    events = []

    def project(ch):
        p = jnp.dot(weights[...], teach[:, ch * LANES:(ch + 2) * LANES], preferred_element_type=jnp.float32)
        part[ch] = p[:, :LANES].reshape(NX, NZ, ROWS, LANES)
        part[ch + 1] = p[:, LANES:].reshape(NX, NZ, ROWS, LANES)

    lo, hi = pl.ds(0, 4), pl.ds(4, 4)
    xr, xl = at_tgt(1, 0), at_tgt(-1, 0)
    zr, zl = at_tgt(0, 1), at_tgt(0, -1)

    def a_start(i, ch):
        remote(part.at[ch, xi[2], lo], xfar.at[i, 0], as_sem.at[i], ar_sem.at[i, 0], xr)
        remote(part.at[ch, xi[2], hi], xfar.at[i, 1], as_sem.at[i], ar_sem.at[i, 1], xl)
        remote(part.at[ch, xi[1], hi], xnear.at[i, 0, hi], as_sem.at[i], ar_sem.at[i, 2], xr)
        remote(part.at[ch, xi[3], lo], xnear.at[i, 1, lo], as_sem.at[i], ar_sem.at[i, 3], xl)

    def a_pass(i, ch):
        arrive(xfar.at[i, 0], ar_sem.at[i, 0])
        part[ch, xi[1], lo] = part[ch, xi[1], lo] + xfar[i, 0]
        remote(part.at[ch, xi[1], lo], xnear.at[i, 0, lo], as_sem.at[i], ar_sem.at[i, 2], xr)
        arrive(xfar.at[i, 1], ar_sem.at[i, 1])
        part[ch, xi[3], hi] = part[ch, xi[3], hi] + xfar[i, 1]
        remote(part.at[ch, xi[3], hi], xnear.at[i, 1, hi], as_sem.at[i], ar_sem.at[i, 3], xl)

    def a_mid(i, ch):
        arrive(xnear.at[i, 0], ar_sem.at[i, 2])
        arrive(xnear.at[i, 1], ar_sem.at[i, 3])
        asum[i] = part[ch, x] + xnear[i, 0] + xnear[i, 1]
        remote(asum.at[i, zi[4], pl.ds(0, 16)], zfar.at[i, 0], zs_sem.at[i], zr_sem.at[i, 0, 0], zr)
        remote(asum.at[i, zi[4], pl.ds(16, 16)], zfar.at[i, 1], zs_sem.at[i], zr_sem.at[i, 1, 0], zl)

    def a_ring(i, step):
        for way, dev, dst in ((0, zr, zi[4 - step]), (1, zl, zi[4 + step])):
            if step == 1:
                arrive(zfar.at[i, way], zr_sem.at[i, way, 0])
                half = pl.ds(16 * way, 16)
                asum[i, dst, half] = asum[i, dst, half] + zfar[i, way]
            else:
                arrive(znear.at[i, way, step - 2], zr_sem.at[i, way, step - 1])
                asum[i, dst] = asum[i, dst] + znear[i, way, step - 2]
            remote(asum.at[i, dst], znear.at[i, way, step - 1], zs_sem.at[i], zr_sem.at[i, way, step], dev)

    def a_end(i, ch):
        arrive(znear.at[i, 0, 2], zr_sem.at[i, 0, 3])
        arrive(znear.at[i, 1, 2], zr_sem.at[i, 1, 3])
        fin[ch] = asum[i, z] + znear[i, 0, 2] + znear[i, 1, 2]

    ends = (pl.ds(0, 2), pl.ds(2, 2))

    def b_start(i, ch):
        for way, dev, near in ((0, zr, zi[3]), (1, zl, zi[5])):
            own = 1 - way
            remote(part.at[ch, ends[way], zi[4]], bfar.at[i, way], bs_sem.at[i], br_sem.at[i, way, 0], dev)
            remote(part.at[ch, ends[own], near], bnear.at[i, way, 0, ends[own]], bs_sem.at[i], br_sem.at[i, way, 1], dev)

    def b_ring(i, ch, step):
        for way, dev, dst in ((0, zr, zi[4 - step]), (1, zl, zi[4 + step])):
            if step == 1:
                arrive(bfar.at[i, way], br_sem.at[i, way, 0])
                part[ch, ends[way], dst] = part[ch, ends[way], dst] + bfar[i, way]
                remote(part.at[ch, ends[way], dst], bnear.at[i, way, 0, ends[way]], bs_sem.at[i], br_sem.at[i, way, 1], dev)
            else:
                arrive(bnear.at[i, way, step - 2], br_sem.at[i, way, step - 1])
                part[ch, :, dst] = part[ch, :, dst] + bnear[i, way, step - 2]
                remote(part.at[ch, :, dst], bnear.at[i, way, step - 1], bs_sem.at[i], br_sem.at[i, way, step], dev)

    def b_mid(i, ch):
        arrive(bnear.at[i, 0, 2], br_sem.at[i, 0, 3])
        arrive(bnear.at[i, 1, 2], br_sem.at[i, 1, 3])
        bsum[i] = part[ch, :, z] + bnear[i, 0, 2] + bnear[i, 1, 2]
        for d in (2, 1, 3):
            remote(bsum.at[i, xi[d]], bx.at[i, d - 1], bxs_sem.at[i], bxr_sem.at[i], at_tgt(d, 0))

    def b_end(i, ch):
        arrive(bx.at[i], bxr_sem.at[i])
        fin[ch] = bsum[i, x] + bx[i, 0] + bx[i, 1] + bx[i, 2]

    def q_start():
        for d in (2, 1, 3):
            remote(tmp4.at[xi[d]], qbuf.at[d - 1], qs_sem.at[0], qr_sem.at[0], at_tgt(d, 0))

    def q_mid():
        arrive(qbuf.at[pl.ds(0, 3)], qr_sem.at[0])
        tmp4[x] = tmp4[x] + qbuf[0] + qbuf[1] + qbuf[2]
        for d in (4, 3, 5, 2, 6, 1, 7):
            remote(tmp4.at[x], qbuf.at[2 + d], qs_sem.at[1], qr_sem.at[1], at_tgt(0, d))

    def q_end():
        arrive(qbuf.at[pl.ds(3, 7)], qr_sem.at[1])
        total = tmp4[x]
        for d in range(7):
            total = total + qbuf[3 + d]
        rcol[0] = col_form(1.0 / total[0:1, :])
        rcol[1] = col_form(1.0 / total[1:2, :])

    for n, ch in enumerate(PAIRS):
        events.append((n * 0.8 - 1.0, functools.partial(project, ch)))
    events += [(-0.9, q_start), (8.0, q_mid), (16.0, q_end)]
    done = {ch: PAIRS.index(ch if ch in PAIRS else ch - 1) * 0.8 - 0.5 for ch in range(CHUNKS)}
    for i, ch in enumerate(A_CHUNKS):
        t0 = 4.2 * i
        events.append((max(done[ch], t0 - 3.0), functools.partial(a_start, i, ch)))
        events.append((t0 + 4.5, functools.partial(a_pass, i, ch)))
        events.append((t0 + 8.7, functools.partial(a_mid, i, ch)))
        for step in (1, 2, 3):
            events.append((t0 + 8.8 + 2.5 * step, functools.partial(a_ring, i, step)))
        events.append((t0 + 19.0, functools.partial(a_end, i, ch)))
    for i, ch in enumerate(B_CHUNKS):
        t0 = 6.0 * i
        events.append((max(done[ch], t0 - 3.0), functools.partial(b_start, i, ch)))
        for step in (1, 2, 3):
            events.append((t0 + 0.1 + 3.5 * step, functools.partial(b_ring, i, ch, step)))
        events.append((t0 + 14.1, functools.partial(b_mid, i, ch)))
        events.append((t0 + 18.0, functools.partial(b_end, i, ch)))
    for _, event in sorted(events, key=lambda e: e[0]):
        event()

    scale = rcol[lax.div(z, 4), pl.ds(lax.rem(z, 4) * ROWS, ROWS), :]
    for ch in range(CHUNKS):
        out[:, lanes(ch)] = (fin[ch] * scale).astype(jnp.bfloat16)

    for e in range(3):
        arrive(rbuf.at[e, pl.ds(0, 31)], rs_sem.at[e])
        arrive(cbuf.at[e, pl.ds(0, 7)], cs_sem.at[e])
    arrive(qbuf.at[pl.ds(0, 3)], qs_sem.at[0])
    arrive(qbuf.at[pl.ds(3, 7)], qs_sem.at[1])
    for i, ch in enumerate(A_CHUNKS):
        arrive(part.at[ch, pl.ds(0, 3)], as_sem.at[i])
        arrive(asum.at[i, pl.ds(0, 7)], zs_sem.at[i])
    for i, ch in enumerate(B_CHUNKS):
        arrive(part.at[ch, :, pl.ds(0, 7)], bs_sem.at[i])
        arrive(bx.at[i], bxs_sem.at[i])


def body(source_features, target_features, source_logmass, target_logmass, teacher_rows):
    na, nb = len(A_CHUNKS), len(B_CHUNKS)
    f32 = jnp.float32
    vmem = pl.BlockSpec(memory_space=pltpu.VMEM)
    dma = pltpu.SemaphoreType.DMA
    projected, f, g = pl.pallas_call(
        functools.partial(kernel, source_features.shape[1]),
        out_shape=(
            jax.ShapeDtypeStruct((ROWS, CHUNKS * LANES), jnp.bfloat16),
            jax.ShapeDtypeStruct((BLK, LANES), f32),
            jax.ShapeDtypeStruct((BLK, LANES), f32),
        ),
        in_specs=[vmem, vmem, vmem, vmem, pl.BlockSpec(memory_space=pl.ANY)],
        out_specs=(vmem, vmem, vmem),
        scratch_shapes=[
            pltpu.VMEM((BLK, LANES, TILE), f32),
            pltpu.VMEM((BLK, LANES, LANES), f32),
            pltpu.VMEM((TILE, TILE), jnp.bfloat16),
            pltpu.VMEM((TILE, CHUNKS * LANES), jnp.bfloat16),
            pltpu.VMEM((CHUNKS, NX, NZ, ROWS, LANES), f32),
            pltpu.VMEM((3, 32, BLK, LANES), f32),
            pltpu.VMEM((3, 8, BLK, LANES), f32),
            pltpu.VMEM((6, BLK, LANES), f32),
            pltpu.VMEM((NX, 2, LANES), f32),
            pltpu.VMEM((10, 2, LANES), f32),
            pltpu.VMEM((na, 2, 4, ROWS, LANES), f32),
            pltpu.VMEM((na, 2, NZ, ROWS, LANES), f32),
            pltpu.VMEM((na, NZ, ROWS, LANES), f32),
            pltpu.VMEM((na, 2, ROWS // 2, LANES), f32),
            pltpu.VMEM((na, 2, 3, ROWS, LANES), f32),
            pltpu.VMEM((nb, 2, 2, ROWS, LANES), f32),
            pltpu.VMEM((nb, 2, 3, NX, ROWS, LANES), f32),
            pltpu.VMEM((nb, NX, ROWS, LANES), f32),
            pltpu.VMEM((nb, 3, ROWS, LANES), f32),
            pltpu.VMEM((CHUNKS, ROWS, LANES), f32),
            pltpu.VMEM((2, LANES, LANES), f32),
            dma, dma((3,)), dma((3,)), dma((3,)), dma((3,)), dma((2,)), dma((2,)),
            dma((na,)), dma((na, 4)), dma((na,)), dma((na, 2, 4)),
            dma((nb,)), dma((nb, 2, 4)), dma((nb,)), dma((nb,)),
        ],
        compiler_params=pltpu.CompilerParams(
            collective_id=0, has_side_effects=True, vmem_limit_bytes=48 * 1024 * 1024),
    )(source_features, target_features, source_logmass.reshape(BLK, LANES),
      target_logmass.reshape(BLK, LANES), teacher_rows)
    return projected, f.reshape(TILE), g.reshape(TILE)


def solution(mesh):
    in_specs = (P("src", None), P("tgt", None), P("src"), P("tgt"), P("tgt", None))
    out_specs = (P(("src", "tgt"), None), P("src"), P("tgt"))
    return jax.shard_map(body, mesh=mesh, in_specs=in_specs, out_specs=out_specs, check_vma=False)
```

```python
import functools
import math

import jax
import jax.numpy as jnp
from jax import lax
from jax.experimental import pallas as pl
from jax.experimental.pallas import tpu as pltpu
from jax.sharding import PartitionSpec as P

MESH = pl.DeviceIdType.MESH
EPS = 0.1
LOG2E = math.log2(math.e)
LN2 = math.log(2.0)
NX, NY, NZ = 4, 4, 8
LANES = 128
TILE = 1024
BLK = TILE // LANES
ROWS = 32
CHUNKS = 12
KINDS = "BABABAABABAB"
SCHEDULE = (
    ("s", 0), ("s", 1), ("s", 2), ("s", 3), ("s", 4), ("br", 0, 1, 0), ("br", 0, 1, 1), ("s", 5), ("s", 6),
    ("ap", 1, 0), ("ap", 1, 1), ("s", 7), ("qm", 0), ("br", 2, 1, 0), ("br", 2, 1, 1), ("s", 8), ("br", 4, 1, 0),
    ("br", 4, 1, 1), ("s", 9), ("s", 10), ("ap", 3, 0), ("ap", 3, 1), ("br", 0, 2, 0), ("br", 0, 2, 1),
    ("br", 7, 1, 0), ("br", 7, 1, 1), ("s", 11), ("br", 2, 2, 0), ("br", 2, 2, 1), ("ap", 5, 0), ("ap", 5, 1),
    ("br", 4, 2, 0), ("br", 4, 2, 1), ("br", 9, 1, 0), ("br", 9, 1, 1), ("ap", 6, 0), ("ap", 6, 1), ("br", 0, 3, 0),
    ("br", 0, 3, 1), ("br", 7, 2, 0), ("br", 7, 2, 1), ("br", 11, 1, 0), ("br", 11, 1, 1), ("am", 1),
    ("br", 2, 3, 0), ("br", 2, 3, 1), ("ap", 8, 0), ("ap", 8, 1), ("br", 4, 3, 0), ("br", 4, 3, 1), ("br", 9, 2, 0),
    ("br", 9, 2, 1), ("ap", 10, 0), ("ap", 10, 1), ("bm", 0), ("br", 7, 3, 0), ("br", 7, 3, 1), ("br", 11, 2, 0),
    ("br", 11, 2, 1), ("ar", 1, 1, 0), ("ar", 1, 1, 1), ("am", 3), ("bm", 2), ("am", 5), ("bm", 4), ("am", 6),
    ("br", 9, 3, 0), ("br", 9, 3, 1), ("am", 8), ("bm", 7), ("am", 10), ("qe", 0), ("be", 0), ("br", 11, 3, 0),
    ("br", 11, 3, 1), ("ar", 1, 2, 0), ("ar", 1, 2, 1), ("ar", 3, 1, 0), ("ar", 3, 1, 1), ("ar", 5, 1, 0),
    ("ar", 5, 1, 1), ("ar", 6, 1, 0), ("ar", 6, 1, 1), ("be", 2), ("be", 4), ("be", 7), ("bm", 9), ("ar", 8, 1, 0),
    ("ar", 8, 1, 1), ("ar", 10, 1, 0), ("ar", 10, 1, 1), ("bm", 11), ("ar", 1, 3, 0), ("ar", 1, 3, 1),
    ("ar", 3, 2, 0), ("ar", 3, 2, 1), ("be", 9), ("ar", 5, 2, 0), ("ar", 5, 2, 1), ("ar", 6, 2, 0), ("ar", 6, 2, 1),
    ("ar", 8, 2, 0), ("ar", 8, 2, 1), ("ar", 10, 2, 0), ("ar", 10, 2, 1), ("ae", 1), ("be", 11), ("ar", 3, 3, 0),
    ("ar", 3, 3, 1), ("ar", 5, 3, 0), ("ar", 5, 3, 1), ("ar", 6, 3, 0), ("ar", 6, 3, 1), ("ar", 8, 3, 0),
    ("ar", 8, 3, 1), ("ar", 10, 3, 0), ("ar", 10, 3, 1), ("ae", 3), ("ae", 5), ("ae", 6), ("ae", 8), ("ae", 10),
)


def chunks_of(kind):
    return [ch for ch in range(CHUNKS) if KINDS[ch] == kind]


def kernel(feat, xs_hbm, ys_hbm, slm_hbm, tlm_hbm, rows_hbm, out, f_out, g_out,
           xs, ys, slm, tlm, score, hcol, weights, teach, part, rbuf, cbuf, vec, tmp4, qbuf,
           xfar, xnear, asum, zfar, znear, bfar, bnear, bsum, bx, rcol,
           load_sem, in_sem, rs_sem, rr_sem, cs_sem, cr_sem, qs_sem, qr_sem,
           as_sem, ar_sem, zs_sem, zr_sem, bs_sem, br_sem, bxs_sem, bxr_sem):
    src = lax.axis_index("src")
    tgt = lax.axis_index("tgt")
    y, c = lax.div(src, 2), lax.rem(src, 2)
    x, z = lax.div(tgt, NZ), lax.rem(tgt, NZ)
    xi = [lax.rem(x + d, NX) for d in range(NX)]
    zi = [lax.rem(z + d, NZ) for d in range(NZ)]

    def at_tgt(dx, dz):
        return (src, xi[dx % NX] * NZ + zi[dz % NZ])

    def at_src(dy, dc):
        return (lax.rem(y + dy, NY) * 2 + lax.rem(c + dc, 2), tgt)

    def hops(d, n):
        return min(d, n - d)

    tgt_peers = sorted([(dx, dz) for dx in range(NX) for dz in range(NZ) if dx or dz],
                       key=lambda o: -hops(o[0], NX) - hops(o[1], NZ))
    src_peers = sorted([(dy, dc) for dy in range(NY) for dc in range(2) if dy or dc],
                       key=lambda o: -hops(o[0], NY) - 0.1 * o[1])

    loads = [pltpu.make_async_copy(a, b, in_sem.at[n]) for n, (a, b) in enumerate(
        ((ys_hbm, ys), (xs_hbm, xs), (slm_hbm, slm), (tlm_hbm, tlm)))]
    for copy in loads:
        copy.start()
    load = pltpu.make_async_copy(rows_hbm, teach, load_sem)
    load.start()
    barrier = pltpu.get_barrier_semaphore()
    for o in tgt_peers:
        pl.semaphore_signal(barrier, inc=1, device_id=at_tgt(*o), device_id_type=MESH)
    for o in src_peers:
        pl.semaphore_signal(barrier, inc=1, device_id=at_src(*o), device_id_type=MESH)

    def remote(a, b, ssem, rsem, dev):
        pltpu.make_async_remote_copy(src_ref=a, dst_ref=b, send_sem=ssem, recv_sem=rsem,
                                     device_id=dev, device_id_type=MESH).start()

    def arrive(ref, sem):
        pltpu.make_async_copy(ref, ref, sem).wait()

    def row_exchange(e, value):
        rbuf[e, tgt] = value
        for o in tgt_peers:
            remote(rbuf.at[e, tgt], rbuf.at[e, tgt], rs_sem.at[e], rr_sem.at[e], at_tgt(*o))
        arrive(rbuf.at[e, pl.ds(0, 31)], rr_sem.at[e])
        return rbuf[e]

    def col_exchange(e, value):
        cbuf[e, src] = value
        for o in src_peers:
            remote(cbuf.at[e, src], cbuf.at[e, src], cs_sem.at[e], cr_sem.at[e], at_src(*o))
        arrive(cbuf.at[e, pl.ds(0, 7)], cr_sem.at[e])
        return cbuf[e]

    def lse2(parts):
        peak = jnp.max(parts, axis=0)
        return peak + jnp.log(jnp.sum(jnp.exp2(parts - peak), axis=0)) * LOG2E

    def col_form(row):
        return jnp.broadcast_to(row, (LANES, LANES)).T

    def lanes(k):
        return slice(k * LANES, (k + 1) * LANES)

    def fold(t):
        return t.reshape(LANES // 8, 8, LANES)

    for copy in loads:
        copy.wait()
    slm2 = slm[...] * LOG2E
    tlm2 = tlm[...] * LOG2E
    norm_scale = LOG2E / (feat * EPS)
    for a in range(BLK):
        xf = xs[pl.ds(a * LANES, LANES), :].astype(jnp.float32)
        yf = ys[pl.ds(a * LANES, LANES), :].astype(jnp.float32)
        vec[0, pl.ds(a, 1), :] = jnp.sum((xf * xf).T, axis=0, keepdims=True)
        vec[1, pl.ds(a, 1), :] = jnp.sum((yf * yf).T, axis=0, keepdims=True)
    nx2 = vec[0] * norm_scale
    ny2 = vec[1] * norm_scale
    bias = tlm2 - ny2

    for a in range(BLK):
        d = lax.dot_general(xs[pl.ds(a * LANES, LANES), :], ys[...], (((1,), (1,)), ((), ())),
                            preferred_element_type=jnp.float32)
        e = d * (2.0 * norm_scale)
        score[a] = e
        t = [e[:, lanes(k)] + bias[k:k + 1, :] for k in range(BLK)]
        m = functools.reduce(jnp.maximum, t)
        m = jnp.max(m, axis=1, keepdims=True)
        s = functools.reduce(jnp.add, [jnp.exp2(v - m) for v in t])
        s = jnp.sum(s, axis=1, keepdims=True)
        lse = m + jnp.log(s) * LOG2E
        vec[2, pl.ds(a, 1), :] = jnp.broadcast_to(lse, (LANES, LANES)).T[0:1, :]
    pl.semaphore_wait(barrier, len(tgt_peers) + len(src_peers))
    row2 = lse2(row_exchange(0, vec[2]))

    h = slm2 - row2
    peaks = [jnp.full((8, LANES), -jnp.inf, jnp.float32)] * BLK
    for a in range(BLK):
        hc = col_form(h[a:a + 1, :])
        hcol[a] = hc
        for k in range(BLK):
            peaks[k] = jnp.maximum(peaks[k], jnp.max(fold(score[a, :, lanes(k)] + hc), axis=0))
    peaks = [jnp.max(p, axis=0, keepdims=True) for p in peaks]
    sums = [jnp.zeros((8, LANES), jnp.float32)] * BLK
    for a in range(BLK):
        hc = hcol[a]
        for k in range(BLK):
            sums[k] = sums[k] + jnp.sum(fold(jnp.exp2(score[a, :, lanes(k)] + hc - peaks[k])), axis=0)
    for k in range(BLK):
        total = jnp.sum(sums[k], axis=0, keepdims=True)
        vec[3, pl.ds(k, 1), :] = peaks[k] + jnp.log(total) * LOG2E
    col2 = lse2(col_exchange(0, vec[3]))

    tmass = jnp.exp(tlm[...])
    smass = jnp.exp(slm[...])
    for a in range(BLK):
        lc = col_form(row2[a:a + 1, :])
        acc = None
        for k in range(BLK):
            q = jnp.exp2(score[a, :, lanes(k)] - lc - col2[k:k + 1, :])
            score[a, :, lanes(k)] = q
            q = q * tmass[k:k + 1, :]
            acc = q if acc is None else acc + q
        vec[4, pl.ds(a, 1), :] = jnp.sum(acc.T, axis=0, keepdims=True)

    def row_step(v):
        for a in range(BLK):
            acc = None
            for k in range(BLK):
                q = score[a, :, lanes(k)] * v[k:k + 1, :]
                acc = q if acc is None else acc + q
            vec[4, pl.ds(a, 1), :] = jnp.sum(acc.T, axis=0, keepdims=True)

    def col_step(u):
        acc = [jnp.zeros((8, LANES), jnp.float32)] * BLK
        for a in range(BLK):
            uc = col_form(u[a:a + 1, :])
            for k in range(BLK):
                acc[k] = acc[k] + jnp.sum(fold(score[a, :, lanes(k)] * uc), axis=0)
        for k in range(BLK):
            vec[5, pl.ds(k, 1), :] = jnp.sum(acc[k], axis=0, keepdims=True)

    r = jnp.sum(row_exchange(1, vec[4]), axis=0)
    col_step(smass / r)
    cs = jnp.sum(col_exchange(1, vec[5]), axis=0)
    row_step(tmass / cs)
    r = jnp.sum(row_exchange(2, vec[4]), axis=0)
    f_out[...] = (nx2 - row2) * (EPS * LN2) - EPS * jnp.log(r)
    col_step(smass / r)
    cs = jnp.sum(col_exchange(2, vec[5]), axis=0)
    g_out[...] = (ny2 - col2) * (EPS * LN2) - EPS * jnp.log(cs)

    v = tmass / cs
    for a in range(BLK):
        acc = None
        for k in range(BLK):
            q = (score[a, :, lanes(k)] * v[k:k + 1, :]).astype(jnp.bfloat16)
            weights[pl.ds(a * LANES, LANES), lanes(k)] = q
            q = q.astype(jnp.float32)
            acc = q if acc is None else acc + q
        tmp4[a // 2, pl.ds(a % 2, 1), :] = jnp.sum(acc.T, axis=0, keepdims=True)
    load.wait()

    def project(ch):
        p = jnp.dot(weights[...], teach[:, ch * LANES:(ch + 2) * LANES], preferred_element_type=jnp.float32)
        part[ch] = p[:, :LANES].reshape(NX, NZ, ROWS, LANES)
        part[ch + 1] = p[:, LANES:].reshape(NX, NZ, ROWS, LANES)

    lo, hi = pl.ds(0, 4), pl.ds(4, 4)
    xr, xl = at_tgt(1, 0), at_tgt(-1, 0)
    zr, zl = at_tgt(0, 1), at_tgt(0, -1)

    def a_start(i, ch):
        remote(part.at[ch, xi[2], lo], xfar.at[i, 0], as_sem.at[i], ar_sem.at[i, 0], xr)
        remote(part.at[ch, xi[2], hi], xfar.at[i, 1], as_sem.at[i], ar_sem.at[i, 1], xl)
        remote(part.at[ch, xi[1], hi], xnear.at[i, 0, hi], as_sem.at[i], ar_sem.at[i, 2], xr)
        remote(part.at[ch, xi[3], lo], xnear.at[i, 1, lo], as_sem.at[i], ar_sem.at[i, 3], xl)

    def a_pass(i, ch, way):
        dev, dst, half = ((xr, xi[1], lo), (xl, xi[3], hi))[way]
        arrive(xfar.at[i, way], ar_sem.at[i, way])
        part[ch, dst, half] = part[ch, dst, half] + xfar[i, way]
        remote(part.at[ch, dst, half], xnear.at[i, way, half], as_sem.at[i], ar_sem.at[i, 2 + way], dev)

    def a_mid(i, ch):
        arrive(xnear.at[i, 0], ar_sem.at[i, 2])
        arrive(xnear.at[i, 1], ar_sem.at[i, 3])
        asum[i] = part[ch, x] + xnear[i, 0] + xnear[i, 1]
        remote(asum.at[i, zi[4], pl.ds(0, 16)], zfar.at[i, 0], zs_sem.at[i], zr_sem.at[i, 0, 0], zr)
        remote(asum.at[i, zi[4], pl.ds(16, 16)], zfar.at[i, 1], zs_sem.at[i], zr_sem.at[i, 1, 0], zl)

    def a_ring(i, ch, step, way):
        dev, dst = ((zr, zi[4 - step]), (zl, zi[4 + step]))[way]
        if step == 1:
            arrive(zfar.at[i, way], zr_sem.at[i, way, 0])
            half = pl.ds(16 * way, 16)
            asum[i, dst, half] = asum[i, dst, half] + zfar[i, way]
        else:
            arrive(znear.at[i, way, step - 2], zr_sem.at[i, way, step - 1])
            asum[i, dst] = asum[i, dst] + znear[i, way, step - 2]
        remote(asum.at[i, dst], znear.at[i, way, step - 1], zs_sem.at[i], zr_sem.at[i, way, step], dev)

    def finish(ch, value):
        scale = rcol[lax.div(z, 4), pl.ds(lax.rem(z, 4) * ROWS, ROWS), :]
        out[:, lanes(ch)] = (value * scale).astype(jnp.bfloat16)

    def a_end(i, ch):
        arrive(znear.at[i, 0, 2], zr_sem.at[i, 0, 3])
        arrive(znear.at[i, 1, 2], zr_sem.at[i, 1, 3])
        finish(ch, asum[i, z] + znear[i, 0, 2] + znear[i, 1, 2])

    ends = (pl.ds(0, 2), pl.ds(2, 2))

    def b_start(i, ch):
        for way, dev, near in ((0, zr, zi[3]), (1, zl, zi[5])):
            own = 1 - way
            remote(part.at[ch, ends[way], zi[4]], bfar.at[i, way], bs_sem.at[i], br_sem.at[i, way, 0], dev)
            remote(part.at[ch, ends[own], near], bnear.at[i, way, 0, ends[own]], bs_sem.at[i], br_sem.at[i, way, 1], dev)

    def b_ring(i, ch, step, way):
        dev, dst = ((zr, zi[4 - step]), (zl, zi[4 + step]))[way]
        if step == 1:
            arrive(bfar.at[i, way], br_sem.at[i, way, 0])
            part[ch, ends[way], dst] = part[ch, ends[way], dst] + bfar[i, way]
            remote(part.at[ch, ends[way], dst], bnear.at[i, way, 0, ends[way]], bs_sem.at[i], br_sem.at[i, way, 1], dev)
        else:
            arrive(bnear.at[i, way, step - 2], br_sem.at[i, way, step - 1])
            part[ch, :, dst] = part[ch, :, dst] + bnear[i, way, step - 2]
            remote(part.at[ch, :, dst], bnear.at[i, way, step - 1], bs_sem.at[i], br_sem.at[i, way, step], dev)

    def b_mid(i, ch):
        arrive(bnear.at[i, 0, 2], br_sem.at[i, 0, 3])
        arrive(bnear.at[i, 1, 2], br_sem.at[i, 1, 3])
        bsum[i] = part[ch, :, z] + bnear[i, 0, 2] + bnear[i, 1, 2]
        for d in (2, 1, 3):
            remote(bsum.at[i, xi[d]], bx.at[i, d - 1], bxs_sem.at[i], bxr_sem.at[i], at_tgt(d, 0))

    def b_end(i, ch):
        arrive(bx.at[i], bxr_sem.at[i])
        finish(ch, bsum[i, x] + bx[i, 0] + bx[i, 1] + bx[i, 2])

    def q_start():
        for d in (2, 1, 3):
            remote(tmp4.at[xi[d]], qbuf.at[d - 1], qs_sem.at[0], qr_sem.at[0], at_tgt(d, 0))

    def q_mid():
        arrive(qbuf.at[pl.ds(0, 3)], qr_sem.at[0])
        tmp4[x] = tmp4[x] + qbuf[0] + qbuf[1] + qbuf[2]
        for d in (4, 3, 5, 2, 6, 1, 7):
            remote(tmp4.at[x], qbuf.at[2 + d], qs_sem.at[1], qr_sem.at[1], at_tgt(0, d))

    def q_end():
        arrive(qbuf.at[pl.ds(3, 7)], qr_sem.at[1])
        total = tmp4[x]
        for d in range(7):
            total = total + qbuf[3 + d]
        rcol[0] = col_form(1.0 / total[0:1, :])
        rcol[1] = col_form(1.0 / total[1:2, :])

    steps = dict(ap=a_pass, am=a_mid, ar=a_ring, ae=a_end, br=b_ring, bm=b_mid, be=b_end)
    ready = set()
    q_start()
    for name, ch, *rest in SCHEDULE:
        if name == "qm":
            q_mid()
        elif name == "qe":
            q_end()
        elif name == "s":
            if ch // 2 not in ready:
                ready.add(ch // 2)
                project(ch // 2 * 2)
            (a_start if KINDS[ch] == "A" else b_start)(KINDS[:ch].count(KINDS[ch]), ch)
        else:
            steps[name](KINDS[:ch].count(KINDS[ch]), ch, *rest)

    for e in range(3):
        arrive(rbuf.at[e, pl.ds(0, 31)], rs_sem.at[e])
        arrive(cbuf.at[e, pl.ds(0, 7)], cs_sem.at[e])
    arrive(qbuf.at[pl.ds(0, 3)], qs_sem.at[0])
    arrive(qbuf.at[pl.ds(3, 7)], qs_sem.at[1])
    for i, ch in enumerate(chunks_of("A")):
        arrive(part.at[ch, pl.ds(0, 3)], as_sem.at[i])
        arrive(asum.at[i, pl.ds(0, 7)], zs_sem.at[i])
    for i, ch in enumerate(chunks_of("B")):
        arrive(part.at[ch, :, pl.ds(0, 7)], bs_sem.at[i])
        arrive(bx.at[i], bxs_sem.at[i])


def body(source_features, target_features, source_logmass, target_logmass, teacher_rows):
    na, nb = KINDS.count("A"), KINDS.count("B")
    f32 = jnp.float32
    vmem = pl.BlockSpec(memory_space=pltpu.VMEM)
    dma = pltpu.SemaphoreType.DMA
    projected, f, g = pl.pallas_call(
        functools.partial(kernel, source_features.shape[1]),
        out_shape=(
            jax.ShapeDtypeStruct((ROWS, CHUNKS * LANES), jnp.bfloat16),
            jax.ShapeDtypeStruct((BLK, LANES), f32),
            jax.ShapeDtypeStruct((BLK, LANES), f32),
        ),
        in_specs=[pl.BlockSpec(memory_space=pltpu.HBM)] * 5,
        out_specs=(vmem, vmem, vmem),
        scratch_shapes=[
            pltpu.VMEM(source_features.shape, source_features.dtype),
            pltpu.VMEM(target_features.shape, target_features.dtype),
            pltpu.VMEM((BLK, LANES), f32),
            pltpu.VMEM((BLK, LANES), f32),
            pltpu.VMEM((BLK, LANES, TILE), f32),
            pltpu.VMEM((BLK, LANES, LANES), f32),
            pltpu.VMEM((TILE, TILE), jnp.bfloat16),
            pltpu.VMEM((TILE, CHUNKS * LANES), jnp.bfloat16),
            pltpu.VMEM((CHUNKS, NX, NZ, ROWS, LANES), f32),
            pltpu.VMEM((3, 32, BLK, LANES), f32),
            pltpu.VMEM((3, 8, BLK, LANES), f32),
            pltpu.VMEM((6, BLK, LANES), f32),
            pltpu.VMEM((NX, 2, LANES), f32),
            pltpu.VMEM((10, 2, LANES), f32),
            pltpu.VMEM((na, 2, 4, ROWS, LANES), f32),
            pltpu.VMEM((na, 2, NZ, ROWS, LANES), f32),
            pltpu.VMEM((na, NZ, ROWS, LANES), f32),
            pltpu.VMEM((na, 2, ROWS // 2, LANES), f32),
            pltpu.VMEM((na, 2, 3, ROWS, LANES), f32),
            pltpu.VMEM((nb, 2, 2, ROWS, LANES), f32),
            pltpu.VMEM((nb, 2, 3, NX, ROWS, LANES), f32),
            pltpu.VMEM((nb, NX, ROWS, LANES), f32),
            pltpu.VMEM((nb, 3, ROWS, LANES), f32),
            pltpu.VMEM((2, LANES, LANES), f32),
            dma, dma((4,)), dma((3,)), dma((3,)), dma((3,)), dma((3,)), dma((2,)), dma((2,)),
            dma((na,)), dma((na, 4)), dma((na,)), dma((na, 2, 4)),
            dma((nb,)), dma((nb, 2, 4)), dma((nb,)), dma((nb,)),
        ],
        compiler_params=pltpu.CompilerParams(
            collective_id=0, has_side_effects=True, vmem_limit_bytes=63 * 1024 * 1024),
    )(source_features, target_features, source_logmass.reshape(BLK, LANES),
      target_logmass.reshape(BLK, LANES), teacher_rows)
    return projected, f.reshape(TILE), g.reshape(TILE)


def solution(mesh):
    in_specs = (P("src", None), P("tgt", None), P("src"), P("tgt"), P("tgt", None))
    out_specs = (P(("src", "tgt"), None), P("src"), P("tgt"))
    return jax.shard_map(body, mesh=mesh, in_specs=in_specs, out_specs=out_specs, check_vma=False)
```

```python
import functools
import math

import jax
import jax.numpy as jnp
from jax import lax
from jax.experimental import pallas as pl
from jax.experimental.pallas import tpu as pltpu
from jax.sharding import PartitionSpec as P

MESH = pl.DeviceIdType.MESH
EPS = 0.1
LOG2E = math.log2(math.e)
LN2 = math.log(2.0)
NX, NY, NZ = 4, 4, 8
LANES = 128
TILE = 1024
BLK = TILE // LANES
ROWS = 32
HALF = TILE // 2
CHUNKS = 12
KINDS = "ABAABBABHHHH"
SCHEDULE = (
    ("s", 0), ("s", 1), ("s", 2), ("s", 3), ("qm", 0), ("s", 4), ("s", 5), ("ap", 0, 0), ("ap", 0, 1),
    ("br", 1, 1, 0), ("br", 1, 1, 1), ("hw", 0), ("hf", 0), ("s", 8), ("br", 4, 1, 0), ("br", 4, 1, 1), ("s", 6),
    ("s", 7), ("ap", 2, 0), ("ap", 2, 1), ("br", 5, 1, 0), ("br", 5, 1, 1), ("s", 9), ("br", 1, 2, 0),
    ("br", 1, 2, 1), ("br", 4, 2, 0), ("br", 4, 2, 1), ("ht", 0), ("s", 10), ("ap", 3, 0), ("ap", 3, 1),
    ("br", 7, 1, 0), ("br", 7, 1, 1), ("s", 11), ("br", 5, 2, 0), ("br", 5, 2, 1), ("am", 0), ("br", 1, 3, 0),
    ("br", 1, 3, 1), ("ap", 6, 0), ("br", 4, 3, 0), ("br", 4, 3, 1), ("br", 7, 2, 0), ("br", 7, 2, 1), ("hm", 8),
    ("br", 5, 3, 0), ("br", 5, 3, 1), ("ar", 0, 1, 0), ("ar", 0, 1, 1), ("ap", 6, 1), ("bm", 1), ("bm", 4),
    ("am", 2), ("hm", 9), ("br", 7, 3, 0), ("br", 7, 3, 1), ("ar", 8, 1, 0), ("ar", 8, 1, 1), ("bm", 5),
    ("ar", 0, 2, 0), ("ar", 0, 2, 1), ("ar", 2, 1, 0), ("ar", 2, 1, 1), ("ar", 9, 1, 0), ("ar", 9, 1, 1), ("hm", 10),
    ("hm", 11), ("am", 3), ("bm", 7), ("ar", 8, 2, 0), ("ar", 8, 2, 1), ("ar", 0, 3, 0), ("ar", 0, 3, 1), ("am", 6),
    ("ar", 2, 2, 0), ("ar", 2, 2, 1), ("ar", 9, 2, 0), ("ar", 9, 2, 1), ("ar", 10, 1, 0), ("ar", 10, 1, 1),
    ("ar", 3, 1, 0), ("ar", 3, 1, 1), ("ar", 11, 1, 0), ("ar", 11, 1, 1), ("qe", 0), ("be", 1), ("ar", 8, 3, 0),
    ("ar", 8, 3, 1), ("be", 4), ("ae", 0), ("ar", 6, 1, 0), ("ar", 6, 1, 1), ("be", 5), ("ar", 2, 3, 0),
    ("ar", 2, 3, 1), ("ar", 9, 3, 0), ("ar", 9, 3, 1), ("be", 7), ("ar", 10, 2, 0), ("ar", 10, 2, 1),
    ("ar", 3, 2, 0), ("ar", 3, 2, 1), ("ar", 11, 2, 0), ("ar", 11, 2, 1), ("ae", 8), ("ar", 6, 2, 0),
    ("ar", 6, 2, 1), ("ae", 2), ("ae", 9), ("ar", 10, 3, 0), ("ar", 10, 3, 1), ("ar", 3, 3, 0), ("ar", 3, 3, 1),
    ("ar", 11, 3, 0), ("ar", 11, 3, 1), ("ar", 6, 3, 0), ("ar", 6, 3, 1), ("ae", 10), ("ae", 3), ("ae", 11),
    ("ae", 6),
)
NA, NH = KINDS.count("A"), KINDS.count("H")


def chunks_of(kind):
    return [ch for ch in range(CHUNKS) if KINDS[ch] == kind]


def kernel(feat, xs_hbm, ys_hbm, slm_hbm, tlm_hbm, rows_hbm, out, f_out, g_out,
           xs, ys, slm, tlm, score, hcol, weights, teach, part, rbuf, cbuf, vec, tmp4, qbuf,
           xfar, xnear, asum, zfar, znear, bfar, bnear, bsum, bx, rcol,
           load_sem, in_sem, rs_sem, rr_sem, cs_sem, cr_sem, qs_sem, qr_sem,
           as_sem, ar_sem, zs_sem, zr_sem, bs_sem, br_sem, bxs_sem, bxr_sem,
           stage, gath, pscore, pweights, pteach, kvec, hsend, hrecv,
           gs_sem, gr_sem, ds_sem, dr_sem, ks_sem, kr_sem, hs_sem, hr_sem):
    src = lax.axis_index("src")
    tgt = lax.axis_index("tgt")
    y, c = lax.div(src, 2), lax.rem(src, 2)
    x, z = lax.div(tgt, NZ), lax.rem(tgt, NZ)
    xi = [lax.rem(x + d, NX) for d in range(NX)]
    zi = [lax.rem(z + d, NZ) for d in range(NZ)]

    def at_tgt(dx, dz):
        return (src, xi[dx % NX] * NZ + zi[dz % NZ])

    def at_src(dy, dc):
        return (lax.rem(y + dy, NY) * 2 + lax.rem(c + dc, 2), tgt)

    def hops(d, n):
        return min(d, n - d)

    tgt_peers = sorted([(dx, dz) for dx in range(NX) for dz in range(NZ) if dx or dz],
                       key=lambda o: -hops(o[0], NX) - hops(o[1], NZ))
    src_peers = sorted([(dy, dc) for dy in range(NY) for dc in range(2) if dy or dc],
                       key=lambda o: -hops(o[0], NY) - 0.1 * o[1])

    loads = [pltpu.make_async_copy(a, b, in_sem.at[n]) for n, (a, b) in enumerate(
        ((ys_hbm, ys), (xs_hbm, xs), (slm_hbm, slm), (tlm_hbm, tlm)))]
    for copy in loads:
        copy.start()
    load = pltpu.make_async_copy(rows_hbm, teach, load_sem)
    load.start()
    barrier = pltpu.get_barrier_semaphore()
    for o in tgt_peers:
        pl.semaphore_signal(barrier, inc=1, device_id=at_tgt(*o), device_id_type=MESH)
    for o in src_peers:
        pl.semaphore_signal(barrier, inc=1, device_id=at_src(*o), device_id_type=MESH)

    def remote(a, b, ssem, rsem, dev):
        pltpu.make_async_remote_copy(src_ref=a, dst_ref=b, send_sem=ssem, recv_sem=rsem,
                                     device_id=dev, device_id_type=MESH).start()

    def arrive(ref, sem):
        pltpu.make_async_copy(ref, ref, sem).wait()

    def row_exchange(e, value, meanwhile=None):
        rbuf[e, tgt] = value
        for o in tgt_peers:
            remote(rbuf.at[e, tgt], rbuf.at[e, tgt], rs_sem.at[e], rr_sem.at[e], at_tgt(*o))
        if meanwhile is not None:
            meanwhile()
        arrive(rbuf.at[e, pl.ds(0, 31)], rr_sem.at[e])
        return rbuf[e]

    def col_exchange(e, value, meanwhile=None):
        cbuf[e, src] = value
        for o in src_peers:
            remote(cbuf.at[e, src], cbuf.at[e, src], cs_sem.at[e], cr_sem.at[e], at_src(*o))
        if meanwhile is not None:
            meanwhile()
        arrive(cbuf.at[e, pl.ds(0, 7)], cr_sem.at[e])
        return cbuf[e]

    def lse2(parts):
        peak = jnp.max(parts, axis=0)
        return peak + jnp.log(jnp.sum(jnp.exp2(parts - peak), axis=0)) * LOG2E

    def col_form(row):
        return jnp.broadcast_to(row, (LANES, LANES)).T

    side = 1 - 2 * lax.rem(x, 2)
    mate_x = [lax.rem(x + side + NX, NX), lax.rem(x - side + NX, NX)]
    mates = [(src, m * NZ + z) for m in mate_x]
    sibling = (y * 2 + 1 - c, tgt)
    mine = pl.ds(c * HALF, HALF)

    def gather_send(u):
        remote(stage.at[u], gath.at[u, c], gs_sem.at[u], gr_sem.at[u], mates[u % 2])

    def gather_share(u):
        arrive(gath.at[u, 0], gr_sem.at[u])
        remote(gath.at[u, c], gath.at[u, c], ds_sem.at[u], dr_sem.at[u], sibling)

    def gather_end(u):
        arrive(gath.at[u, 0], dr_sem.at[u])

    def lanes(k):
        return slice(k * LANES, (k + 1) * LANES)

    def fold(t):
        return t.reshape(LANES // 8, 8, LANES)

    for copy in loads:
        copy.wait()
    slm2 = slm[...] * LOG2E
    tlm2 = tlm[...] * LOG2E
    norm_scale = LOG2E / (feat * EPS)
    for a in range(BLK):
        xf = xs[pl.ds(a * LANES, LANES), :].astype(jnp.float32)
        yf = ys[pl.ds(a * LANES, LANES), :].astype(jnp.float32)
        vec[0, pl.ds(a, 1), :] = jnp.sum((xf * xf).T, axis=0, keepdims=True)
        vec[1, pl.ds(a, 1), :] = jnp.sum((yf * yf).T, axis=0, keepdims=True)
    nx2 = vec[0] * norm_scale
    ny2 = vec[1] * norm_scale
    bias = tlm2 - ny2

    for a in range(BLK):
        d = lax.dot_general(xs[pl.ds(a * LANES, LANES), :], ys[...], (((1,), (1,)), ((), ())),
                            preferred_element_type=jnp.float32)
        e = d * (2.0 * norm_scale)
        score[a] = e
        t = [e[:, lanes(k)] + bias[k:k + 1, :] for k in range(BLK)]
        m = functools.reduce(jnp.maximum, t)
        m = jnp.max(m, axis=1, keepdims=True)
        s = functools.reduce(jnp.add, [jnp.exp2(v - m) for v in t])
        s = jnp.sum(s, axis=1, keepdims=True)
        lse = m + jnp.log(s) * LOG2E
        vec[2, pl.ds(a, 1), :] = jnp.broadcast_to(lse, (LANES, LANES)).T[0:1, :]
    stage[0] = ys[mine, :].astype(jnp.float32)
    stage[1] = stage[0]
    load.wait()
    for n, ch in enumerate(chunks_of("H")):
        stage[2 + n] = teach[mine, lanes(ch)].astype(jnp.float32)
    pl.semaphore_wait(barrier, len(tgt_peers) + len(src_peers))
    row2 = lse2(row_exchange(0, vec[2]))
    vec[6] = row2
    gather_send(0)
    gather_send(1)

    h = slm2 - row2
    peaks = [jnp.full((8, LANES), -jnp.inf, jnp.float32)] * BLK
    for a in range(BLK):
        hc = col_form(h[a:a + 1, :])
        hcol[a] = hc
        for k in range(BLK):
            peaks[k] = jnp.maximum(peaks[k], jnp.max(fold(score[a, :, lanes(k)] + hc), axis=0))
    peaks = [jnp.max(p, axis=0, keepdims=True) for p in peaks]
    sums = [jnp.zeros((8, LANES), jnp.float32)] * BLK
    for a in range(BLK):
        hc = hcol[a]
        for k in range(BLK):
            sums[k] = sums[k] + jnp.sum(fold(jnp.exp2(score[a, :, lanes(k)] + hc - peaks[k])), axis=0)
    for k in range(BLK):
        total = jnp.sum(sums[k], axis=0, keepdims=True)
        vec[3, pl.ds(k, 1), :] = peaks[k] + jnp.log(total) * LOG2E
    col2 = lse2(col_exchange(0, vec[3]))

    tmass = jnp.exp(tlm[...])
    smass = jnp.exp(slm[...])
    for a in range(BLK):
        lc = col_form(row2[a:a + 1, :])
        acc = None
        for k in range(BLK):
            q = jnp.exp2(score[a, :, lanes(k)] - lc - col2[k:k + 1, :])
            score[a, :, lanes(k)] = q
            q = q * tmass[k:k + 1, :]
            acc = q if acc is None else acc + q
        vec[4, pl.ds(a, 1), :] = jnp.sum(acc.T, axis=0, keepdims=True)

    def row_step(v):
        for a in range(BLK):
            acc = None
            for k in range(BLK):
                q = score[a, :, lanes(k)] * v[k:k + 1, :]
                acc = q if acc is None else acc + q
            vec[4, pl.ds(a, 1), :] = jnp.sum(acc.T, axis=0, keepdims=True)

    def col_step(u):
        acc = [jnp.zeros((8, LANES), jnp.float32)] * BLK
        for a in range(BLK):
            uc = col_form(u[a:a + 1, :])
            for k in range(BLK):
                acc[k] = acc[k] + jnp.sum(fold(score[a, :, lanes(k)] * uc), axis=0)
        for k in range(BLK):
            vec[5, pl.ds(k, 1), :] = jnp.sum(acc[k], axis=0, keepdims=True)

    def share(*units):
        for u in units:
            gather_share(u)

    def mate_scores():
        for kind in range(2):
            gather_end(kind)
            feats = gath[kind].reshape(TILE, LANES).astype(jnp.bfloat16)
            for part_at, xb in enumerate((x, mate_x[1 - kind])):
                d = lax.dot_general(xs[pl.ds(xb * 256, 256), :], feats, (((1,), (1,)), ((), ())),
                                    preferred_element_type=jnp.float32)
                pscore[kind, pl.ds(part_at * 256, 256), :] = d * (2.0 * norm_scale)

    def take(n):
        gather_end(2 + n)
        pteach[n] = gath[2 + n].reshape(TILE, LANES).astype(jnp.bfloat16)

    def mate_weights():
        for kind in range(2):
            arrive(kvec.at[1 + kind], kr_sem.at[kind])
            for b in range(4):
                xb = (x, mate_x[1 - kind])[b // 2]
                lc = col_form(vec[6, pl.ds(2 * xb + b % 2, 1), :])
                for k in range(BLK):
                    w = jnp.exp2(pscore[kind, pl.ds(b * LANES, LANES), lanes(k)] - lc + kvec[1 + kind, k:k + 1, :])
                    pweights[kind, pl.ds(b * LANES, LANES), lanes(k)] = w.astype(jnp.bfloat16)

    r = jnp.sum(row_exchange(1, vec[4], lambda: share(0, 1)), axis=0)
    gather_send(2)
    gather_send(3)
    col_step(smass / r)
    cs = jnp.sum(col_exchange(1, vec[5], mate_scores), axis=0)
    row_step(tmass / cs)
    r = jnp.sum(row_exchange(2, vec[4], lambda: share(2, 3)), axis=0)
    gather_send(4)
    gather_send(5)
    f_out[...] = (nx2 - row2) * (EPS * LN2) - EPS * jnp.log(r)
    col_step(smass / r)
    def take_first():
        take(0)
        take(1)

    cs = jnp.sum(col_exchange(2, vec[5], take_first), axis=0)
    kvec[0] = tlm2 - jnp.log(cs) * LOG2E - col2
    for kind in range(2):
        remote(kvec.at[0], kvec.at[1 + kind], ks_sem.at[kind], kr_sem.at[kind], mates[kind])
    g_out[...] = (ny2 - col2) * (EPS * LN2) - EPS * jnp.log(cs)

    v = tmass / cs
    for a in range(BLK):
        acc = None
        for k in range(BLK):
            q = (score[a, :, lanes(k)] * v[k:k + 1, :]).astype(jnp.bfloat16)
            weights[pl.ds(a * LANES, LANES), lanes(k)] = q
            q = q.astype(jnp.float32)
            acc = q if acc is None else acc + q
        tmp4[a // 2, pl.ds(a % 2, 1), :] = jnp.sum(acc.T, axis=0, keepdims=True)

    def project(ch):
        p = jnp.dot(weights[...], teach[:, ch * LANES:(ch + 2) * LANES], preferred_element_type=jnp.float32)
        part[ch] = p[:, :LANES].reshape(NX, NZ, ROWS, LANES)
        part[ch + 1] = p[:, LANES:].reshape(NX, NZ, ROWS, LANES)

    lo, hi = pl.ds(0, 4), pl.ds(4, 4)
    xr, xl = at_tgt(1, 0), at_tgt(-1, 0)
    zr, zl = at_tgt(0, 1), at_tgt(0, -1)

    def a_start(i, ch):
        remote(part.at[ch, xi[2], lo], xfar.at[i, 0], as_sem.at[i], ar_sem.at[i, 0], xr)
        remote(part.at[ch, xi[2], hi], xfar.at[i, 1], as_sem.at[i], ar_sem.at[i, 1], xl)
        remote(part.at[ch, xi[1], hi], xnear.at[i, 0, hi], as_sem.at[i], ar_sem.at[i, 2], xr)
        remote(part.at[ch, xi[3], lo], xnear.at[i, 1, lo], as_sem.at[i], ar_sem.at[i, 3], xl)

    def a_pass(i, ch, way):
        dev, dst, half = ((xr, xi[1], lo), (xl, xi[3], hi))[way]
        arrive(xfar.at[i, way], ar_sem.at[i, way])
        part[ch, dst, half] = part[ch, dst, half] + xfar[i, way]
        remote(part.at[ch, dst, half], xnear.at[i, way, half], as_sem.at[i], ar_sem.at[i, 2 + way], dev)

    def a_mid(i, ch):
        arrive(xnear.at[i, 0], ar_sem.at[i, 2])
        arrive(xnear.at[i, 1], ar_sem.at[i, 3])
        asum[i] = part[ch, x] + xnear[i, 0] + xnear[i, 1]
        remote(asum.at[i, zi[4], pl.ds(0, 16)], zfar.at[i, 0], zs_sem.at[i], zr_sem.at[i, 0, 0], zr)
        remote(asum.at[i, zi[4], pl.ds(16, 16)], zfar.at[i, 1], zs_sem.at[i], zr_sem.at[i, 1, 0], zl)

    def a_ring(i, ch, step, way):
        dev, dst = ((zr, zi[4 - step]), (zl, zi[4 + step]))[way]
        if step == 1:
            arrive(zfar.at[i, way], zr_sem.at[i, way, 0])
            half = pl.ds(16 * way, 16)
            asum[i, dst, half] = asum[i, dst, half] + zfar[i, way]
        else:
            arrive(znear.at[i, way, step - 2], zr_sem.at[i, way, step - 1])
            asum[i, dst] = asum[i, dst] + znear[i, way, step - 2]
        remote(asum.at[i, dst], znear.at[i, way, step - 1], zs_sem.at[i], zr_sem.at[i, way, step], dev)

    def finish(ch, value):
        scale = rcol[lax.div(z, 4), pl.ds(lax.rem(z, 4) * ROWS, ROWS), :]
        out[:, lanes(ch)] = (value * scale).astype(jnp.bfloat16)

    def a_end(i, ch):
        arrive(znear.at[i, 0, 2], zr_sem.at[i, 0, 3])
        arrive(znear.at[i, 1, 2], zr_sem.at[i, 1, 3])
        finish(ch, asum[i, z] + znear[i, 0, 2] + znear[i, 1, 2])

    ends = (pl.ds(0, 2), pl.ds(2, 2))

    def b_start(i, ch):
        for way, dev, near in ((0, zr, zi[3]), (1, zl, zi[5])):
            own = 1 - way
            remote(part.at[ch, ends[way], zi[4]], bfar.at[i, way], bs_sem.at[i], br_sem.at[i, way, 0], dev)
            remote(part.at[ch, ends[own], near], bnear.at[i, way, 0, ends[own]], bs_sem.at[i], br_sem.at[i, way, 1], dev)

    def b_ring(i, ch, step, way):
        dev, dst = ((zr, zi[4 - step]), (zl, zi[4 + step]))[way]
        if step == 1:
            arrive(bfar.at[i, way], br_sem.at[i, way, 0])
            part[ch, ends[way], dst] = part[ch, ends[way], dst] + bfar[i, way]
            remote(part.at[ch, ends[way], dst], bnear.at[i, way, 0, ends[way]], bs_sem.at[i], br_sem.at[i, way, 1], dev)
        else:
            arrive(bnear.at[i, way, step - 2], br_sem.at[i, way, step - 1])
            part[ch, :, dst] = part[ch, :, dst] + bnear[i, way, step - 2]
            remote(part.at[ch, :, dst], bnear.at[i, way, step - 1], bs_sem.at[i], br_sem.at[i, way, step], dev)

    def b_mid(i, ch):
        arrive(bnear.at[i, 0, 2], br_sem.at[i, 0, 3])
        arrive(bnear.at[i, 1, 2], br_sem.at[i, 1, 3])
        bsum[i] = part[ch, :, z] + bnear[i, 0, 2] + bnear[i, 1, 2]
        for d in (2, 1, 3):
            remote(bsum.at[i, xi[d]], bx.at[i, d - 1], bxs_sem.at[i], bxr_sem.at[i], at_tgt(d, 0))

    def b_end(i, ch):
        arrive(bx.at[i], bxr_sem.at[i])
        finish(ch, bsum[i, x] + bx[i, 0] + bx[i, 1] + bx[i, 2])

    def h_start(n, ch):
        kind = n % 2
        for part_at, xb in enumerate((x, mate_x[1 - kind])):
            p = jnp.dot(weights[pl.ds(xb * 256, 256), :], teach[:, lanes(ch)], preferred_element_type=jnp.float32)
            p = p + jnp.dot(pweights[kind, pl.ds(part_at * 256, 256), :], pteach[n], preferred_element_type=jnp.float32)
            if part_at == 0:
                asum[NA + n] = p.reshape(NZ, ROWS, LANES)
            else:
                hsend[n] = p.reshape(NZ, ROWS, LANES)
        remote(hsend.at[n], hrecv.at[n], hs_sem.at[n], hr_sem.at[n], mates[1 - kind])

    def z_start(i):
        remote(asum.at[i, zi[4], pl.ds(0, 16)], zfar.at[i, 0], zs_sem.at[i], zr_sem.at[i, 0, 0], zr)
        remote(asum.at[i, zi[4], pl.ds(16, 16)], zfar.at[i, 1], zs_sem.at[i], zr_sem.at[i, 1, 0], zl)

    def h_mid(n, ch):
        arrive(hrecv.at[n], hr_sem.at[n])
        asum[NA + n] = asum[NA + n] + hrecv[n]
        z_start(NA + n)

    def q_start():
        for d in (2, 1, 3):
            remote(tmp4.at[xi[d]], qbuf.at[d - 1], qs_sem.at[0], qr_sem.at[0], at_tgt(d, 0))

    def q_mid():
        arrive(qbuf.at[pl.ds(0, 3)], qr_sem.at[0])
        tmp4[x] = tmp4[x] + qbuf[0] + qbuf[1] + qbuf[2]
        for d in (4, 3, 5, 2, 6, 1, 7):
            remote(tmp4.at[x], qbuf.at[2 + d], qs_sem.at[1], qr_sem.at[1], at_tgt(0, d))

    def q_end():
        arrive(qbuf.at[pl.ds(3, 7)], qr_sem.at[1])
        total = tmp4[x]
        for d in range(7):
            total = total + qbuf[3 + d]
        rcol[0] = col_form(1.0 / total[0:1, :])
        rcol[1] = col_form(1.0 / total[1:2, :])

    steps = dict(hm=h_mid, ap=a_pass, am=a_mid, ar=a_ring, ae=a_end, br=b_ring, bm=b_mid, be=b_end)
    ready = set()
    q_start()
    for name, ch, *rest in SCHEDULE:
        if name == "qm":
            q_mid()
        elif name == "qe":
            q_end()
        elif name == "hw":
            mate_weights()
        elif name == "hf":
            share(4, 5)
        elif name == "ht":
            take(2)
            take(3)
        elif name == "s" and KINDS[ch] == "H":
            h_start(KINDS[:ch].count("H"), ch)
        elif name == "s":
            if ch // 2 not in ready:
                ready.add(ch // 2)
                project(ch // 2 * 2)
            (a_start if KINDS[ch] == "A" else b_start)(KINDS[:ch].count(KINDS[ch]), ch)
        elif KINDS[ch] == "H" and name in ("ar", "ae"):
            steps[name](NA + KINDS[:ch].count("H"), ch, *rest)
        else:
            steps[name](KINDS[:ch].count(KINDS[ch]), ch, *rest)

    for e in range(3):
        arrive(rbuf.at[e, pl.ds(0, 31)], rs_sem.at[e])
        arrive(cbuf.at[e, pl.ds(0, 7)], cs_sem.at[e])
    arrive(qbuf.at[pl.ds(0, 3)], qs_sem.at[0])
    arrive(qbuf.at[pl.ds(3, 7)], qs_sem.at[1])
    for i, ch in enumerate(chunks_of("A")):
        arrive(part.at[ch, pl.ds(0, 3)], as_sem.at[i])
    for i in range(NA + NH):
        arrive(asum.at[i, pl.ds(0, 7)], zs_sem.at[i])
    for n in range(NH):
        arrive(hsend.at[n], hs_sem.at[n])
    for u in range(2 + NH):
        arrive(stage.at[u], gs_sem.at[u])
        arrive(stage.at[u], ds_sem.at[u])
    for kind in range(2):
        arrive(kvec.at[0], ks_sem.at[kind])
    for i, ch in enumerate(chunks_of("B")):
        arrive(part.at[ch, :, pl.ds(0, 7)], bs_sem.at[i])
        arrive(bx.at[i], bxs_sem.at[i])


def settle(*refs):
    sem = refs[-1]
    copies = [pltpu.make_async_copy(refs[n], refs[3 + n], sem.at[n]) for n in range(3)]
    for copy in copies:
        copy.start()
    for copy in copies:
        copy.wait()


def body(source_features, target_features, source_logmass, target_logmass, teacher_rows):
    na, nb, nz = NA, KINDS.count("B"), NA + NH
    f32 = jnp.float32
    vmem = pl.BlockSpec(memory_space=pltpu.VMEM)
    dma = pltpu.SemaphoreType.DMA
    projected, f, g = pl.pallas_call(
        functools.partial(kernel, source_features.shape[1]),
        out_shape=(
            jax.ShapeDtypeStruct((ROWS, CHUNKS * LANES), jnp.bfloat16),
            jax.ShapeDtypeStruct((BLK, LANES), f32),
            jax.ShapeDtypeStruct((BLK, LANES), f32),
        ),
        in_specs=[pl.BlockSpec(memory_space=pltpu.HBM)] * 5,
        out_specs=(vmem, vmem, vmem),
        scratch_shapes=[
            pltpu.VMEM(source_features.shape, source_features.dtype),
            pltpu.VMEM(target_features.shape, target_features.dtype),
            pltpu.VMEM((BLK, LANES), f32),
            pltpu.VMEM((BLK, LANES), f32),
            pltpu.VMEM((BLK, LANES, TILE), f32),
            pltpu.VMEM((BLK, LANES, LANES), f32),
            pltpu.VMEM((TILE, TILE), jnp.bfloat16),
            pltpu.VMEM((TILE, CHUNKS * LANES), jnp.bfloat16),
            pltpu.VMEM((CHUNKS, NX, NZ, ROWS, LANES), f32),
            pltpu.VMEM((3, 32, BLK, LANES), f32),
            pltpu.VMEM((3, 8, BLK, LANES), f32),
            pltpu.VMEM((7, BLK, LANES), f32),
            pltpu.VMEM((NX, 2, LANES), f32),
            pltpu.VMEM((10, 2, LANES), f32),
            pltpu.VMEM((na, 2, 4, ROWS, LANES), f32),
            pltpu.VMEM((na, 2, NZ, ROWS, LANES), f32),
            pltpu.VMEM((nz, NZ, ROWS, LANES), f32),
            pltpu.VMEM((nz, 2, ROWS // 2, LANES), f32),
            pltpu.VMEM((nz, 2, 3, ROWS, LANES), f32),
            pltpu.VMEM((nb, 2, 2, ROWS, LANES), f32),
            pltpu.VMEM((nb, 2, 3, NX, ROWS, LANES), f32),
            pltpu.VMEM((nb, NX, ROWS, LANES), f32),
            pltpu.VMEM((nb, 3, ROWS, LANES), f32),
            pltpu.VMEM((2, LANES, LANES), f32),
            dma, dma((4,)), dma((3,)), dma((3,)), dma((3,)), dma((3,)), dma((2,)), dma((2,)),
            dma((na,)), dma((na, 4)), dma((nz,)), dma((nz, 2, 4)),
            dma((nb,)), dma((nb, 2, 4)), dma((nb,)), dma((nb,)),
            pltpu.VMEM((2 + NH, HALF, LANES), f32),
            pltpu.VMEM((2 + NH, 2, HALF, LANES), f32),
            pltpu.VMEM((2, HALF, TILE), f32),
            pltpu.VMEM((2, HALF, TILE), jnp.bfloat16),
            pltpu.VMEM((NH, TILE, LANES), jnp.bfloat16),
            pltpu.VMEM((3, BLK, LANES), f32),
            pltpu.VMEM((NH, NZ, ROWS, LANES), f32),
            pltpu.VMEM((NH, NZ, ROWS, LANES), f32),
            dma((2 + NH,)), dma((2 + NH,)), dma((2 + NH,)), dma((2 + NH,)), dma((2,)), dma((2,)), dma((NH,)), dma((NH,)),
        ],
        compiler_params=pltpu.CompilerParams(
            collective_id=0, has_side_effects=True, vmem_limit_bytes=(64 * 1024 - 192) * 1024),
    )(source_features, target_features, source_logmass.reshape(BLK, LANES),
      target_logmass.reshape(BLK, LANES), teacher_rows)
    return pl.pallas_call(
        settle,
        out_shape=(
            jax.ShapeDtypeStruct(projected.shape, jnp.bfloat16),
            jax.ShapeDtypeStruct((TILE,), f32),
            jax.ShapeDtypeStruct((TILE,), f32),
        ),
        in_specs=[vmem] * 3,
        out_specs=(pl.BlockSpec(memory_space=pl.ANY),) * 3,
        scratch_shapes=[dma((3,))],
    )(projected, f.reshape(TILE), g.reshape(TILE))


def solution(mesh):
    in_specs = (P("src", None), P("tgt", None), P("src"), P("tgt"), P("tgt", None))
    out_specs = (P(("src", "tgt"), None), P("src"), P("tgt"))
    return jax.shard_map(body, mesh=mesh, in_specs=in_specs, out_specs=out_specs, check_vma=False)
```

```python
import functools
import math

import jax
import jax.numpy as jnp
from jax import lax
from jax.experimental import pallas as pl
from jax.experimental.pallas import tpu as pltpu
from jax.sharding import PartitionSpec as P

MESH = pl.DeviceIdType.MESH
EPS = 0.1
LOG2E = math.log2(math.e)
LN2 = math.log(2.0)
NX, NY, NZ = 4, 4, 8
LANES = 128
TILE = 1024
BLK = TILE // LANES
ROWS = 32
HALF = TILE // 2
NEAR = 4
CHUNKS = 12
KINDS = "ABABBAHHHHHH"
DIRECT = (1, 3, 5)
SCHEDULE = (
    ("s", 0), ("s", 1), ("ao", 0), ("bo", 1), ("s", 2), ("s", 3), ("qm", 0), ("s", 4), ("br", 1, 1, 0),
    ("br", 1, 1, 1), ("ao", 2), ("bo", 3), ("ap", 0, 0), ("ap", 0, 1), ("bo", 4), ("hw", 0), ("s", 6), ("hf", 0),
    ("br", 3, 1, 0), ("br", 3, 1, 1), ("s", 7), ("br", 4, 1, 0), ("ap", 2, 0), ("ap", 2, 1), ("br", 4, 1, 1),
    ("br", 1, 2, 0), ("br", 1, 2, 1), ("s", 8), ("s", 9), ("ht", 0), ("s", 10), ("br", 3, 2, 0), ("br", 3, 2, 1),
    ("am", 0), ("br", 4, 2, 0), ("br", 4, 2, 1), ("s", 11), ("br", 1, 3, 0), ("br", 1, 3, 1), ("hm", 7), ("hm", 6),
    ("br", 3, 3, 0), ("br", 3, 3, 1), ("ar", 0, 1, 0), ("ar", 0, 1, 1), ("am", 2), ("br", 4, 3, 0), ("br", 4, 3, 1),
    ("s", 5), ("ao", 5), ("bm", 1), ("ar", 7, 1, 0), ("ar", 7, 1, 1), ("ar", 6, 1, 0), ("ar", 6, 1, 1), ("hm", 8),
    ("hm", 9), ("bm", 3), ("ar", 0, 2, 0), ("ar", 0, 2, 1), ("ar", 2, 1, 0), ("ar", 2, 1, 1), ("hm", 11), ("hm", 10),
    ("bm", 4), ("ar", 7, 2, 0), ("ar", 7, 2, 1), ("ar", 6, 2, 0), ("ar", 6, 2, 1), ("ar", 8, 1, 0), ("ar", 8, 1, 1),
    ("ar", 9, 1, 0), ("ar", 9, 1, 1), ("ap", 5, 0), ("ar", 0, 3, 0), ("ar", 0, 3, 1), ("ap", 5, 1), ("ar", 2, 2, 0),
    ("ar", 2, 2, 1), ("ar", 11, 1, 0), ("ar", 11, 1, 1), ("ar", 10, 1, 0), ("ar", 10, 1, 1), ("qe", 0), ("be", 1),
    ("ar", 7, 3, 0), ("ar", 7, 3, 1), ("ar", 6, 3, 0), ("ar", 6, 3, 1), ("be", 3), ("ar", 8, 2, 0), ("ar", 8, 2, 1),
    ("ar", 9, 2, 0), ("ar", 9, 2, 1), ("be", 4), ("ae", 0), ("ar", 2, 3, 0), ("ar", 2, 3, 1), ("ar", 11, 2, 0),
    ("ar", 11, 2, 1), ("ar", 10, 2, 0), ("ar", 10, 2, 1), ("am", 5), ("ae", 7), ("ae", 6), ("ar", 8, 3, 0),
    ("ar", 8, 3, 1), ("ar", 9, 3, 0), ("ar", 9, 3, 1), ("ae", 2), ("ar", 11, 3, 0), ("ar", 11, 3, 1),
    ("ar", 10, 3, 0), ("ar", 10, 3, 1), ("ad", 5), ("ae", 8), ("ae", 9), ("ae", 11), ("ae", 10),
)
NA, NH = KINDS.count("A"), KINDS.count("H")


def chunks_of(kind):
    return [ch for ch in range(CHUNKS) if KINDS[ch] == kind]


def kernel(feat, xs_hbm, ys_hbm, slm_hbm, tlm_hbm, rows_hbm, out, f_out, g_out,
           xs, ys, slm, tlm, score, hcol, weights, teach, part, rbuf, cbuf, vec, tmp4, qbuf,
           xfar, xnear, asum, zfar, znear, bfar, bnear, bsum, bx, rcol,
           load_sem, in_sem, rs_sem, rr_sem, cs_sem, cr_sem, qs_sem, qr_sem,
           as_sem, ar_sem, zs_sem, zr_sem, bs_sem, br_sem, bxs_sem, bxr_sem,
           zall, stage, gath, pscore, pweights, pteach, kvec, hsend, hrecv,
           gs_sem, gr_sem, ds_sem, dr_sem, ys_sem, yr_sem, ks_sem, kr_sem, hs_sem, hr_sem):
    src = lax.axis_index("src")
    tgt = lax.axis_index("tgt")
    y, c = lax.div(src, 2), lax.rem(src, 2)
    x, z = lax.div(tgt, NZ), lax.rem(tgt, NZ)
    xi = [lax.rem(x + d, NX) for d in range(NX)]
    zi = [lax.rem(z + d, NZ) for d in range(NZ)]

    def at_tgt(dx, dz):
        return (src, xi[dx % NX] * NZ + zi[dz % NZ])

    def at_src(dy, dc):
        return (lax.rem(y + dy, NY) * 2 + lax.rem(c + dc, 2), tgt)

    def hops(d, n):
        return min(d, n - d)

    tgt_peers = sorted([(dx, dz) for dx in range(NX) for dz in range(NZ) if dx or dz],
                       key=lambda o: -hops(o[0], NX) - hops(o[1], NZ))
    src_peers = sorted([(dy, dc) for dy in range(NY) for dc in range(2) if dy or dc],
                       key=lambda o: -hops(o[0], NY) - 0.1 * o[1])

    loads = [pltpu.make_async_copy(a, b, in_sem.at[n]) for n, (a, b) in enumerate(
        ((ys_hbm, ys), (xs_hbm, xs), (slm_hbm, slm), (tlm_hbm, tlm)))]
    for copy in loads:
        copy.start()
    load = pltpu.make_async_copy(rows_hbm, teach, load_sem)
    load.start()
    barrier = pltpu.get_barrier_semaphore()
    for o in tgt_peers:
        pl.semaphore_signal(barrier, inc=1, device_id=at_tgt(*o), device_id_type=MESH)
    for o in src_peers:
        pl.semaphore_signal(barrier, inc=1, device_id=at_src(*o), device_id_type=MESH)

    def remote(a, b, ssem, rsem, dev):
        pltpu.make_async_remote_copy(src_ref=a, dst_ref=b, send_sem=ssem, recv_sem=rsem,
                                     device_id=dev, device_id_type=MESH).start()

    def arrive(ref, sem):
        pltpu.make_async_copy(ref, ref, sem).wait()

    def row_exchange(e, value, meanwhile=None):
        rbuf[e, tgt] = value
        for o in tgt_peers:
            remote(rbuf.at[e, tgt], rbuf.at[e, tgt], rs_sem.at[e], rr_sem.at[e], at_tgt(*o))
        if meanwhile is not None:
            meanwhile()
        arrive(rbuf.at[e, pl.ds(0, 31)], rr_sem.at[e])
        return rbuf[e]

    def col_exchange(e, value, meanwhile=None):
        cbuf[e, src] = value
        for o in src_peers:
            remote(cbuf.at[e, src], cbuf.at[e, src], cs_sem.at[e], cr_sem.at[e], at_src(*o))
        if meanwhile is not None:
            meanwhile()
        arrive(cbuf.at[e, pl.ds(0, 7)], cr_sem.at[e])
        return cbuf[e]

    def lse2(parts):
        peak = jnp.max(parts, axis=0)
        return peak + jnp.log(jnp.sum(jnp.exp2(parts - peak), axis=0)) * LOG2E

    def col_form(row):
        return jnp.broadcast_to(row, (LANES, LANES)).T

    side = 1 - 2 * lax.rem(x, 2)
    mate_x = [lax.rem(x + side + NX, NX), lax.rem(x - side + NX, NX)]
    mates = [(src, m * NZ + z) for m in mate_x]
    sibling = (y * 2 + 1 - c, tgt)
    mine = pl.ds(c * HALF, HALF)

    def shared(u):
        return u < 2 or u >= 2 + NEAR

    def gather_send(*units):
        for u in units:
            at = (u, y) if shared(u) else (u,)
            remote(stage.at[at], gath.at[(u, c) + at[1:]], gs_sem.at[u], gr_sem.at[u], mates[u % 2])

    def gather_spread(*units):
        for u in units:
            arrive(gath.at[u, 0, 0], gr_sem.at[u])
            for d in (2, 1, 3):
                remote(gath.at[u, c, y], gath.at[u, c, y], ys_sem.at[u], yr_sem.at[u], at_src(d, 0))

    def gather_share(*units):
        for u in units:
            if shared(u):
                arrive(gath.at[u, 0, pl.ds(0, 3)], yr_sem.at[u])
            else:
                arrive(gath.at[u, 0], gr_sem.at[u])
            remote(gath.at[u, c], gath.at[u, c], ds_sem.at[u], dr_sem.at[u], sibling)

    def gather_end(u):
        arrive(gath.at[u, 0], dr_sem.at[u])

    def lanes(k):
        return slice(k * LANES, (k + 1) * LANES)

    def fold(t):
        return t.reshape(LANES // 8, 8, LANES)

    for copy in loads:
        copy.wait()
    slm2 = slm[...] * LOG2E
    tlm2 = tlm[...] * LOG2E
    norm_scale = LOG2E / (feat * EPS)
    for a in range(BLK):
        xf = xs[pl.ds(a * LANES, LANES), :].astype(jnp.float32)
        yf = ys[pl.ds(a * LANES, LANES), :].astype(jnp.float32)
        vec[0, pl.ds(a, 1), :] = jnp.sum((xf * xf).T, axis=0, keepdims=True)
        vec[1, pl.ds(a, 1), :] = jnp.sum((yf * yf).T, axis=0, keepdims=True)
    nx2 = vec[0] * norm_scale
    ny2 = vec[1] * norm_scale
    bias = tlm2 - ny2

    for a in range(BLK):
        d = lax.dot_general(xs[pl.ds(a * LANES, LANES), :], ys[...], (((1,), (1,)), ((), ())),
                            preferred_element_type=jnp.float32)
        e = d * (2.0 * norm_scale)
        score[a] = e
        t = [e[:, lanes(k)] + bias[k:k + 1, :] for k in range(BLK)]
        m = functools.reduce(jnp.maximum, t)
        m = jnp.max(m, axis=1, keepdims=True)
        s = functools.reduce(jnp.add, [jnp.exp2(v - m) for v in t])
        s = jnp.sum(s, axis=1, keepdims=True)
        lse = m + jnp.log(s) * LOG2E
        vec[2, pl.ds(a, 1), :] = jnp.broadcast_to(lse, (LANES, LANES)).T[0:1, :]
    stage[0] = ys[mine, :].astype(jnp.float32).reshape(4, LANES, LANES)
    stage[1] = stage[0]
    load.wait()
    for n, ch in enumerate(chunks_of("H")):
        stage[2 + n] = teach[mine, lanes(ch)].astype(jnp.float32).reshape(4, LANES, LANES)
    pl.semaphore_wait(barrier, len(tgt_peers) + len(src_peers))
    row2 = lse2(row_exchange(0, vec[2]))
    vec[6] = row2
    gather_send(0, 1, 2, 3)

    h = slm2 - row2
    peaks = [jnp.full((8, LANES), -jnp.inf, jnp.float32)] * BLK
    for a in range(BLK):
        hc = col_form(h[a:a + 1, :])
        hcol[a] = hc
        for k in range(BLK):
            peaks[k] = jnp.maximum(peaks[k], jnp.max(fold(score[a, :, lanes(k)] + hc), axis=0))
    peaks = [jnp.max(p, axis=0, keepdims=True) for p in peaks]
    sums = [jnp.zeros((8, LANES), jnp.float32)] * BLK
    for a in range(BLK):
        hc = hcol[a]
        for k in range(BLK):
            sums[k] = sums[k] + jnp.sum(fold(jnp.exp2(score[a, :, lanes(k)] + hc - peaks[k])), axis=0)
    for k in range(BLK):
        total = jnp.sum(sums[k], axis=0, keepdims=True)
        vec[3, pl.ds(k, 1), :] = peaks[k] + jnp.log(total) * LOG2E
    col2 = lse2(col_exchange(0, vec[3]))
    gather_spread(0, 1)

    tmass = jnp.exp(tlm[...])
    smass = jnp.exp(slm[...])
    for a in range(BLK):
        lc = col_form(row2[a:a + 1, :])
        acc = None
        for k in range(BLK):
            q = jnp.exp2(score[a, :, lanes(k)] - lc - col2[k:k + 1, :])
            score[a, :, lanes(k)] = q
            q = q * tmass[k:k + 1, :]
            acc = q if acc is None else acc + q
        vec[4, pl.ds(a, 1), :] = jnp.sum(acc.T, axis=0, keepdims=True)

    def row_step(v):
        for a in range(BLK):
            acc = None
            for k in range(BLK):
                q = score[a, :, lanes(k)] * v[k:k + 1, :]
                acc = q if acc is None else acc + q
            vec[4, pl.ds(a, 1), :] = jnp.sum(acc.T, axis=0, keepdims=True)

    def col_step(u):
        acc = [jnp.zeros((8, LANES), jnp.float32)] * BLK
        for a in range(BLK):
            uc = col_form(u[a:a + 1, :])
            for k in range(BLK):
                acc[k] = acc[k] + jnp.sum(fold(score[a, :, lanes(k)] * uc), axis=0)
        for k in range(BLK):
            vec[5, pl.ds(k, 1), :] = jnp.sum(acc[k], axis=0, keepdims=True)

    def mate_scores():
        for kind in range(2):
            gather_end(kind)
            feats = gath[kind].reshape(TILE, LANES).astype(jnp.bfloat16)
            for part_at, xb in enumerate((x, mate_x[1 - kind])):
                d = lax.dot_general(xs[pl.ds(xb * 256, 256), :], feats, (((1,), (1,)), ((), ())),
                                    preferred_element_type=jnp.float32)
                pscore[kind, pl.ds(part_at * 256, 256), :] = d * (2.0 * norm_scale)

    def take(n):
        gather_end(2 + n)
        pteach[n] = gath[2 + n].reshape(TILE, LANES).astype(jnp.bfloat16)

    def mate_weights():
        for kind in range(2):
            arrive(kvec.at[1 + kind], kr_sem.at[kind])
            for b in range(4):
                xb = (x, mate_x[1 - kind])[b // 2]
                lc = col_form(vec[6, pl.ds(2 * xb + b % 2, 1), :])
                for k in range(BLK):
                    w = jnp.exp2(pscore[kind, pl.ds(b * LANES, LANES), lanes(k)] - lc + kvec[1 + kind, k:k + 1, :])
                    pweights[kind, pl.ds(b * LANES, LANES), lanes(k)] = w.astype(jnp.bfloat16)

    def during_col1():
        take(0)
        take(1)
        gather_share(0, 1)

    def during_row2():
        mate_scores()
        gather_share(4, 5)

    def during_col2():
        take(2)
        take(3)

    r = jnp.sum(row_exchange(1, vec[4], lambda: gather_share(2, 3)), axis=0)
    gather_send(4, 5)
    col_step(smass / r)
    cs = jnp.sum(col_exchange(1, vec[5], during_col1), axis=0)
    row_step(tmass / cs)
    r = jnp.sum(row_exchange(2, vec[4], during_row2), axis=0)
    gather_send(*range(6, 2 + NH))
    f_out[...] = (nx2 - row2) * (EPS * LN2) - EPS * jnp.log(r)
    col_step(smass / r)
    cs = jnp.sum(col_exchange(2, vec[5], during_col2), axis=0)
    kvec[0] = tlm2 - jnp.log(cs) * LOG2E - col2
    for kind in range(2):
        remote(kvec.at[0], kvec.at[1 + kind], ks_sem.at[kind], kr_sem.at[kind], mates[kind])
    gather_spread(*range(6, 2 + NH))
    g_out[...] = (ny2 - col2) * (EPS * LN2) - EPS * jnp.log(cs)

    v = tmass / cs
    for a in range(BLK):
        acc = None
        for k in range(BLK):
            q = (score[a, :, lanes(k)] * v[k:k + 1, :]).astype(jnp.bfloat16)
            weights[pl.ds(a * LANES, LANES), lanes(k)] = q
            q = q.astype(jnp.float32)
            acc = q if acc is None else acc + q
        tmp4[a // 2, pl.ds(a % 2, 1), :] = jnp.sum(acc.T, axis=0, keepdims=True)

    def project(ch):
        p = jnp.dot(weights[...], teach[:, ch * LANES:(ch + 2) * LANES], preferred_element_type=jnp.float32)
        part[ch] = p[:, :LANES].reshape(NX, NZ, ROWS, LANES)
        part[ch + 1] = p[:, LANES:].reshape(NX, NZ, ROWS, LANES)

    lo, hi = pl.ds(0, 4), pl.ds(4, 4)
    xr, xl = at_tgt(1, 0), at_tgt(-1, 0)
    zr, zl = at_tgt(0, 1), at_tgt(0, -1)

    def a_start(i, ch):
        remote(part.at[ch, xi[2], lo], xfar.at[i, 0], as_sem.at[i], ar_sem.at[i, 0], xr)
        remote(part.at[ch, xi[2], hi], xfar.at[i, 1], as_sem.at[i], ar_sem.at[i, 1], xl)

    def a_own(i, ch):
        remote(part.at[ch, xi[1], hi], xnear.at[i, 0, hi], as_sem.at[i], ar_sem.at[i, 2], xr)
        remote(part.at[ch, xi[3], lo], xnear.at[i, 1, lo], as_sem.at[i], ar_sem.at[i, 3], xl)

    def a_pass(i, ch, way):
        dev, dst, half = ((xr, xi[1], lo), (xl, xi[3], hi))[way]
        arrive(xfar.at[i, way], ar_sem.at[i, way])
        part[ch, dst, half] = part[ch, dst, half] + xfar[i, way]
        remote(part.at[ch, dst, half], xnear.at[i, way, half], as_sem.at[i], ar_sem.at[i, 2 + way], dev)

    def a_mid(i, ch):
        arrive(xnear.at[i, 0], ar_sem.at[i, 2])
        arrive(xnear.at[i, 1], ar_sem.at[i, 3])
        asum[i] = part[ch, x] + xnear[i, 0] + xnear[i, 1]
        z_start(i, ch)

    def a_ring(i, ch, step, way):
        dev, dst = ((zr, zi[4 - step]), (zl, zi[4 + step]))[way]
        if step == 1:
            arrive(zfar.at[i, way], zr_sem.at[i, way, 0])
            half = pl.ds(16 * way, 16)
            asum[i, dst, half] = asum[i, dst, half] + zfar[i, way]
        else:
            arrive(znear.at[i, way, step - 2], zr_sem.at[i, way, step - 1])
            asum[i, dst] = asum[i, dst] + znear[i, way, step - 2]
        remote(asum.at[i, dst], znear.at[i, way, step - 1], zs_sem.at[i], zr_sem.at[i, way, step], dev)

    def finish(ch, value):
        scale = rcol[lax.div(z, 4), pl.ds(lax.rem(z, 4) * ROWS, ROWS), :]
        out[:, lanes(ch)] = (value * scale).astype(jnp.bfloat16)

    def a_end(i, ch):
        arrive(znear.at[i, 0, 2], zr_sem.at[i, 0, 3])
        arrive(znear.at[i, 1, 2], zr_sem.at[i, 1, 3])
        finish(ch, asum[i, z] + znear[i, 0, 2] + znear[i, 1, 2])

    ends = (pl.ds(0, 2), pl.ds(2, 2))

    def b_start(i, ch):
        for way, dev in ((0, zr), (1, zl)):
            remote(part.at[ch, ends[way], zi[4]], bfar.at[i, way], bs_sem.at[i], br_sem.at[i, way, 0], dev)

    def b_own(i, ch):
        for way, dev, near in ((0, zr, zi[3]), (1, zl, zi[5])):
            own = 1 - way
            remote(part.at[ch, ends[own], near], bnear.at[i, way, 0, ends[own]], bs_sem.at[i], br_sem.at[i, way, 1], dev)

    def b_ring(i, ch, step, way):
        dev, dst = ((zr, zi[4 - step]), (zl, zi[4 + step]))[way]
        if step == 1:
            arrive(bfar.at[i, way], br_sem.at[i, way, 0])
            part[ch, ends[way], dst] = part[ch, ends[way], dst] + bfar[i, way]
            remote(part.at[ch, ends[way], dst], bnear.at[i, way, 0, ends[way]], bs_sem.at[i], br_sem.at[i, way, 1], dev)
        else:
            arrive(bnear.at[i, way, step - 2], br_sem.at[i, way, step - 1])
            part[ch, :, dst] = part[ch, :, dst] + bnear[i, way, step - 2]
            remote(part.at[ch, :, dst], bnear.at[i, way, step - 1], bs_sem.at[i], br_sem.at[i, way, step], dev)

    def b_mid(i, ch):
        arrive(bnear.at[i, 0, 2], br_sem.at[i, 0, 3])
        arrive(bnear.at[i, 1, 2], br_sem.at[i, 1, 3])
        bsum[i] = part[ch, :, z] + bnear[i, 0, 2] + bnear[i, 1, 2]
        for d in (2, 1, 3):
            remote(bsum.at[i, xi[d]], bx.at[i, d - 1], bxs_sem.at[i], bxr_sem.at[i], at_tgt(d, 0))

    def b_end(i, ch):
        arrive(bx.at[i], bxr_sem.at[i])
        finish(ch, bsum[i, x] + bx[i, 0] + bx[i, 1] + bx[i, 2])

    def h_start(n, ch):
        kind = n % 2
        for part_at, xb in enumerate((x, mate_x[1 - kind])):
            p = jnp.dot(weights[pl.ds(xb * 256, 256), :], teach[:, lanes(ch)], preferred_element_type=jnp.float32)
            p = p + jnp.dot(pweights[kind, pl.ds(part_at * 256, 256), :], pteach[n], preferred_element_type=jnp.float32)
            if part_at == 0:
                asum[NA + n] = p.reshape(NZ, ROWS, LANES)
            else:
                hsend[n] = p.reshape(NZ, ROWS, LANES)
        remote(hsend.at[n], hrecv.at[n], hs_sem.at[n], hr_sem.at[n], mates[1 - kind])

    def z_start(i, ch):
        if ch in DIRECT:
            for d in (4, 3, 5, 2, 6, 1, 7):
                remote(asum.at[i, zi[d]], zall.at[DIRECT.index(ch), d - 1], zs_sem.at[i], zr_sem.at[i, 0, 0], at_tgt(0, d))
        else:
            remote(asum.at[i, zi[4], pl.ds(0, 16)], zfar.at[i, 0], zs_sem.at[i], zr_sem.at[i, 0, 0], zr)
            remote(asum.at[i, zi[4], pl.ds(16, 16)], zfar.at[i, 1], zs_sem.at[i], zr_sem.at[i, 1, 0], zl)

    def a_direct(i, ch):
        n = DIRECT.index(ch)
        arrive(zall.at[n], zr_sem.at[i, 0, 0])
        total = asum[i, z]
        for d in range(7):
            total = total + zall[n, d]
        finish(ch, total)

    def h_mid(n, ch):
        arrive(hrecv.at[n], hr_sem.at[n])
        asum[NA + n] = asum[NA + n] + hrecv[n]
        z_start(NA + n, ch)

    def q_start():
        for d in (2, 1, 3):
            remote(tmp4.at[xi[d]], qbuf.at[d - 1], qs_sem.at[0], qr_sem.at[0], at_tgt(d, 0))

    def q_mid():
        arrive(qbuf.at[pl.ds(0, 3)], qr_sem.at[0])
        tmp4[x] = tmp4[x] + qbuf[0] + qbuf[1] + qbuf[2]
        for d in (4, 3, 5, 2, 6, 1, 7):
            remote(tmp4.at[x], qbuf.at[2 + d], qs_sem.at[1], qr_sem.at[1], at_tgt(0, d))

    def q_end():
        arrive(qbuf.at[pl.ds(3, 7)], qr_sem.at[1])
        total = tmp4[x]
        for d in range(7):
            total = total + qbuf[3 + d]
        rcol[0] = col_form(1.0 / total[0:1, :])
        rcol[1] = col_form(1.0 / total[1:2, :])

    steps = dict(ad=a_direct, hm=h_mid, ap=a_pass, am=a_mid, ar=a_ring, ae=a_end, br=b_ring, bm=b_mid, be=b_end)
    ready = set()
    q_start()
    for name, ch, *rest in SCHEDULE:
        if name == "qm":
            q_mid()
        elif name == "qe":
            q_end()
        elif name == "hw":
            mate_weights()
        elif name == "hf":
            gather_share(6 + 2 * ch, 7 + 2 * ch)
        elif name == "ht":
            take(4 + 2 * ch)
            take(5 + 2 * ch)
        elif name == "ao":
            a_own(KINDS[:ch].count("A"), ch)
        elif name == "bo":
            b_own(KINDS[:ch].count("B"), ch)
        elif name == "s" and KINDS[ch] == "H":
            h_start(KINDS[:ch].count("H"), ch)
        elif name == "s":
            if ch // 2 not in ready:
                ready.add(ch // 2)
                project(ch // 2 * 2)
            (a_start if KINDS[ch] == "A" else b_start)(KINDS[:ch].count(KINDS[ch]), ch)
        elif KINDS[ch] == "H" and name in ("ar", "ae", "ad"):
            steps[name](NA + KINDS[:ch].count("H"), ch, *rest)
        else:
            steps[name](KINDS[:ch].count(KINDS[ch]), ch, *rest)

    for e in range(3):
        arrive(rbuf.at[e, pl.ds(0, 31)], rs_sem.at[e])
        arrive(cbuf.at[e, pl.ds(0, 7)], cs_sem.at[e])
    arrive(qbuf.at[pl.ds(0, 3)], qs_sem.at[0])
    arrive(qbuf.at[pl.ds(3, 7)], qs_sem.at[1])
    for i, ch in enumerate(chunks_of("A")):
        arrive(part.at[ch, pl.ds(0, 3)], as_sem.at[i])
    for i in range(NA + NH):
        arrive(asum.at[i, pl.ds(0, 7)], zs_sem.at[i])
    for n in range(NH):
        arrive(hsend.at[n], hs_sem.at[n])
    for u in range(2 + NH):
        if shared(u):
            arrive(stage.at[u, 0], gs_sem.at[u])
            arrive(gath.at[u, 0, pl.ds(0, 3)], ys_sem.at[u])
        else:
            arrive(stage.at[u], gs_sem.at[u])
        arrive(stage.at[u], ds_sem.at[u])
    for kind in range(2):
        arrive(kvec.at[0], ks_sem.at[kind])
    for i, ch in enumerate(chunks_of("B")):
        arrive(part.at[ch, :, pl.ds(0, 7)], bs_sem.at[i])
        arrive(bx.at[i], bxs_sem.at[i])


def settle(*refs):
    sem = refs[-1]
    copies = [pltpu.make_async_copy(refs[n], refs[3 + n], sem.at[n]) for n in range(3)]
    for copy in copies:
        copy.start()
    for copy in copies:
        copy.wait()


def body(source_features, target_features, source_logmass, target_logmass, teacher_rows):
    na, nb, nz = NA, KINDS.count("B"), NA + NH
    f32 = jnp.float32
    vmem = pl.BlockSpec(memory_space=pltpu.VMEM)
    dma = pltpu.SemaphoreType.DMA
    projected, f, g = pl.pallas_call(
        functools.partial(kernel, source_features.shape[1]),
        out_shape=(
            jax.ShapeDtypeStruct((ROWS, CHUNKS * LANES), jnp.bfloat16),
            jax.ShapeDtypeStruct((BLK, LANES), f32),
            jax.ShapeDtypeStruct((BLK, LANES), f32),
        ),
        in_specs=[pl.BlockSpec(memory_space=pltpu.HBM)] * 5,
        out_specs=(vmem, vmem, vmem),
        scratch_shapes=[
            pltpu.VMEM(source_features.shape, source_features.dtype),
            pltpu.VMEM(target_features.shape, target_features.dtype),
            pltpu.VMEM((BLK, LANES), f32),
            pltpu.VMEM((BLK, LANES), f32),
            pltpu.VMEM((BLK, LANES, TILE), f32),
            pltpu.VMEM((BLK, LANES, LANES), f32),
            pltpu.VMEM((TILE, TILE), jnp.bfloat16),
            pltpu.VMEM((TILE, CHUNKS * LANES), jnp.bfloat16),
            pltpu.VMEM((CHUNKS, NX, NZ, ROWS, LANES), f32),
            pltpu.VMEM((3, 32, BLK, LANES), f32),
            pltpu.VMEM((3, 8, BLK, LANES), f32),
            pltpu.VMEM((7, BLK, LANES), f32),
            pltpu.VMEM((NX, 2, LANES), f32),
            pltpu.VMEM((10, 2, LANES), f32),
            pltpu.VMEM((na, 2, 4, ROWS, LANES), f32),
            pltpu.VMEM((na, 2, NZ, ROWS, LANES), f32),
            pltpu.VMEM((nz, NZ, ROWS, LANES), f32),
            pltpu.VMEM((nz, 2, ROWS // 2, LANES), f32),
            pltpu.VMEM((nz, 2, 3, ROWS, LANES), f32),
            pltpu.VMEM((nb, 2, 2, ROWS, LANES), f32),
            pltpu.VMEM((nb, 2, 3, NX, ROWS, LANES), f32),
            pltpu.VMEM((nb, NX, ROWS, LANES), f32),
            pltpu.VMEM((nb, 3, ROWS, LANES), f32),
            pltpu.VMEM((2, LANES, LANES), f32),
            dma, dma((4,)), dma((3,)), dma((3,)), dma((3,)), dma((3,)), dma((2,)), dma((2,)),
            dma((na,)), dma((na, 4)), dma((nz,)), dma((nz, 2, 4)),
            dma((nb,)), dma((nb, 2, 4)), dma((nb,)), dma((nb,)),
            pltpu.VMEM((max(1, len(DIRECT)), 7, ROWS, LANES), f32),
            pltpu.VMEM((2 + NH, 4, LANES, LANES), f32),
            pltpu.VMEM((2 + NH, 2, 4, LANES, LANES), f32),
            pltpu.VMEM((2, HALF, TILE), f32),
            pltpu.VMEM((2, HALF, TILE), jnp.bfloat16),
            pltpu.VMEM((NH, TILE, LANES), jnp.bfloat16),
            pltpu.VMEM((3, BLK, LANES), f32),
            pltpu.VMEM((NH, NZ, ROWS, LANES), f32),
            pltpu.VMEM((NH, NZ, ROWS, LANES), f32),
            dma((2 + NH,)), dma((2 + NH,)), dma((2 + NH,)), dma((2 + NH,)), dma((2 + NH,)), dma((2 + NH,)), dma((2,)), dma((2,)), dma((NH,)), dma((NH,)),
        ],
        compiler_params=pltpu.CompilerParams(
            collective_id=0, has_side_effects=True, vmem_limit_bytes=(64 * 1024 - 192) * 1024),
    )(source_features, target_features, source_logmass.reshape(BLK, LANES),
      target_logmass.reshape(BLK, LANES), teacher_rows)
    return pl.pallas_call(
        settle,
        out_shape=(
            jax.ShapeDtypeStruct(projected.shape, jnp.bfloat16),
            jax.ShapeDtypeStruct((TILE,), f32),
            jax.ShapeDtypeStruct((TILE,), f32),
        ),
        in_specs=[vmem] * 3,
        out_specs=(pl.BlockSpec(memory_space=pl.ANY),) * 3,
        scratch_shapes=[dma((3,))],
    )(projected, f.reshape(TILE), g.reshape(TILE))


def solution(mesh):
    in_specs = (P("src", None), P("tgt", None), P("src"), P("tgt"), P("tgt", None))
    out_specs = (P(("src", "tgt"), None), P("src"), P("tgt"))
    return jax.shard_map(body, mesh=mesh, in_specs=in_specs, out_specs=out_specs, check_vma=False)
```

```python
import functools
import math

import jax
import jax.numpy as jnp
from jax import lax
from jax.experimental import pallas as pl
from jax.experimental.pallas import tpu as pltpu
from jax.sharding import PartitionSpec as P

MESH = pl.DeviceIdType.MESH
EPS = 0.1
LOG2E = math.log2(math.e)
LN2 = math.log(2.0)
NX, NY, NZ = 4, 4, 8
LANES = 128
TILE = 1024
BLK = TILE // LANES
ROWS = 32
HALF = TILE // 2
NEAR = 4
CHUNKS = 12
KINDS = "ABBABAHHHHHH"
DIRECT = (2, 4, 5)
SCHEDULE = (
    ("s", 0), ("s", 1), ("s", 2), ("ao", 0), ("bo", 1), ("bo", 2), ("s", 3), ("qm", 0), ("s", 4), ("ao", 3),
    ("bo", 4), ("br", 1, 1, 0), ("br", 1, 1, 1), ("hw", 0), ("s", 6), ("br", 2, 1, 0), ("br", 2, 1, 1), ("ap", 0, 0),
    ("ap", 0, 1), ("hf", 0), ("br", 4, 1, 0), ("br", 4, 1, 1), ("s", 7), ("ap", 3, 0), ("ap", 3, 1), ("br", 1, 2, 0),
    ("br", 1, 2, 1), ("s", 8), ("br", 2, 2, 0), ("br", 2, 2, 1), ("br", 4, 2, 0), ("br", 4, 2, 1), ("s", 9),
    ("hm", 6), ("br", 1, 3, 0), ("br", 1, 3, 1), ("ht", 0), ("s", 10), ("hm", 7), ("br", 2, 3, 0), ("br", 2, 3, 1),
    ("am", 0), ("s", 11), ("am", 3), ("br", 4, 3, 0), ("br", 4, 3, 1), ("ar", 6, 1, 0), ("ar", 6, 1, 1), ("s", 5),
    ("ao", 5), ("bm", 1), ("ar", 7, 1, 0), ("hm", 9), ("hm", 8), ("ar", 7, 1, 1), ("bm", 2), ("ar", 0, 1, 0),
    ("ar", 0, 1, 1), ("ar", 3, 1, 0), ("ar", 3, 1, 1), ("hm", 11), ("bm", 4), ("hm", 10), ("ar", 6, 2, 0),
    ("ar", 6, 2, 1), ("ar", 9, 1, 0), ("ar", 9, 1, 1), ("ar", 8, 1, 0), ("ar", 8, 1, 1), ("ap", 5, 0), ("ap", 5, 1),
    ("ar", 7, 2, 0), ("ar", 7, 2, 1), ("ar", 0, 2, 0), ("ar", 0, 2, 1), ("ar", 3, 2, 0), ("ar", 3, 2, 1),
    ("ar", 11, 1, 0), ("ar", 11, 1, 1), ("ar", 10, 1, 0), ("ar", 10, 1, 1), ("ar", 6, 3, 0), ("qe", 0), ("be", 1),
    ("ar", 6, 3, 1), ("ar", 9, 2, 0), ("ar", 9, 2, 1), ("ar", 8, 2, 0), ("be", 2), ("ar", 8, 2, 1), ("ar", 7, 3, 0),
    ("ar", 7, 3, 1), ("ar", 0, 3, 0), ("be", 4), ("ar", 0, 3, 1), ("ar", 3, 3, 0), ("ar", 3, 3, 1), ("ar", 11, 2, 0),
    ("ar", 11, 2, 1), ("ar", 10, 2, 0), ("ar", 10, 2, 1), ("am", 5), ("ae", 6), ("ar", 9, 3, 0), ("ar", 9, 3, 1),
    ("ar", 8, 3, 0), ("ar", 8, 3, 1), ("ae", 7), ("ae", 0), ("ae", 3), ("ar", 11, 3, 0), ("ar", 11, 3, 1),
    ("ar", 10, 3, 0), ("ar", 10, 3, 1), ("ad", 5), ("ae", 9), ("ae", 8), ("ae", 11), ("ae", 10),
)
NA, NH = KINDS.count("A"), KINDS.count("H")


def chunks_of(kind):
    return [ch for ch in range(CHUNKS) if KINDS[ch] == kind]


def kernel(feat, xs_hbm, ys_hbm, slm_hbm, tlm_hbm, rows_hbm, out, f_out, g_out,
           xs, ys, slm, tlm, score, hcol, weights, teach, part, rbuf, cbuf, vec, tmp4, qbuf,
           xfar, xnear, asum, zfar, znear, bfar, bnear, bsum, bx, rcol,
           load_sem, in_sem, rs_sem, rr_sem, cs_sem, cr_sem, qs_sem, qr_sem,
           as_sem, ar_sem, zs_sem, zr_sem, bs_sem, br_sem, bxs_sem, bxr_sem,
           zall, stage, gath, pscore, pweights, pteach, kvec, hsend, hrecv,
           gs_sem, gr_sem, ds_sem, dr_sem, ys_sem, yr_sem, ks_sem, kr_sem, hs_sem, hr_sem):
    src = lax.axis_index("src")
    tgt = lax.axis_index("tgt")
    y, c = lax.div(src, 2), lax.rem(src, 2)
    x, z = lax.div(tgt, NZ), lax.rem(tgt, NZ)
    xi = [lax.rem(x + d, NX) for d in range(NX)]
    zi = [lax.rem(z + d, NZ) for d in range(NZ)]

    def at_tgt(dx, dz):
        return (src, xi[dx % NX] * NZ + zi[dz % NZ])

    def at_src(dy, dc):
        return (lax.rem(y + dy, NY) * 2 + lax.rem(c + dc, 2), tgt)

    def hops(d, n):
        return min(d, n - d)

    tgt_peers = sorted([(dx, dz) for dx in range(NX) for dz in range(NZ) if dx or dz],
                       key=lambda o: -hops(o[0], NX) - hops(o[1], NZ))
    src_peers = sorted([(dy, dc) for dy in range(NY) for dc in range(2) if dy or dc],
                       key=lambda o: -hops(o[0], NY) - 0.1 * o[1])

    loads = [pltpu.make_async_copy(a, b, in_sem.at[n]) for n, (a, b) in enumerate(
        ((ys_hbm, ys), (xs_hbm, xs), (slm_hbm, slm), (tlm_hbm, tlm)))]
    for copy in loads:
        copy.start()
    load = pltpu.make_async_copy(rows_hbm, teach, load_sem)
    load.start()
    barrier = pltpu.get_barrier_semaphore()
    for o in tgt_peers:
        pl.semaphore_signal(barrier, inc=1, device_id=at_tgt(*o), device_id_type=MESH)
    for o in src_peers:
        pl.semaphore_signal(barrier, inc=1, device_id=at_src(*o), device_id_type=MESH)

    def remote(a, b, ssem, rsem, dev):
        pltpu.make_async_remote_copy(src_ref=a, dst_ref=b, send_sem=ssem, recv_sem=rsem,
                                     device_id=dev, device_id_type=MESH).start()

    def arrive(ref, sem):
        pltpu.make_async_copy(ref, ref, sem).wait()

    def row_exchange(e, value, meanwhile=None):
        rbuf[e, tgt] = value
        for o in tgt_peers:
            remote(rbuf.at[e, tgt], rbuf.at[e, tgt], rs_sem.at[e], rr_sem.at[e], at_tgt(*o))
        if meanwhile is not None:
            meanwhile()
        arrive(rbuf.at[e, pl.ds(0, 31)], rr_sem.at[e])
        return rbuf[e]

    def col_exchange(e, value, meanwhile=None):
        cbuf[e, src] = value
        for o in src_peers:
            remote(cbuf.at[e, src], cbuf.at[e, src], cs_sem.at[e], cr_sem.at[e], at_src(*o))
        if meanwhile is not None:
            meanwhile()
        arrive(cbuf.at[e, pl.ds(0, 7)], cr_sem.at[e])
        return cbuf[e]

    def lse2(parts):
        peak = jnp.max(parts, axis=0)
        return peak + jnp.log(jnp.sum(jnp.exp2(parts - peak), axis=0)) * LOG2E

    def col_form(row):
        return jnp.broadcast_to(row, (LANES, LANES)).T

    side = 1 - 2 * lax.rem(x, 2)
    mate_x = [lax.rem(x + side + NX, NX), lax.rem(x - side + NX, NX)]
    mates = [(src, m * NZ + z) for m in mate_x]
    sibling = (y * 2 + 1 - c, tgt)
    mine = pl.ds(c * HALF, HALF)

    def shared(u):
        return u < 2 or u >= 2 + NEAR

    def gather_send(*units):
        for u in units:
            at = (u, y) if shared(u) else (u,)
            remote(stage.at[at], gath.at[(u, c) + at[1:]], gs_sem.at[u], gr_sem.at[u], mates[u % 2])

    def gather_spread(*units):
        for u in units:
            arrive(gath.at[u, 0, 0], gr_sem.at[u])
            for d in (2, 1, 3):
                remote(gath.at[u, c, y], gath.at[u, c, y], ys_sem.at[u], yr_sem.at[u], at_src(d, 0))

    def gather_share(*units):
        for u in units:
            if shared(u):
                arrive(gath.at[u, 0, pl.ds(0, 3)], yr_sem.at[u])
            else:
                arrive(gath.at[u, 0], gr_sem.at[u])
            remote(gath.at[u, c], gath.at[u, c], ds_sem.at[u], dr_sem.at[u], sibling)

    def gather_end(u):
        arrive(gath.at[u, 0], dr_sem.at[u])

    def lanes(k):
        return slice(k * LANES, (k + 1) * LANES)

    def fold(t):
        return t.reshape(LANES // 8, 8, LANES)

    for copy in loads:
        copy.wait()
    slm2 = slm[...] * LOG2E
    tlm2 = tlm[...] * LOG2E
    norm_scale = LOG2E / (feat * EPS)
    for a in range(BLK):
        xf = xs[pl.ds(a * LANES, LANES), :].astype(jnp.float32)
        yf = ys[pl.ds(a * LANES, LANES), :].astype(jnp.float32)
        vec[0, pl.ds(a, 1), :] = jnp.sum((xf * xf).T, axis=0, keepdims=True)
        vec[1, pl.ds(a, 1), :] = jnp.sum((yf * yf).T, axis=0, keepdims=True)
    nx2 = vec[0] * norm_scale
    ny2 = vec[1] * norm_scale
    bias = tlm2 - ny2

    for a in range(BLK):
        d = lax.dot_general(xs[pl.ds(a * LANES, LANES), :], ys[...], (((1,), (1,)), ((), ())),
                            preferred_element_type=jnp.float32)
        e = d * (2.0 * norm_scale)
        score[a] = e
        t = [e[:, lanes(k)] + bias[k:k + 1, :] for k in range(BLK)]
        m = functools.reduce(jnp.maximum, t)
        m = jnp.max(m, axis=1, keepdims=True)
        s = functools.reduce(jnp.add, [jnp.exp2(v - m) for v in t])
        s = jnp.sum(s, axis=1, keepdims=True)
        lse = m + jnp.log(s) * LOG2E
        vec[2, pl.ds(a, 1), :] = jnp.broadcast_to(lse, (LANES, LANES)).T[0:1, :]
    def fill_stage():
        stage[0] = ys[mine, :].astype(jnp.float32).reshape(4, LANES, LANES)
        stage[1] = stage[0]
        load.wait()
        for n, ch in enumerate(chunks_of("H")):
            stage[2 + n] = teach[mine, lanes(ch)].astype(jnp.float32).reshape(4, LANES, LANES)

    pl.semaphore_wait(barrier, len(tgt_peers) + len(src_peers))
    row2 = lse2(row_exchange(0, vec[2], fill_stage))
    vec[6] = row2
    gather_send(0, 1, 2, 3)

    h = slm2 - row2
    peaks = [jnp.full((8, LANES), -jnp.inf, jnp.float32)] * BLK
    for a in range(BLK):
        hc = col_form(h[a:a + 1, :])
        hcol[a] = hc
        for k in range(BLK):
            peaks[k] = jnp.maximum(peaks[k], jnp.max(fold(score[a, :, lanes(k)] + hc), axis=0))
    peaks = [jnp.max(p, axis=0, keepdims=True) for p in peaks]
    sums = [jnp.zeros((8, LANES), jnp.float32)] * BLK
    for a in range(BLK):
        hc = hcol[a]
        for k in range(BLK):
            sums[k] = sums[k] + jnp.sum(fold(jnp.exp2(score[a, :, lanes(k)] + hc - peaks[k])), axis=0)
    for k in range(BLK):
        total = jnp.sum(sums[k], axis=0, keepdims=True)
        vec[3, pl.ds(k, 1), :] = peaks[k] + jnp.log(total) * LOG2E
    col2 = lse2(col_exchange(0, vec[3]))
    gather_spread(0, 1)

    tmass = jnp.exp(tlm[...])
    smass = jnp.exp(slm[...])
    for a in range(BLK):
        lc = col_form(row2[a:a + 1, :])
        acc = None
        for k in range(BLK):
            q = jnp.exp2(score[a, :, lanes(k)] - lc - col2[k:k + 1, :])
            score[a, :, lanes(k)] = q
            q = q * tmass[k:k + 1, :]
            acc = q if acc is None else acc + q
        vec[4, pl.ds(a, 1), :] = jnp.sum(acc.T, axis=0, keepdims=True)

    def row_step(v):
        for a in range(BLK):
            acc = None
            for k in range(BLK):
                q = score[a, :, lanes(k)] * v[k:k + 1, :]
                acc = q if acc is None else acc + q
            vec[4, pl.ds(a, 1), :] = jnp.sum(acc.T, axis=0, keepdims=True)

    def col_step(u):
        acc = [jnp.zeros((8, LANES), jnp.float32)] * BLK
        for a in range(BLK):
            uc = col_form(u[a:a + 1, :])
            for k in range(BLK):
                acc[k] = acc[k] + jnp.sum(fold(score[a, :, lanes(k)] * uc), axis=0)
        for k in range(BLK):
            vec[5, pl.ds(k, 1), :] = jnp.sum(acc[k], axis=0, keepdims=True)

    def mate_scores():
        for kind in range(2):
            gather_end(kind)
            feats = gath[kind].reshape(TILE, LANES).astype(jnp.bfloat16)
            for part_at, xb in enumerate((x, mate_x[1 - kind])):
                d = lax.dot_general(xs[pl.ds(xb * 256, 256), :], feats, (((1,), (1,)), ((), ())),
                                    preferred_element_type=jnp.float32)
                pscore[kind, pl.ds(part_at * 256, 256), :] = d * (2.0 * norm_scale)

    def take(n):
        gather_end(2 + n)
        pteach[n] = gath[2 + n].reshape(TILE, LANES).astype(jnp.bfloat16)

    def mate_weights():
        for kind in range(2):
            arrive(kvec.at[1 + kind], kr_sem.at[kind])
            for b in range(4):
                xb = (x, mate_x[1 - kind])[b // 2]
                lc = col_form(vec[6, pl.ds(2 * xb + b % 2, 1), :])
                for k in range(BLK):
                    w = jnp.exp2(pscore[kind, pl.ds(b * LANES, LANES), lanes(k)] - lc + kvec[1 + kind, k:k + 1, :])
                    pweights[kind, pl.ds(b * LANES, LANES), lanes(k)] = w.astype(jnp.bfloat16)

    def during_col1():
        take(0)
        take(1)
        gather_share(0, 1)

    def during_row2():
        mate_scores()
        gather_share(4, 5)

    def during_col2():
        take(2)
        take(3)

    r = jnp.sum(row_exchange(1, vec[4], lambda: gather_share(2, 3)), axis=0)
    gather_send(4, 5)
    col_step(smass / r)
    cs = jnp.sum(col_exchange(1, vec[5], during_col1), axis=0)
    row_step(tmass / cs)
    r = jnp.sum(row_exchange(2, vec[4], during_row2), axis=0)
    gather_send(*range(6, 2 + NH))
    f_out[...] = (nx2 - row2) * (EPS * LN2) - EPS * jnp.log(r)
    col_step(smass / r)
    cs = jnp.sum(col_exchange(2, vec[5], during_col2), axis=0)
    kvec[0] = tlm2 - jnp.log(cs) * LOG2E - col2
    for kind in range(2):
        remote(kvec.at[0], kvec.at[1 + kind], ks_sem.at[kind], kr_sem.at[kind], mates[kind])
    gather_spread(*range(6, 2 + NH))
    g_out[...] = (ny2 - col2) * (EPS * LN2) - EPS * jnp.log(cs)

    v = tmass / cs
    for a in range(BLK):
        acc = None
        for k in range(BLK):
            q = (score[a, :, lanes(k)] * v[k:k + 1, :]).astype(jnp.bfloat16)
            weights[pl.ds(a * LANES, LANES), lanes(k)] = q
            q = q.astype(jnp.float32)
            acc = q if acc is None else acc + q
        tmp4[a // 2, pl.ds(a % 2, 1), :] = jnp.sum(acc.T, axis=0, keepdims=True)

    def project(ch):
        p = jnp.dot(weights[...], teach[:, ch * LANES:(ch + 2) * LANES], preferred_element_type=jnp.float32)
        part[ch] = p[:, :LANES].reshape(NX, NZ, ROWS, LANES)
        part[ch + 1] = p[:, LANES:].reshape(NX, NZ, ROWS, LANES)

    lo, hi = pl.ds(0, 4), pl.ds(4, 4)
    xr, xl = at_tgt(1, 0), at_tgt(-1, 0)
    zr, zl = at_tgt(0, 1), at_tgt(0, -1)

    def a_start(i, ch):
        remote(part.at[ch, xi[2], lo], xfar.at[i, 0], as_sem.at[i], ar_sem.at[i, 0], xr)
        remote(part.at[ch, xi[2], hi], xfar.at[i, 1], as_sem.at[i], ar_sem.at[i, 1], xl)

    def a_own(i, ch):
        remote(part.at[ch, xi[1], hi], xnear.at[i, 0, hi], as_sem.at[i], ar_sem.at[i, 2], xr)
        remote(part.at[ch, xi[3], lo], xnear.at[i, 1, lo], as_sem.at[i], ar_sem.at[i, 3], xl)

    def a_pass(i, ch, way):
        dev, dst, half = ((xr, xi[1], lo), (xl, xi[3], hi))[way]
        arrive(xfar.at[i, way], ar_sem.at[i, way])
        part[ch, dst, half] = part[ch, dst, half] + xfar[i, way]
        remote(part.at[ch, dst, half], xnear.at[i, way, half], as_sem.at[i], ar_sem.at[i, 2 + way], dev)

    def a_mid(i, ch):
        arrive(xnear.at[i, 0], ar_sem.at[i, 2])
        arrive(xnear.at[i, 1], ar_sem.at[i, 3])
        asum[i] = part[ch, x] + xnear[i, 0] + xnear[i, 1]
        z_start(i, ch)

    def a_ring(i, ch, step, way):
        dev, dst = ((zr, zi[4 - step]), (zl, zi[4 + step]))[way]
        if step == 1:
            arrive(zfar.at[i, way], zr_sem.at[i, way, 0])
            half = pl.ds(16 * way, 16)
            asum[i, dst, half] = asum[i, dst, half] + zfar[i, way]
        else:
            arrive(znear.at[i, way, step - 2], zr_sem.at[i, way, step - 1])
            asum[i, dst] = asum[i, dst] + znear[i, way, step - 2]
        remote(asum.at[i, dst], znear.at[i, way, step - 1], zs_sem.at[i], zr_sem.at[i, way, step], dev)

    def finish(ch, value):
        scale = rcol[lax.div(z, 4), pl.ds(lax.rem(z, 4) * ROWS, ROWS), :]
        out[:, lanes(ch)] = (value * scale).astype(jnp.bfloat16)

    def a_end(i, ch):
        arrive(znear.at[i, 0, 2], zr_sem.at[i, 0, 3])
        arrive(znear.at[i, 1, 2], zr_sem.at[i, 1, 3])
        finish(ch, asum[i, z] + znear[i, 0, 2] + znear[i, 1, 2])

    ends = (pl.ds(0, 2), pl.ds(2, 2))

    def b_start(i, ch):
        for way, dev in ((0, zr), (1, zl)):
            remote(part.at[ch, ends[way], zi[4]], bfar.at[i, way], bs_sem.at[i], br_sem.at[i, way, 0], dev)

    def b_own(i, ch):
        for way, dev, near in ((0, zr, zi[3]), (1, zl, zi[5])):
            own = 1 - way
            remote(part.at[ch, ends[own], near], bnear.at[i, way, 0, ends[own]], bs_sem.at[i], br_sem.at[i, way, 1], dev)

    def b_ring(i, ch, step, way):
        dev, dst = ((zr, zi[4 - step]), (zl, zi[4 + step]))[way]
        if step == 1:
            arrive(bfar.at[i, way], br_sem.at[i, way, 0])
            part[ch, ends[way], dst] = part[ch, ends[way], dst] + bfar[i, way]
            remote(part.at[ch, ends[way], dst], bnear.at[i, way, 0, ends[way]], bs_sem.at[i], br_sem.at[i, way, 1], dev)
        else:
            arrive(bnear.at[i, way, step - 2], br_sem.at[i, way, step - 1])
            part[ch, :, dst] = part[ch, :, dst] + bnear[i, way, step - 2]
            remote(part.at[ch, :, dst], bnear.at[i, way, step - 1], bs_sem.at[i], br_sem.at[i, way, step], dev)

    def b_mid(i, ch):
        arrive(bnear.at[i, 0, 2], br_sem.at[i, 0, 3])
        arrive(bnear.at[i, 1, 2], br_sem.at[i, 1, 3])
        bsum[i] = part[ch, :, z] + bnear[i, 0, 2] + bnear[i, 1, 2]
        for d in (2, 1, 3):
            remote(bsum.at[i, xi[d]], bx.at[i, d - 1], bxs_sem.at[i], bxr_sem.at[i], at_tgt(d, 0))

    def b_end(i, ch):
        arrive(bx.at[i], bxr_sem.at[i])
        finish(ch, bsum[i, x] + bx[i, 0] + bx[i, 1] + bx[i, 2])

    def h_start(n, ch):
        kind = n % 2
        for part_at, xb in enumerate((x, mate_x[1 - kind])):
            p = jnp.dot(weights[pl.ds(xb * 256, 256), :], teach[:, lanes(ch)], preferred_element_type=jnp.float32)
            p = p + jnp.dot(pweights[kind, pl.ds(part_at * 256, 256), :], pteach[n], preferred_element_type=jnp.float32)
            if part_at == 0:
                asum[NA + n] = p.reshape(NZ, ROWS, LANES)
            else:
                hsend[n] = p.reshape(NZ, ROWS, LANES)
        remote(hsend.at[n], hrecv.at[n], hs_sem.at[n], hr_sem.at[n], mates[1 - kind])

    def z_start(i, ch):
        if ch in DIRECT:
            for d in (4, 3, 5, 2, 6, 1, 7):
                remote(asum.at[i, zi[d]], zall.at[DIRECT.index(ch), d - 1], zs_sem.at[i], zr_sem.at[i, 0, 0], at_tgt(0, d))
        else:
            remote(asum.at[i, zi[4], pl.ds(0, 16)], zfar.at[i, 0], zs_sem.at[i], zr_sem.at[i, 0, 0], zr)
            remote(asum.at[i, zi[4], pl.ds(16, 16)], zfar.at[i, 1], zs_sem.at[i], zr_sem.at[i, 1, 0], zl)

    def a_direct(i, ch):
        n = DIRECT.index(ch)
        arrive(zall.at[n], zr_sem.at[i, 0, 0])
        total = asum[i, z]
        for d in range(7):
            total = total + zall[n, d]
        finish(ch, total)

    def h_mid(n, ch):
        arrive(hrecv.at[n], hr_sem.at[n])
        asum[NA + n] = asum[NA + n] + hrecv[n]
        z_start(NA + n, ch)

    def q_start():
        for d in (2, 1, 3):
            remote(tmp4.at[xi[d]], qbuf.at[d - 1], qs_sem.at[0], qr_sem.at[0], at_tgt(d, 0))

    def q_mid():
        arrive(qbuf.at[pl.ds(0, 3)], qr_sem.at[0])
        tmp4[x] = tmp4[x] + qbuf[0] + qbuf[1] + qbuf[2]
        for d in (4, 3, 5, 2, 6, 1, 7):
            remote(tmp4.at[x], qbuf.at[2 + d], qs_sem.at[1], qr_sem.at[1], at_tgt(0, d))

    def q_end():
        arrive(qbuf.at[pl.ds(3, 7)], qr_sem.at[1])
        total = tmp4[x]
        for d in range(7):
            total = total + qbuf[3 + d]
        rcol[0] = col_form(1.0 / total[0:1, :])
        rcol[1] = col_form(1.0 / total[1:2, :])

    steps = dict(ad=a_direct, hm=h_mid, ap=a_pass, am=a_mid, ar=a_ring, ae=a_end, br=b_ring, bm=b_mid, be=b_end)
    ready = set()
    q_start()
    for name, ch, *rest in SCHEDULE:
        if name == "qm":
            q_mid()
        elif name == "qe":
            q_end()
        elif name == "hw":
            mate_weights()
        elif name == "hf":
            gather_share(6 + 2 * ch, 7 + 2 * ch)
        elif name == "ht":
            take(4 + 2 * ch)
            take(5 + 2 * ch)
        elif name == "ao":
            a_own(KINDS[:ch].count("A"), ch)
        elif name == "bo":
            b_own(KINDS[:ch].count("B"), ch)
        elif name == "s" and KINDS[ch] == "H":
            h_start(KINDS[:ch].count("H"), ch)
        elif name == "s":
            if ch // 2 not in ready:
                ready.add(ch // 2)
                project(ch // 2 * 2)
            (a_start if KINDS[ch] == "A" else b_start)(KINDS[:ch].count(KINDS[ch]), ch)
        elif KINDS[ch] == "H" and name in ("ar", "ae", "ad"):
            steps[name](NA + KINDS[:ch].count("H"), ch, *rest)
        else:
            steps[name](KINDS[:ch].count(KINDS[ch]), ch, *rest)

    for e in range(3):
        arrive(rbuf.at[e, pl.ds(0, 31)], rs_sem.at[e])
        arrive(cbuf.at[e, pl.ds(0, 7)], cs_sem.at[e])
    arrive(qbuf.at[pl.ds(0, 3)], qs_sem.at[0])
    arrive(qbuf.at[pl.ds(3, 7)], qs_sem.at[1])
    for i, ch in enumerate(chunks_of("A")):
        arrive(part.at[ch, pl.ds(0, 3)], as_sem.at[i])
    for i in range(NA + NH):
        arrive(asum.at[i, pl.ds(0, 7)], zs_sem.at[i])
    for n in range(NH):
        arrive(hsend.at[n], hs_sem.at[n])
    for u in range(2 + NH):
        if shared(u):
            arrive(stage.at[u, 0], gs_sem.at[u])
            arrive(gath.at[u, 0, pl.ds(0, 3)], ys_sem.at[u])
        else:
            arrive(stage.at[u], gs_sem.at[u])
        arrive(stage.at[u], ds_sem.at[u])
    for kind in range(2):
        arrive(kvec.at[0], ks_sem.at[kind])
    for i, ch in enumerate(chunks_of("B")):
        arrive(part.at[ch, :, pl.ds(0, 7)], bs_sem.at[i])
        arrive(bx.at[i], bxs_sem.at[i])


def settle(*refs):
    sem = refs[-1]
    copies = [pltpu.make_async_copy(refs[n], refs[3 + n], sem.at[n]) for n in range(3)]
    for copy in copies:
        copy.start()
    for copy in copies:
        copy.wait()


def body(source_features, target_features, source_logmass, target_logmass, teacher_rows):
    na, nb, nz = NA, KINDS.count("B"), NA + NH
    f32 = jnp.float32
    vmem = pl.BlockSpec(memory_space=pltpu.VMEM)
    dma = pltpu.SemaphoreType.DMA
    projected, f, g = pl.pallas_call(
        functools.partial(kernel, source_features.shape[1]),
        out_shape=(
            jax.ShapeDtypeStruct((ROWS, CHUNKS * LANES), jnp.bfloat16),
            jax.ShapeDtypeStruct((BLK, LANES), f32),
            jax.ShapeDtypeStruct((BLK, LANES), f32),
        ),
        in_specs=[pl.BlockSpec(memory_space=pltpu.HBM)] * 5,
        out_specs=(vmem, vmem, vmem),
        scratch_shapes=[
            pltpu.VMEM(source_features.shape, source_features.dtype),
            pltpu.VMEM(target_features.shape, target_features.dtype),
            pltpu.VMEM((BLK, LANES), f32),
            pltpu.VMEM((BLK, LANES), f32),
            pltpu.VMEM((BLK, LANES, TILE), f32),
            pltpu.VMEM((BLK, LANES, LANES), f32),
            pltpu.VMEM((TILE, TILE), jnp.bfloat16),
            pltpu.VMEM((TILE, CHUNKS * LANES), jnp.bfloat16),
            pltpu.VMEM((CHUNKS, NX, NZ, ROWS, LANES), f32),
            pltpu.VMEM((3, 32, BLK, LANES), f32),
            pltpu.VMEM((3, 8, BLK, LANES), f32),
            pltpu.VMEM((7, BLK, LANES), f32),
            pltpu.VMEM((NX, 2, LANES), f32),
            pltpu.VMEM((10, 2, LANES), f32),
            pltpu.VMEM((na, 2, 4, ROWS, LANES), f32),
            pltpu.VMEM((na, 2, NZ, ROWS, LANES), f32),
            pltpu.VMEM((nz, NZ, ROWS, LANES), f32),
            pltpu.VMEM((nz, 2, ROWS // 2, LANES), f32),
            pltpu.VMEM((nz, 2, 3, ROWS, LANES), f32),
            pltpu.VMEM((nb, 2, 2, ROWS, LANES), f32),
            pltpu.VMEM((nb, 2, 3, NX, ROWS, LANES), f32),
            pltpu.VMEM((nb, NX, ROWS, LANES), f32),
            pltpu.VMEM((nb, 3, ROWS, LANES), f32),
            pltpu.VMEM((2, LANES, LANES), f32),
            dma, dma((4,)), dma((3,)), dma((3,)), dma((3,)), dma((3,)), dma((2,)), dma((2,)),
            dma((na,)), dma((na, 4)), dma((nz,)), dma((nz, 2, 4)),
            dma((nb,)), dma((nb, 2, 4)), dma((nb,)), dma((nb,)),
            pltpu.VMEM((max(1, len(DIRECT)), 7, ROWS, LANES), f32),
            pltpu.VMEM((2 + NH, 4, LANES, LANES), f32),
            pltpu.VMEM((2 + NH, 2, 4, LANES, LANES), f32),
            pltpu.VMEM((2, HALF, TILE), f32),
            pltpu.VMEM((2, HALF, TILE), jnp.bfloat16),
            pltpu.VMEM((NH, TILE, LANES), jnp.bfloat16),
            pltpu.VMEM((3, BLK, LANES), f32),
            pltpu.VMEM((NH, NZ, ROWS, LANES), f32),
            pltpu.VMEM((NH, NZ, ROWS, LANES), f32),
            dma((2 + NH,)), dma((2 + NH,)), dma((2 + NH,)), dma((2 + NH,)), dma((2 + NH,)), dma((2 + NH,)), dma((2,)), dma((2,)), dma((NH,)), dma((NH,)),
        ],
        compiler_params=pltpu.CompilerParams(
            collective_id=0, has_side_effects=True, vmem_limit_bytes=(64 * 1024 - 192) * 1024),
    )(source_features, target_features, source_logmass.reshape(BLK, LANES),
      target_logmass.reshape(BLK, LANES), teacher_rows)
    return pl.pallas_call(
        settle,
        out_shape=(
            jax.ShapeDtypeStruct(projected.shape, jnp.bfloat16),
            jax.ShapeDtypeStruct((TILE,), f32),
            jax.ShapeDtypeStruct((TILE,), f32),
        ),
        in_specs=[vmem] * 3,
        out_specs=(pl.BlockSpec(memory_space=pl.ANY),) * 3,
        scratch_shapes=[dma((3,))],
    )(projected, f.reshape(TILE), g.reshape(TILE))


def solution(mesh):
    in_specs = (P("src", None), P("tgt", None), P("src"), P("tgt"), P("tgt", None))
    out_specs = (P(("src", "tgt"), None), P("src"), P("tgt"))
    return jax.shard_map(body, mesh=mesh, in_specs=in_specs, out_specs=out_specs, check_vma=False)
```

```python
import functools
import math

import jax
import jax.numpy as jnp
from jax import lax
from jax.experimental import pallas as pl
from jax.experimental.pallas import tpu as pltpu
from jax.sharding import PartitionSpec as P

MESH = pl.DeviceIdType.MESH
EPS = 0.1
LOG2E = math.log2(math.e)
LN2 = math.log(2.0)
NX, NY, NZ = 4, 4, 8
LANES = 128
TILE = 1024
BLK = TILE // LANES
ROWS = 32
HALF = TILE // 2
NEAR = 4
CHUNKS = 12
KINDS = "ABBABAHHHHHH"
DIRECT = (2, 4, 5)
SCHEDULE = (
    ("s", 0), ("s", 1), ("s", 2), ("ao", 0), ("bo", 1), ("bo", 2), ("s", 3), ("qm", 0), ("s", 4), ("ao", 3),
    ("bo", 4), ("br", 1, 1, 0), ("br", 1, 1, 1), ("hw", 0), ("s", 6), ("br", 2, 1, 0), ("br", 2, 1, 1), ("ap", 0, 0),
    ("ap", 0, 1), ("hf", 0), ("br", 4, 1, 0), ("br", 4, 1, 1), ("s", 7), ("ap", 3, 0), ("ap", 3, 1), ("br", 1, 2, 0),
    ("br", 1, 2, 1), ("s", 8), ("br", 2, 2, 0), ("br", 2, 2, 1), ("br", 4, 2, 0), ("br", 4, 2, 1), ("s", 9),
    ("hm", 6), ("br", 1, 3, 0), ("br", 1, 3, 1), ("ht", 0), ("s", 10), ("hm", 7), ("br", 2, 3, 0), ("br", 2, 3, 1),
    ("am", 0), ("s", 11), ("am", 3), ("br", 4, 3, 0), ("br", 4, 3, 1), ("ar", 6, 1, 0), ("ar", 6, 1, 1), ("s", 5),
    ("ao", 5), ("bm", 1), ("ar", 7, 1, 0), ("hm", 9), ("hm", 8), ("ar", 7, 1, 1), ("bm", 2), ("ar", 0, 1, 0),
    ("ar", 0, 1, 1), ("ar", 3, 1, 0), ("ar", 3, 1, 1), ("hm", 11), ("bm", 4), ("hm", 10), ("ar", 6, 2, 0),
    ("ar", 6, 2, 1), ("ar", 9, 1, 0), ("ar", 9, 1, 1), ("ar", 8, 1, 0), ("ar", 8, 1, 1), ("ap", 5, 0), ("ap", 5, 1),
    ("ar", 7, 2, 0), ("ar", 7, 2, 1), ("ar", 0, 2, 0), ("ar", 0, 2, 1), ("ar", 3, 2, 0), ("ar", 3, 2, 1),
    ("ar", 11, 1, 0), ("ar", 11, 1, 1), ("ar", 10, 1, 0), ("ar", 10, 1, 1), ("ar", 6, 3, 0), ("qe", 0), ("be", 1),
    ("ar", 6, 3, 1), ("ar", 9, 2, 0), ("ar", 9, 2, 1), ("ar", 8, 2, 0), ("be", 2), ("ar", 8, 2, 1), ("ar", 7, 3, 0),
    ("ar", 7, 3, 1), ("ar", 0, 3, 0), ("be", 4), ("ar", 0, 3, 1), ("ar", 3, 3, 0), ("ar", 3, 3, 1), ("ar", 11, 2, 0),
    ("ar", 11, 2, 1), ("ar", 10, 2, 0), ("ar", 10, 2, 1), ("am", 5), ("ae", 6), ("ar", 9, 3, 0), ("ar", 9, 3, 1),
    ("ar", 8, 3, 0), ("ar", 8, 3, 1), ("ae", 7), ("ae", 0), ("ae", 3), ("ar", 11, 3, 0), ("ar", 11, 3, 1),
    ("ar", 10, 3, 0), ("ar", 10, 3, 1), ("ad", 5), ("ae", 9), ("ae", 8), ("ae", 11), ("ae", 10),
)
NA, NH = KINDS.count("A"), KINDS.count("H")


def chunks_of(kind):
    return [ch for ch in range(CHUNKS) if KINDS[ch] == kind]


def kernel(feat, xs_hbm, ys_hbm, slm_hbm, tlm_hbm, rows_hbm, out, f_out, g_out,
           xs, ys, slm, tlm, score, hcol, weights, teach, part, rbuf, cbuf, vec, tmp4, qbuf,
           xfar, xnear, asum, zfar, znear, bfar, bnear, bsum, bx, rcol,
           load_sem, in_sem, rs_sem, rr_sem, cs_sem, cr_sem, qs_sem, qr_sem,
           as_sem, ar_sem, zs_sem, zr_sem, bs_sem, br_sem, bxs_sem, bxr_sem,
           zall, stage, gath, pscore, pweights, pteach, kvec, hsend, hrecv,
           gs_sem, gr_sem, ds_sem, dr_sem, ys_sem, yr_sem, ks_sem, kr_sem, hs_sem, hr_sem):
    src = lax.axis_index("src")
    tgt = lax.axis_index("tgt")
    y, c = lax.div(src, 2), lax.rem(src, 2)
    x, z = lax.div(tgt, NZ), lax.rem(tgt, NZ)
    xi = [lax.rem(x + d, NX) for d in range(NX)]
    zi = [lax.rem(z + d, NZ) for d in range(NZ)]

    def at_tgt(dx, dz):
        return (src, xi[dx % NX] * NZ + zi[dz % NZ])

    def at_src(dy, dc):
        return (lax.rem(y + dy, NY) * 2 + lax.rem(c + dc, 2), tgt)

    def hops(d, n):
        return min(d, n - d)

    tgt_peers = sorted([(dx, dz) for dx in range(NX) for dz in range(NZ) if dx or dz],
                       key=lambda o: -hops(o[0], NX) - hops(o[1], NZ))
    src_peers = sorted([(dy, dc) for dy in range(NY) for dc in range(2) if dy or dc],
                       key=lambda o: -hops(o[0], NY) - 0.1 * o[1])

    loads = [pltpu.make_async_copy(a, b, in_sem.at[n]) for n, (a, b) in enumerate(
        ((ys_hbm, ys), (xs_hbm, xs), (slm_hbm, slm), (tlm_hbm, tlm)))]
    for copy in loads:
        copy.start()
    load = pltpu.make_async_copy(rows_hbm, teach, load_sem)
    load.start()
    barrier = pltpu.get_barrier_semaphore()
    for o in tgt_peers:
        pl.semaphore_signal(barrier, inc=1, device_id=at_tgt(*o), device_id_type=MESH)
    for o in src_peers:
        pl.semaphore_signal(barrier, inc=1, device_id=at_src(*o), device_id_type=MESH)

    def remote(a, b, ssem, rsem, dev):
        pltpu.make_async_remote_copy(src_ref=a, dst_ref=b, send_sem=ssem, recv_sem=rsem,
                                     device_id=dev, device_id_type=MESH).start()

    def arrive(ref, sem):
        pltpu.make_async_copy(ref, ref, sem).wait()

    def row_exchange(e, value, meanwhile=None):
        rbuf[e, tgt] = value
        for o in tgt_peers:
            remote(rbuf.at[e, tgt], rbuf.at[e, tgt], rs_sem.at[e], rr_sem.at[e], at_tgt(*o))
        if meanwhile is not None:
            meanwhile()
        arrive(rbuf.at[e, pl.ds(0, 31)], rr_sem.at[e])
        return rbuf[e]

    def col_exchange(e, value, meanwhile=None):
        cbuf[e, src] = value
        for o in src_peers:
            remote(cbuf.at[e, src], cbuf.at[e, src], cs_sem.at[e], cr_sem.at[e], at_src(*o))
        if meanwhile is not None:
            meanwhile()
        arrive(cbuf.at[e, pl.ds(0, 7)], cr_sem.at[e])
        return cbuf[e]

    def lse2(parts):
        peak = jnp.max(parts, axis=0)
        return peak + jnp.log(jnp.sum(jnp.exp2(parts - peak), axis=0)) * LOG2E

    def col_form(row):
        return jnp.broadcast_to(row, (LANES, LANES)).T

    side = 1 - 2 * lax.rem(x, 2)
    mate_x = [lax.rem(x + side + NX, NX), lax.rem(x - side + NX, NX)]
    mates = [(src, m * NZ + z) for m in mate_x]
    sibling = (y * 2 + 1 - c, tgt)
    mine = pl.ds(c * HALF, HALF)

    def shared(u):
        return u < 2 or u >= 2 + NEAR

    def gather_send(*units):
        for u in units:
            at = (u, y) if shared(u) else (u,)
            remote(stage.at[at], gath.at[(u, c) + at[1:]], gs_sem.at[u], gr_sem.at[u], mates[u % 2])

    def gather_spread(*units):
        for u in units:
            arrive(gath.at[u, 0, 0], gr_sem.at[u])
            for d in (2, 1, 3):
                remote(gath.at[u, c, y], gath.at[u, c, y], ys_sem.at[u], yr_sem.at[u], at_src(d, 0))

    def gather_share(*units):
        for u in units:
            if shared(u):
                arrive(gath.at[u, 0, pl.ds(0, 3)], yr_sem.at[u])
            else:
                arrive(gath.at[u, 0], gr_sem.at[u])
            remote(gath.at[u, c], gath.at[u, c], ds_sem.at[u], dr_sem.at[u], sibling)

    def gather_end(u):
        arrive(gath.at[u, 0], dr_sem.at[u])

    def lanes(k):
        return slice(k * LANES, (k + 1) * LANES)

    def fold(t):
        return t.reshape(LANES // 8, 8, LANES)

    for copy in loads:
        copy.wait()
    slm2 = slm[...] * LOG2E
    tlm2 = tlm[...] * LOG2E
    norm_scale = LOG2E / (feat * EPS)
    for a in range(BLK):
        xf = xs[pl.ds(a * LANES, LANES), :].astype(jnp.float32)
        yf = ys[pl.ds(a * LANES, LANES), :].astype(jnp.float32)
        vec[0, pl.ds(a, 1), :] = jnp.sum((xf * xf).T, axis=0, keepdims=True)
        vec[1, pl.ds(a, 1), :] = jnp.sum((yf * yf).T, axis=0, keepdims=True)
    nx2 = vec[0] * norm_scale
    ny2 = vec[1] * norm_scale
    bias = tlm2 - ny2

    for a in range(BLK):
        d = lax.dot_general(xs[pl.ds(a * LANES, LANES), :], ys[...], (((1,), (1,)), ((), ())),
                            preferred_element_type=jnp.float32)
        e = d * (2.0 * norm_scale)
        score[a] = e
        t = [e[:, lanes(k)] + bias[k:k + 1, :] for k in range(BLK)]
        m = functools.reduce(jnp.maximum, t)
        m = jnp.max(m, axis=1, keepdims=True)
        s = functools.reduce(jnp.add, [jnp.exp2(v - m) for v in t])
        s = jnp.sum(s, axis=1, keepdims=True)
        lse = m + jnp.log(s) * LOG2E
        vec[2, pl.ds(a, 1), :] = jnp.broadcast_to(lse, (LANES, LANES)).T[0:1, :]
    def fill_stage():
        stage[0] = ys[mine, :].astype(jnp.float32).reshape(4, LANES, LANES)
        stage[1] = stage[0]
        load.wait()
        for n, ch in enumerate(chunks_of("H")):
            stage[2 + n] = teach[mine, lanes(ch)].astype(jnp.float32).reshape(4, LANES, LANES)

    pl.semaphore_wait(barrier, len(tgt_peers) + len(src_peers))
    row2 = lse2(row_exchange(0, vec[2], fill_stage))
    vec[6] = row2
    gather_send(0, 1, 2, 3)

    h = slm2 - row2
    peaks = [jnp.full((8, LANES), -jnp.inf, jnp.float32)] * BLK
    for a in range(BLK):
        hc = col_form(h[a:a + 1, :])
        hcol[a] = hc
        for k in range(BLK):
            peaks[k] = jnp.maximum(peaks[k], jnp.max(fold(score[a, :, lanes(k)] + hc), axis=0))
    peaks = [jnp.max(p, axis=0, keepdims=True) for p in peaks]
    sums = [jnp.zeros((8, LANES), jnp.float32)] * BLK
    for a in range(BLK):
        hc = hcol[a]
        for k in range(BLK):
            sums[k] = sums[k] + jnp.sum(fold(jnp.exp2(score[a, :, lanes(k)] + hc - peaks[k])), axis=0)
    for k in range(BLK):
        total = jnp.sum(sums[k], axis=0, keepdims=True)
        vec[3, pl.ds(k, 1), :] = peaks[k] + jnp.log(total) * LOG2E
    col2 = lse2(col_exchange(0, vec[3]))
    kvec[3] = col2
    for kind in range(2):
        remote(kvec.at[3], kvec.at[4 + kind], ks_sem.at[2 + kind], kr_sem.at[2 + kind], mates[kind])
    gather_spread(0, 1)

    tmass = jnp.exp(tlm[...])
    smass = jnp.exp(slm[...])
    for a in range(BLK):
        lc = col_form(row2[a:a + 1, :])
        acc = None
        for k in range(BLK):
            q = jnp.exp2(score[a, :, lanes(k)] - lc - col2[k:k + 1, :])
            score[a, :, lanes(k)] = q
            q = q * tmass[k:k + 1, :]
            acc = q if acc is None else acc + q
        vec[4, pl.ds(a, 1), :] = jnp.sum(acc.T, axis=0, keepdims=True)

    def row_step(v):
        for a in range(BLK):
            acc = None
            for k in range(BLK):
                q = score[a, :, lanes(k)] * v[k:k + 1, :]
                acc = q if acc is None else acc + q
            vec[4, pl.ds(a, 1), :] = jnp.sum(acc.T, axis=0, keepdims=True)

    def col_step(u):
        acc = [jnp.zeros((8, LANES), jnp.float32)] * BLK
        for a in range(BLK):
            uc = col_form(u[a:a + 1, :])
            for k in range(BLK):
                acc[k] = acc[k] + jnp.sum(fold(score[a, :, lanes(k)] * uc), axis=0)
        for k in range(BLK):
            vec[5, pl.ds(k, 1), :] = jnp.sum(acc[k], axis=0, keepdims=True)

    def mate_scores():
        for kind in range(2):
            gather_end(kind)
            feats = gath[kind].reshape(TILE, LANES).astype(jnp.bfloat16)
            for part_at, xb in enumerate((x, mate_x[1 - kind])):
                d = lax.dot_general(xs[pl.ds(xb * 256, 256), :], feats, (((1,), (1,)), ((), ())),
                                    preferred_element_type=jnp.float32)
                pscore[kind, pl.ds(part_at * 256, 256), :] = d * (2.0 * norm_scale)
            arrive(kvec.at[4 + kind], kr_sem.at[2 + kind])
            for b in range(4):
                xb = (x, mate_x[1 - kind])[b // 2]
                lc = col_form(vec[6, pl.ds(2 * xb + b % 2, 1), :])
                for k in range(BLK):
                    at = (kind, pl.ds(b * LANES, LANES), lanes(k))
                    pscore[at] = jnp.exp2(pscore[at] - lc - kvec[4 + kind, k:k + 1, :])

    def take(n):
        gather_end(2 + n)
        pteach[n] = gath[2 + n].reshape(TILE, LANES).astype(jnp.bfloat16)

    def mate_weights():
        for kind in range(2):
            arrive(kvec.at[1 + kind], kr_sem.at[kind])
            for b in range(4):
                for k in range(BLK):
                    w = pscore[kind, pl.ds(b * LANES, LANES), lanes(k)] * kvec[1 + kind, k:k + 1, :]
                    pweights[kind, pl.ds(b * LANES, LANES), lanes(k)] = w.astype(jnp.bfloat16)

    def during_col1():
        take(0)
        take(1)
        gather_share(0, 1)

    def during_row2():
        mate_scores()
        gather_share(4, 5)

    def during_col2():
        take(2)
        take(3)

    r = jnp.sum(row_exchange(1, vec[4], lambda: gather_share(2, 3)), axis=0)
    gather_send(4, 5)
    col_step(smass / r)
    cs = jnp.sum(col_exchange(1, vec[5], during_col1), axis=0)
    row_step(tmass / cs)
    r = jnp.sum(row_exchange(2, vec[4], during_row2), axis=0)
    gather_send(*range(6, 2 + NH))
    f_out[...] = (nx2 - row2) * (EPS * LN2) - EPS * jnp.log(r)
    col_step(smass / r)
    cs = jnp.sum(col_exchange(2, vec[5], during_col2), axis=0)
    kvec[0] = tmass / cs
    for kind in range(2):
        remote(kvec.at[0], kvec.at[1 + kind], ks_sem.at[kind], kr_sem.at[kind], mates[kind])
    gather_spread(*range(6, 2 + NH))
    g_out[...] = (ny2 - col2) * (EPS * LN2) - EPS * jnp.log(cs)

    v = tmass / cs
    for a in range(BLK):
        acc = None
        for k in range(BLK):
            q = (score[a, :, lanes(k)] * v[k:k + 1, :]).astype(jnp.bfloat16)
            weights[pl.ds(a * LANES, LANES), lanes(k)] = q
            q = q.astype(jnp.float32)
            acc = q if acc is None else acc + q
        tmp4[a // 2, pl.ds(a % 2, 1), :] = jnp.sum(acc.T, axis=0, keepdims=True)

    def project(ch):
        p = jnp.dot(weights[...], teach[:, ch * LANES:(ch + 2) * LANES], preferred_element_type=jnp.float32)
        part[ch] = p[:, :LANES].reshape(NX, NZ, ROWS, LANES)
        part[ch + 1] = p[:, LANES:].reshape(NX, NZ, ROWS, LANES)

    lo, hi = pl.ds(0, 4), pl.ds(4, 4)
    xr, xl = at_tgt(1, 0), at_tgt(-1, 0)
    zr, zl = at_tgt(0, 1), at_tgt(0, -1)

    def a_start(i, ch):
        remote(part.at[ch, xi[2], lo], xfar.at[i, 0], as_sem.at[i], ar_sem.at[i, 0], xr)
        remote(part.at[ch, xi[2], hi], xfar.at[i, 1], as_sem.at[i], ar_sem.at[i, 1], xl)

    def a_own(i, ch):
        remote(part.at[ch, xi[1], hi], xnear.at[i, 0, hi], as_sem.at[i], ar_sem.at[i, 2], xr)
        remote(part.at[ch, xi[3], lo], xnear.at[i, 1, lo], as_sem.at[i], ar_sem.at[i, 3], xl)

    def a_pass(i, ch, way):
        dev, dst, half = ((xr, xi[1], lo), (xl, xi[3], hi))[way]
        arrive(xfar.at[i, way], ar_sem.at[i, way])
        part[ch, dst, half] = part[ch, dst, half] + xfar[i, way]
        remote(part.at[ch, dst, half], xnear.at[i, way, half], as_sem.at[i], ar_sem.at[i, 2 + way], dev)

    def a_mid(i, ch):
        arrive(xnear.at[i, 0], ar_sem.at[i, 2])
        arrive(xnear.at[i, 1], ar_sem.at[i, 3])
        asum[i] = part[ch, x] + xnear[i, 0] + xnear[i, 1]
        z_start(i, ch)

    def a_ring(i, ch, step, way):
        dev, dst = ((zr, zi[4 - step]), (zl, zi[4 + step]))[way]
        if step == 1:
            arrive(zfar.at[i, way], zr_sem.at[i, way, 0])
            half = pl.ds(16 * way, 16)
            asum[i, dst, half] = asum[i, dst, half] + zfar[i, way]
        else:
            arrive(znear.at[i, way, step - 2], zr_sem.at[i, way, step - 1])
            asum[i, dst] = asum[i, dst] + znear[i, way, step - 2]
        remote(asum.at[i, dst], znear.at[i, way, step - 1], zs_sem.at[i], zr_sem.at[i, way, step], dev)

    def finish(ch, value):
        scale = rcol[lax.div(z, 4), pl.ds(lax.rem(z, 4) * ROWS, ROWS), :]
        out[:, lanes(ch)] = (value * scale).astype(jnp.bfloat16)

    def a_end(i, ch):
        arrive(znear.at[i, 0, 2], zr_sem.at[i, 0, 3])
        arrive(znear.at[i, 1, 2], zr_sem.at[i, 1, 3])
        finish(ch, asum[i, z] + znear[i, 0, 2] + znear[i, 1, 2])

    ends = (pl.ds(0, 2), pl.ds(2, 2))

    def b_start(i, ch):
        for way, dev in ((0, zr), (1, zl)):
            remote(part.at[ch, ends[way], zi[4]], bfar.at[i, way], bs_sem.at[i], br_sem.at[i, way, 0], dev)

    def b_own(i, ch):
        for way, dev, near in ((0, zr, zi[3]), (1, zl, zi[5])):
            own = 1 - way
            remote(part.at[ch, ends[own], near], bnear.at[i, way, 0, ends[own]], bs_sem.at[i], br_sem.at[i, way, 1], dev)

    def b_ring(i, ch, step, way):
        dev, dst = ((zr, zi[4 - step]), (zl, zi[4 + step]))[way]
        if step == 1:
            arrive(bfar.at[i, way], br_sem.at[i, way, 0])
            part[ch, ends[way], dst] = part[ch, ends[way], dst] + bfar[i, way]
            remote(part.at[ch, ends[way], dst], bnear.at[i, way, 0, ends[way]], bs_sem.at[i], br_sem.at[i, way, 1], dev)
        else:
            arrive(bnear.at[i, way, step - 2], br_sem.at[i, way, step - 1])
            part[ch, :, dst] = part[ch, :, dst] + bnear[i, way, step - 2]
            remote(part.at[ch, :, dst], bnear.at[i, way, step - 1], bs_sem.at[i], br_sem.at[i, way, step], dev)

    def b_mid(i, ch):
        arrive(bnear.at[i, 0, 2], br_sem.at[i, 0, 3])
        arrive(bnear.at[i, 1, 2], br_sem.at[i, 1, 3])
        bsum[i] = part[ch, :, z] + bnear[i, 0, 2] + bnear[i, 1, 2]
        for d in (2, 1, 3):
            remote(bsum.at[i, xi[d]], bx.at[i, d - 1], bxs_sem.at[i], bxr_sem.at[i], at_tgt(d, 0))

    def b_end(i, ch):
        arrive(bx.at[i], bxr_sem.at[i])
        finish(ch, bsum[i, x] + bx[i, 0] + bx[i, 1] + bx[i, 2])

    def h_start(n, ch):
        kind = n % 2
        for part_at, xb in enumerate((x, mate_x[1 - kind])):
            p = jnp.dot(weights[pl.ds(xb * 256, 256), :], teach[:, lanes(ch)], preferred_element_type=jnp.float32)
            p = p + jnp.dot(pweights[kind, pl.ds(part_at * 256, 256), :], pteach[n], preferred_element_type=jnp.float32)
            if part_at == 0:
                asum[NA + n] = p.reshape(NZ, ROWS, LANES)
            else:
                hsend[n] = p.reshape(NZ, ROWS, LANES)
        remote(hsend.at[n], hrecv.at[n], hs_sem.at[n], hr_sem.at[n], mates[1 - kind])

    def z_start(i, ch):
        if ch in DIRECT:
            for d in (4, 3, 5, 2, 6, 1, 7):
                remote(asum.at[i, zi[d]], zall.at[DIRECT.index(ch), d - 1], zs_sem.at[i], zr_sem.at[i, 0, 0], at_tgt(0, d))
        else:
            remote(asum.at[i, zi[4], pl.ds(0, 16)], zfar.at[i, 0], zs_sem.at[i], zr_sem.at[i, 0, 0], zr)
            remote(asum.at[i, zi[4], pl.ds(16, 16)], zfar.at[i, 1], zs_sem.at[i], zr_sem.at[i, 1, 0], zl)

    def a_direct(i, ch):
        n = DIRECT.index(ch)
        arrive(zall.at[n], zr_sem.at[i, 0, 0])
        total = asum[i, z]
        for d in range(7):
            total = total + zall[n, d]
        finish(ch, total)

    def h_mid(n, ch):
        arrive(hrecv.at[n], hr_sem.at[n])
        asum[NA + n] = asum[NA + n] + hrecv[n]
        z_start(NA + n, ch)

    def q_start():
        for d in (2, 1, 3):
            remote(tmp4.at[xi[d]], qbuf.at[d - 1], qs_sem.at[0], qr_sem.at[0], at_tgt(d, 0))

    def q_mid():
        arrive(qbuf.at[pl.ds(0, 3)], qr_sem.at[0])
        tmp4[x] = tmp4[x] + qbuf[0] + qbuf[1] + qbuf[2]
        for d in (4, 3, 5, 2, 6, 1, 7):
            remote(tmp4.at[x], qbuf.at[2 + d], qs_sem.at[1], qr_sem.at[1], at_tgt(0, d))

    def q_end():
        arrive(qbuf.at[pl.ds(3, 7)], qr_sem.at[1])
        total = tmp4[x]
        for d in range(7):
            total = total + qbuf[3 + d]
        rcol[0] = col_form(1.0 / total[0:1, :])
        rcol[1] = col_form(1.0 / total[1:2, :])

    steps = dict(ad=a_direct, hm=h_mid, ap=a_pass, am=a_mid, ar=a_ring, ae=a_end, br=b_ring, bm=b_mid, be=b_end)
    ready = set()
    q_start()
    for name, ch, *rest in SCHEDULE:
        if name == "qm":
            q_mid()
        elif name == "qe":
            q_end()
        elif name == "hw":
            mate_weights()
        elif name == "hf":
            gather_share(6 + 2 * ch, 7 + 2 * ch)
        elif name == "ht":
            take(4 + 2 * ch)
            take(5 + 2 * ch)
        elif name == "ao":
            a_own(KINDS[:ch].count("A"), ch)
        elif name == "bo":
            b_own(KINDS[:ch].count("B"), ch)
        elif name == "s" and KINDS[ch] == "H":
            h_start(KINDS[:ch].count("H"), ch)
        elif name == "s":
            if ch // 2 not in ready:
                ready.add(ch // 2)
                project(ch // 2 * 2)
            (a_start if KINDS[ch] == "A" else b_start)(KINDS[:ch].count(KINDS[ch]), ch)
        elif KINDS[ch] == "H" and name in ("ar", "ae", "ad"):
            steps[name](NA + KINDS[:ch].count("H"), ch, *rest)
        else:
            steps[name](KINDS[:ch].count(KINDS[ch]), ch, *rest)

    for e in range(3):
        arrive(rbuf.at[e, pl.ds(0, 31)], rs_sem.at[e])
        arrive(cbuf.at[e, pl.ds(0, 7)], cs_sem.at[e])
    arrive(qbuf.at[pl.ds(0, 3)], qs_sem.at[0])
    arrive(qbuf.at[pl.ds(3, 7)], qs_sem.at[1])
    for i, ch in enumerate(chunks_of("A")):
        arrive(part.at[ch, pl.ds(0, 3)], as_sem.at[i])
    for i in range(NA + NH):
        arrive(asum.at[i, pl.ds(0, 7)], zs_sem.at[i])
    for n in range(NH):
        arrive(hsend.at[n], hs_sem.at[n])
    for u in range(2 + NH):
        if shared(u):
            arrive(stage.at[u, 0], gs_sem.at[u])
            arrive(gath.at[u, 0, pl.ds(0, 3)], ys_sem.at[u])
        else:
            arrive(stage.at[u], gs_sem.at[u])
        arrive(stage.at[u], ds_sem.at[u])
    for kind in range(4):
        arrive(kvec.at[0], ks_sem.at[kind])
    for i, ch in enumerate(chunks_of("B")):
        arrive(part.at[ch, :, pl.ds(0, 7)], bs_sem.at[i])
        arrive(bx.at[i], bxs_sem.at[i])


def settle(*refs):
    sem = refs[-1]
    copies = [pltpu.make_async_copy(refs[n], refs[3 + n], sem.at[n]) for n in range(3)]
    for copy in copies:
        copy.start()
    for copy in copies:
        copy.wait()


def body(source_features, target_features, source_logmass, target_logmass, teacher_rows):
    na, nb, nz = NA, KINDS.count("B"), NA + NH
    f32 = jnp.float32
    vmem = pl.BlockSpec(memory_space=pltpu.VMEM)
    dma = pltpu.SemaphoreType.DMA
    projected, f, g = pl.pallas_call(
        functools.partial(kernel, source_features.shape[1]),
        out_shape=(
            jax.ShapeDtypeStruct((ROWS, CHUNKS * LANES), jnp.bfloat16),
            jax.ShapeDtypeStruct((BLK, LANES), f32),
            jax.ShapeDtypeStruct((BLK, LANES), f32),
        ),
        in_specs=[pl.BlockSpec(memory_space=pltpu.HBM)] * 5,
        out_specs=(vmem, vmem, vmem),
        scratch_shapes=[
            pltpu.VMEM(source_features.shape, source_features.dtype),
            pltpu.VMEM(target_features.shape, target_features.dtype),
            pltpu.VMEM((BLK, LANES), f32),
            pltpu.VMEM((BLK, LANES), f32),
            pltpu.VMEM((BLK, LANES, TILE), f32),
            pltpu.VMEM((BLK, LANES, LANES), f32),
            pltpu.VMEM((TILE, TILE), jnp.bfloat16),
            pltpu.VMEM((TILE, CHUNKS * LANES), jnp.bfloat16),
            pltpu.VMEM((CHUNKS, NX, NZ, ROWS, LANES), f32),
            pltpu.VMEM((3, 32, BLK, LANES), f32),
            pltpu.VMEM((3, 8, BLK, LANES), f32),
            pltpu.VMEM((7, BLK, LANES), f32),
            pltpu.VMEM((NX, 2, LANES), f32),
            pltpu.VMEM((10, 2, LANES), f32),
            pltpu.VMEM((na, 2, 4, ROWS, LANES), f32),
            pltpu.VMEM((na, 2, NZ, ROWS, LANES), f32),
            pltpu.VMEM((nz, NZ, ROWS, LANES), f32),
            pltpu.VMEM((nz, 2, ROWS // 2, LANES), f32),
            pltpu.VMEM((nz, 2, 3, ROWS, LANES), f32),
            pltpu.VMEM((nb, 2, 2, ROWS, LANES), f32),
            pltpu.VMEM((nb, 2, 3, NX, ROWS, LANES), f32),
            pltpu.VMEM((nb, NX, ROWS, LANES), f32),
            pltpu.VMEM((nb, 3, ROWS, LANES), f32),
            pltpu.VMEM((2, LANES, LANES), f32),
            dma, dma((4,)), dma((3,)), dma((3,)), dma((3,)), dma((3,)), dma((2,)), dma((2,)),
            dma((na,)), dma((na, 4)), dma((nz,)), dma((nz, 2, 4)),
            dma((nb,)), dma((nb, 2, 4)), dma((nb,)), dma((nb,)),
            pltpu.VMEM((max(1, len(DIRECT)), 7, ROWS, LANES), f32),
            pltpu.VMEM((2 + NH, 4, LANES, LANES), f32),
            pltpu.VMEM((2 + NH, 2, 4, LANES, LANES), f32),
            pltpu.VMEM((2, HALF, TILE), f32),
            pltpu.VMEM((2, HALF, TILE), jnp.bfloat16),
            pltpu.VMEM((NH, TILE, LANES), jnp.bfloat16),
            pltpu.VMEM((6, BLK, LANES), f32),
            pltpu.VMEM((NH, NZ, ROWS, LANES), f32),
            pltpu.VMEM((NH, NZ, ROWS, LANES), f32),
            dma((2 + NH,)), dma((2 + NH,)), dma((2 + NH,)), dma((2 + NH,)), dma((2 + NH,)), dma((2 + NH,)), dma((4,)), dma((4,)), dma((NH,)), dma((NH,)),
        ],
        compiler_params=pltpu.CompilerParams(
            collective_id=0, has_side_effects=True, vmem_limit_bytes=(64 * 1024 - 192) * 1024),
    )(source_features, target_features, source_logmass.reshape(BLK, LANES),
      target_logmass.reshape(BLK, LANES), teacher_rows)
    return pl.pallas_call(
        settle,
        out_shape=(
            jax.ShapeDtypeStruct(projected.shape, jnp.bfloat16),
            jax.ShapeDtypeStruct((TILE,), f32),
            jax.ShapeDtypeStruct((TILE,), f32),
        ),
        in_specs=[vmem] * 3,
        out_specs=(pl.BlockSpec(memory_space=pl.ANY),) * 3,
        scratch_shapes=[dma((3,))],
    )(projected, f.reshape(TILE), g.reshape(TILE))


def solution(mesh):
    in_specs = (P("src", None), P("tgt", None), P("src"), P("tgt"), P("tgt", None))
    out_specs = (P(("src", "tgt"), None), P("src"), P("tgt"))
    return jax.shard_map(body, mesh=mesh, in_specs=in_specs, out_specs=out_specs, check_vma=False)
```

```python
import functools
import math

import jax
import jax.numpy as jnp
from jax import lax
from jax.experimental import pallas as pl
from jax.experimental.pallas import tpu as pltpu
from jax.sharding import PartitionSpec as P

MESH = pl.DeviceIdType.MESH
EPS = 0.1
LOG2E = math.log2(math.e)
LN2 = math.log(2.0)
NX, NY, NZ = 4, 4, 8
LANES = 128
TILE = 1024
BLK = TILE // LANES
ROWS = 32
HALF = TILE // 2
NEAR = 4
CHUNKS = 12
KINDS = "ABBABAHHHHHH"
DIRECT = (2, 4, 5)
SCHEDULE = (
    ("s", 0), ("s", 1), ("s", 2), ("ao", 0), ("bo", 1), ("bo", 2), ("s", 3), ("qm", 0), ("s", 4), ("ao", 3),
    ("bo", 4), ("br", 1, 1, 0), ("br", 1, 1, 1), ("hw", 0), ("s", 6), ("br", 2, 1, 0), ("br", 2, 1, 1), ("ap", 0, 0),
    ("ap", 0, 1), ("hf", 0), ("br", 4, 1, 0), ("br", 4, 1, 1), ("s", 7), ("ap", 3, 0), ("ap", 3, 1), ("br", 1, 2, 0),
    ("br", 1, 2, 1), ("s", 8), ("br", 2, 2, 0), ("br", 2, 2, 1), ("br", 4, 2, 0), ("br", 4, 2, 1), ("s", 9),
    ("hm", 6), ("br", 1, 3, 0), ("br", 1, 3, 1), ("ht", 0), ("s", 10), ("hm", 7), ("br", 2, 3, 0), ("br", 2, 3, 1),
    ("am", 0), ("s", 11), ("am", 3), ("br", 4, 3, 0), ("br", 4, 3, 1), ("ar", 6, 1, 0), ("ar", 6, 1, 1), ("s", 5),
    ("ao", 5), ("bm", 1), ("ar", 7, 1, 0), ("hm", 9), ("hm", 8), ("ar", 7, 1, 1), ("bm", 2), ("ar", 0, 1, 0),
    ("ar", 0, 1, 1), ("ar", 3, 1, 0), ("ar", 3, 1, 1), ("hm", 11), ("bm", 4), ("hm", 10), ("ar", 6, 2, 0),
    ("ar", 6, 2, 1), ("ar", 9, 1, 0), ("ar", 9, 1, 1), ("ar", 8, 1, 0), ("ar", 8, 1, 1), ("ap", 5, 0), ("ap", 5, 1),
    ("ar", 7, 2, 0), ("ar", 7, 2, 1), ("ar", 0, 2, 0), ("ar", 0, 2, 1), ("ar", 3, 2, 0), ("ar", 3, 2, 1),
    ("ar", 11, 1, 0), ("ar", 11, 1, 1), ("ar", 10, 1, 0), ("ar", 10, 1, 1), ("ar", 6, 3, 0), ("qe", 0), ("be", 1),
    ("ar", 6, 3, 1), ("ar", 9, 2, 0), ("ar", 9, 2, 1), ("ar", 8, 2, 0), ("be", 2), ("ar", 8, 2, 1), ("ar", 7, 3, 0),
    ("ar", 7, 3, 1), ("ar", 0, 3, 0), ("be", 4), ("ar", 0, 3, 1), ("ar", 3, 3, 0), ("ar", 3, 3, 1), ("ar", 11, 2, 0),
    ("ar", 11, 2, 1), ("ar", 10, 2, 0), ("ar", 10, 2, 1), ("am", 5), ("ae", 6), ("ar", 9, 3, 0), ("ar", 9, 3, 1),
    ("ar", 8, 3, 0), ("ar", 8, 3, 1), ("ae", 7), ("ae", 0), ("ae", 3), ("ar", 11, 3, 0), ("ar", 11, 3, 1),
    ("ar", 10, 3, 0), ("ar", 10, 3, 1), ("ad", 5), ("ae", 9), ("ae", 8), ("ae", 11), ("ae", 10),
)
NA, NH = KINDS.count("A"), KINDS.count("H")


def chunks_of(kind):
    return [ch for ch in range(CHUNKS) if KINDS[ch] == kind]


def kernel(feat, xs_hbm, ys_hbm, slm_hbm, tlm_hbm, rows_hbm, out, f_out, g_out,
           xs, ys, slm, tlm, score, hcol, weights, teach, part, rbuf, cbuf, vec, tmp4, qbuf,
           xfar, xnear, asum, zfar, znear, bfar, bnear, bsum, bx, rcol,
           load_sem, in_sem, rs_sem, rr_sem, cs_sem, cr_sem, qs_sem, qr_sem,
           as_sem, ar_sem, zs_sem, zr_sem, bs_sem, br_sem, bxs_sem, bxr_sem,
           zall, stage, gath, pscore, pweights, pteach, kvec, hsend, hrecv,
           gs_sem, gr_sem, ds_sem, dr_sem, ys_sem, yr_sem, ks_sem, kr_sem, hs_sem, hr_sem):
    src = lax.axis_index("src")
    tgt = lax.axis_index("tgt")
    y, c = lax.div(src, 2), lax.rem(src, 2)
    x, z = lax.div(tgt, NZ), lax.rem(tgt, NZ)
    xi = [lax.rem(x + d, NX) for d in range(NX)]
    zi = [lax.rem(z + d, NZ) for d in range(NZ)]

    def at_tgt(dx, dz):
        return (src, xi[dx % NX] * NZ + zi[dz % NZ])

    def at_src(dy, dc):
        return (lax.rem(y + dy, NY) * 2 + lax.rem(c + dc, 2), tgt)

    def hops(d, n):
        return min(d, n - d)

    tgt_peers = sorted([(dx, dz) for dx in range(NX) for dz in range(NZ) if dx or dz],
                       key=lambda o: -hops(o[0], NX) - hops(o[1], NZ))
    src_peers = sorted([(dy, dc) for dy in range(NY) for dc in range(2) if dy or dc],
                       key=lambda o: -hops(o[0], NY) - 0.1 * o[1])

    loads = [pltpu.make_async_copy(a, b, in_sem.at[n]) for n, (a, b) in enumerate(
        ((ys_hbm, ys), (xs_hbm, xs), (slm_hbm, slm), (tlm_hbm, tlm)))]
    for copy in loads:
        copy.start()
    load = pltpu.make_async_copy(rows_hbm, teach, load_sem)
    load.start()
    barrier = pltpu.get_barrier_semaphore()
    for o in tgt_peers:
        pl.semaphore_signal(barrier, inc=1, device_id=at_tgt(*o), device_id_type=MESH)
    for o in src_peers:
        pl.semaphore_signal(barrier, inc=1, device_id=at_src(*o), device_id_type=MESH)

    def remote(a, b, ssem, rsem, dev):
        pltpu.make_async_remote_copy(src_ref=a, dst_ref=b, send_sem=ssem, recv_sem=rsem,
                                     device_id=dev, device_id_type=MESH).start()

    def arrive(ref, sem):
        pltpu.make_async_copy(ref, ref, sem).wait()

    def row_exchange(e, value, meanwhile=None):
        rbuf[e, tgt] = value
        for o in tgt_peers:
            remote(rbuf.at[e, tgt], rbuf.at[e, tgt], rs_sem.at[e], rr_sem.at[e], at_tgt(*o))
        if meanwhile is not None:
            meanwhile()
        arrive(rbuf.at[e, pl.ds(0, 31)], rr_sem.at[e])
        return rbuf[e]

    def col_exchange(e, value, meanwhile=None):
        cbuf[e, src] = value
        for o in src_peers:
            remote(cbuf.at[e, src], cbuf.at[e, src], cs_sem.at[e], cr_sem.at[e], at_src(*o))
        if meanwhile is not None:
            meanwhile()
        arrive(cbuf.at[e, pl.ds(0, 7)], cr_sem.at[e])
        return cbuf[e]

    def lse2(parts):
        peak = jnp.max(parts, axis=0)
        return peak + jnp.log(jnp.sum(jnp.exp2(parts - peak), axis=0)) * LOG2E

    def col_form(row):
        return jnp.broadcast_to(row, (LANES, LANES)).T

    side = 1 - 2 * lax.rem(x, 2)
    mate_x = [lax.rem(x + side + NX, NX), lax.rem(x - side + NX, NX)]
    mates = [(src, m * NZ + z) for m in mate_x]
    sibling = (y * 2 + 1 - c, tgt)
    mine = pl.ds(c * HALF, HALF)

    def shared(u):
        return u < 2 or u >= 2 + NEAR

    def gather_send(*units):
        for u in units:
            at = (u, y) if shared(u) else (u,)
            remote(stage.at[at], gath.at[(u, c) + at[1:]], gs_sem.at[u], gr_sem.at[u], mates[u % 2])

    def gather_spread(*units):
        for u in units:
            arrive(gath.at[u, 0, 0], gr_sem.at[u])
            for d in (2, 1, 3):
                remote(gath.at[u, c, y], gath.at[u, c, y], ys_sem.at[u], yr_sem.at[u], at_src(d, 0))

    def gather_share(*units):
        for u in units:
            if shared(u):
                arrive(gath.at[u, 0, pl.ds(0, 3)], yr_sem.at[u])
            else:
                arrive(gath.at[u, 0], gr_sem.at[u])
            remote(gath.at[u, c], gath.at[u, c], ds_sem.at[u], dr_sem.at[u], sibling)

    def gather_end(u):
        arrive(gath.at[u, 0], dr_sem.at[u])

    def lanes(k):
        return slice(k * LANES, (k + 1) * LANES)

    def fold(t):
        return t.reshape(LANES // 8, 8, LANES)

    for copy in loads:
        copy.wait()
    slm2 = slm[...] * LOG2E
    tlm2 = tlm[...] * LOG2E
    norm_scale = LOG2E / (feat * EPS)
    for a in range(BLK):
        xf = xs[pl.ds(a * LANES, LANES), :].astype(jnp.float32)
        yf = ys[pl.ds(a * LANES, LANES), :].astype(jnp.float32)
        vec[0, pl.ds(a, 1), :] = jnp.sum((xf * xf).T, axis=0, keepdims=True)
        vec[1, pl.ds(a, 1), :] = jnp.sum((yf * yf).T, axis=0, keepdims=True)
    nx2 = vec[0] * norm_scale
    ny2 = vec[1] * norm_scale
    bias = tlm2 - ny2

    for a in range(BLK):
        d = lax.dot_general(xs[pl.ds(a * LANES, LANES), :], ys[...], (((1,), (1,)), ((), ())),
                            preferred_element_type=jnp.float32)
        e = d * (2.0 * norm_scale)
        score[a] = e
        t = [e[:, lanes(k)] + bias[k:k + 1, :] for k in range(BLK)]
        m = functools.reduce(jnp.maximum, t)
        m = jnp.max(m, axis=1, keepdims=True)
        s = functools.reduce(jnp.add, [jnp.exp2(v - m) for v in t])
        s = jnp.sum(s, axis=1, keepdims=True)
        lse = m + jnp.log(s) * LOG2E
        vec[2, pl.ds(a, 1), :] = jnp.broadcast_to(lse, (LANES, LANES)).T[0:1, :]
    def fill_stage():
        stage[0] = ys[mine, :].astype(jnp.float32).reshape(4, LANES, LANES)
        stage[1] = stage[0]
        load.wait()
        for n, ch in enumerate(chunks_of("H")):
            stage[2 + n] = teach[mine, lanes(ch)].astype(jnp.float32).reshape(4, LANES, LANES)

    pl.semaphore_wait(barrier, len(tgt_peers) + len(src_peers))
    row2 = lse2(row_exchange(0, vec[2], fill_stage))
    vec[6] = row2
    gather_send(0, 1, 2, 3)

    h = slm2 - row2
    peaks = [jnp.full((8, LANES), -jnp.inf, jnp.float32)] * BLK
    for a in range(BLK):
        hc = col_form(h[a:a + 1, :])
        hcol[a] = hc
        for k in range(BLK):
            peaks[k] = jnp.maximum(peaks[k], jnp.max(fold(score[a, :, lanes(k)] + hc), axis=0))
    peaks = [jnp.max(p, axis=0, keepdims=True) for p in peaks]
    sums = [jnp.zeros((8, LANES), jnp.float32)] * BLK
    for a in range(BLK):
        hc = hcol[a]
        for k in range(BLK):
            sums[k] = sums[k] + jnp.sum(fold(jnp.exp2(score[a, :, lanes(k)] + hc - peaks[k])), axis=0)
    for k in range(BLK):
        total = jnp.sum(sums[k], axis=0, keepdims=True)
        vec[3, pl.ds(k, 1), :] = peaks[k] + jnp.log(total) * LOG2E
    col2 = lse2(col_exchange(0, vec[3]))
    kvec[3] = col2
    for kind in range(2):
        remote(kvec.at[3], kvec.at[4 + kind], ks_sem.at[2 + kind], kr_sem.at[2 + kind], mates[kind])
    gather_spread(0, 1)

    tmass = jnp.exp(tlm[...])
    smass = jnp.exp(slm[...])
    for a in range(BLK):
        lc = col_form(row2[a:a + 1, :])
        acc = None
        for k in range(BLK):
            q = jnp.exp2(score[a, :, lanes(k)] - lc - col2[k:k + 1, :])
            score[a, :, lanes(k)] = q
            q = q * tmass[k:k + 1, :]
            acc = q if acc is None else acc + q
        vec[4, pl.ds(a, 1), :] = jnp.sum(acc.T, axis=0, keepdims=True)

    def row_step(v):
        for a in range(BLK):
            acc = None
            for k in range(BLK):
                q = score[a, :, lanes(k)] * v[k:k + 1, :]
                acc = q if acc is None else acc + q
            vec[4, pl.ds(a, 1), :] = jnp.sum(acc.T, axis=0, keepdims=True)

    def col_step(u):
        acc = [jnp.zeros((8, LANES), jnp.float32)] * BLK
        for a in range(BLK):
            uc = col_form(u[a:a + 1, :])
            for k in range(BLK):
                acc[k] = acc[k] + jnp.sum(fold(score[a, :, lanes(k)] * uc), axis=0)
        for k in range(BLK):
            vec[5, pl.ds(k, 1), :] = jnp.sum(acc[k], axis=0, keepdims=True)

    def mate_scores():
        for kind in range(2):
            gather_end(kind)
            feats = gath[kind].reshape(TILE, LANES).astype(jnp.bfloat16)
            for part_at, xb in enumerate((x, mate_x[1 - kind])):
                d = lax.dot_general(xs[pl.ds(xb * 256, 256), :], feats, (((1,), (1,)), ((), ())),
                                    preferred_element_type=jnp.float32)
                pscore[kind, pl.ds(part_at * 256, 256), :] = d * (2.0 * norm_scale)
            arrive(kvec.at[4 + kind], kr_sem.at[2 + kind])
            for b in range(4):
                xb = (x, mate_x[1 - kind])[b // 2]
                lc = col_form(vec[6, pl.ds(2 * xb + b % 2, 1), :])
                for k in range(BLK):
                    at = (kind, pl.ds(b * LANES, LANES), lanes(k))
                    pscore[at] = jnp.exp2(pscore[at] - lc - kvec[4 + kind, k:k + 1, :])

    def take(n):
        gather_end(2 + n)
        pteach[n] = gath[2 + n].reshape(TILE, LANES).astype(jnp.bfloat16)

    def mate_weights():
        for kind in range(2):
            arrive(kvec.at[1 + kind], kr_sem.at[kind])
            for b in range(4):
                for k in range(BLK):
                    w = pscore[kind, pl.ds(b * LANES, LANES), lanes(k)] * kvec[1 + kind, k:k + 1, :]
                    pweights[kind, pl.ds(b * LANES, LANES), lanes(k)] = w.astype(jnp.bfloat16)

    def during_col1():
        take(0)
        take(1)
        gather_share(0, 1)

    def during_row2():
        mate_scores()
        gather_share(4, 5)

    def during_col2():
        take(2)
        take(3)

    r = jnp.sum(row_exchange(1, vec[4], lambda: gather_share(2, 3)), axis=0)
    gather_send(4, 5)
    col_step(smass / r)
    cs = jnp.sum(col_exchange(1, vec[5], during_col1), axis=0)
    row_step(tmass / cs)
    r = jnp.sum(row_exchange(2, vec[4], during_row2), axis=0)
    gather_send(*range(6, 2 + NH))
    f_out[...] = (nx2 - row2) * (EPS * LN2) - EPS * jnp.log(r)
    col_step(smass / r)
    cs = jnp.sum(col_exchange(2, vec[5], during_col2), axis=0)
    kvec[0] = tmass / cs
    for kind in range(2):
        remote(kvec.at[0], kvec.at[1 + kind], ks_sem.at[kind], kr_sem.at[kind], mates[kind])
    gather_spread(*range(6, 2 + NH))
    g_out[...] = (ny2 - col2) * (EPS * LN2) - EPS * jnp.log(cs)

    v = tmass / cs
    for a in range(BLK):
        acc = None
        for k in range(BLK):
            q = (score[a, :, lanes(k)] * v[k:k + 1, :]).astype(jnp.bfloat16)
            weights[pl.ds(a * LANES, LANES), lanes(k)] = q
            q = q.astype(jnp.float32)
            acc = q if acc is None else acc + q
        tmp4[a // 2, pl.ds(a % 2, 1), :] = jnp.sum(acc.T, axis=0, keepdims=True)

    def project(ch):
        p = jnp.dot(weights[...], teach[:, ch * LANES:(ch + 2) * LANES], preferred_element_type=jnp.float32)
        part[ch] = p[:, :LANES].reshape(NX, NZ, ROWS, LANES)
        part[ch + 1] = p[:, LANES:].reshape(NX, NZ, ROWS, LANES)

    def project_one(ch):
        p = jnp.dot(weights[...], teach[:, lanes(ch)], preferred_element_type=jnp.float32)
        part[ch] = p.reshape(NX, NZ, ROWS, LANES)

    lo, hi = pl.ds(0, 4), pl.ds(4, 4)
    xr, xl = at_tgt(1, 0), at_tgt(-1, 0)
    zr, zl = at_tgt(0, 1), at_tgt(0, -1)

    def a_start(i, ch):
        remote(part.at[ch, xi[2], lo], xfar.at[i, 0], as_sem.at[i], ar_sem.at[i, 0], xr)
        remote(part.at[ch, xi[2], hi], xfar.at[i, 1], as_sem.at[i], ar_sem.at[i, 1], xl)

    def a_own(i, ch):
        remote(part.at[ch, xi[1], hi], xnear.at[i, 0, hi], as_sem.at[i], ar_sem.at[i, 2], xr)
        remote(part.at[ch, xi[3], lo], xnear.at[i, 1, lo], as_sem.at[i], ar_sem.at[i, 3], xl)

    def a_pass(i, ch, way):
        dev, dst, half = ((xr, xi[1], lo), (xl, xi[3], hi))[way]
        arrive(xfar.at[i, way], ar_sem.at[i, way])
        part[ch, dst, half] = part[ch, dst, half] + xfar[i, way]
        remote(part.at[ch, dst, half], xnear.at[i, way, half], as_sem.at[i], ar_sem.at[i, 2 + way], dev)

    def a_mid(i, ch):
        arrive(xnear.at[i, 0], ar_sem.at[i, 2])
        arrive(xnear.at[i, 1], ar_sem.at[i, 3])
        asum[i] = part[ch, x] + xnear[i, 0] + xnear[i, 1]
        z_start(i, ch)

    def a_ring(i, ch, step, way):
        dev, dst = ((zr, zi[4 - step]), (zl, zi[4 + step]))[way]
        if step == 1:
            arrive(zfar.at[i, way], zr_sem.at[i, way, 0])
            half = pl.ds(16 * way, 16)
            asum[i, dst, half] = asum[i, dst, half] + zfar[i, way]
        else:
            arrive(znear.at[i, way, step - 2], zr_sem.at[i, way, step - 1])
            asum[i, dst] = asum[i, dst] + znear[i, way, step - 2]
        remote(asum.at[i, dst], znear.at[i, way, step - 1], zs_sem.at[i], zr_sem.at[i, way, step], dev)

    def finish(ch, value):
        scale = rcol[lax.div(z, 4), pl.ds(lax.rem(z, 4) * ROWS, ROWS), :]
        out[:, lanes(ch)] = (value * scale).astype(jnp.bfloat16)

    def a_end(i, ch):
        arrive(znear.at[i, 0, 2], zr_sem.at[i, 0, 3])
        arrive(znear.at[i, 1, 2], zr_sem.at[i, 1, 3])
        finish(ch, asum[i, z] + znear[i, 0, 2] + znear[i, 1, 2])

    ends = (pl.ds(0, 2), pl.ds(2, 2))

    def b_start(i, ch):
        for way, dev in ((0, zr), (1, zl)):
            remote(part.at[ch, ends[way], zi[4]], bfar.at[i, way], bs_sem.at[i], br_sem.at[i, way, 0], dev)

    def b_own(i, ch):
        for way, dev, near in ((0, zr, zi[3]), (1, zl, zi[5])):
            own = 1 - way
            remote(part.at[ch, ends[own], near], bnear.at[i, way, 0, ends[own]], bs_sem.at[i], br_sem.at[i, way, 1], dev)

    def b_ring(i, ch, step, way):
        dev, dst = ((zr, zi[4 - step]), (zl, zi[4 + step]))[way]
        if step == 1:
            arrive(bfar.at[i, way], br_sem.at[i, way, 0])
            part[ch, ends[way], dst] = part[ch, ends[way], dst] + bfar[i, way]
            remote(part.at[ch, ends[way], dst], bnear.at[i, way, 0, ends[way]], bs_sem.at[i], br_sem.at[i, way, 1], dev)
        else:
            arrive(bnear.at[i, way, step - 2], br_sem.at[i, way, step - 1])
            part[ch, :, dst] = part[ch, :, dst] + bnear[i, way, step - 2]
            remote(part.at[ch, :, dst], bnear.at[i, way, step - 1], bs_sem.at[i], br_sem.at[i, way, step], dev)

    def b_mid(i, ch):
        arrive(bnear.at[i, 0, 2], br_sem.at[i, 0, 3])
        arrive(bnear.at[i, 1, 2], br_sem.at[i, 1, 3])
        bsum[i] = part[ch, :, z] + bnear[i, 0, 2] + bnear[i, 1, 2]
        for d in (2, 1, 3):
            remote(bsum.at[i, xi[d]], bx.at[i, d - 1], bxs_sem.at[i], bxr_sem.at[i], at_tgt(d, 0))

    def b_end(i, ch):
        arrive(bx.at[i], bxr_sem.at[i])
        finish(ch, bsum[i, x] + bx[i, 0] + bx[i, 1] + bx[i, 2])

    def h_start(n, ch):
        kind = n % 2
        for part_at, xb in enumerate((x, mate_x[1 - kind])):
            p = jnp.dot(weights[pl.ds(xb * 256, 256), :], teach[:, lanes(ch)], preferred_element_type=jnp.float32)
            p = p + jnp.dot(pweights[kind, pl.ds(part_at * 256, 256), :], pteach[n], preferred_element_type=jnp.float32)
            if part_at == 0:
                asum[NA + n] = p.reshape(NZ, ROWS, LANES)
            else:
                hsend[n] = p.reshape(NZ, ROWS, LANES)
        remote(hsend.at[n], hrecv.at[n], hs_sem.at[n], hr_sem.at[n], mates[1 - kind])

    def z_start(i, ch):
        if ch in DIRECT:
            for d in (4, 3, 5, 2, 6, 1, 7):
                remote(asum.at[i, zi[d]], zall.at[DIRECT.index(ch), d - 1], zs_sem.at[i], zr_sem.at[i, 0, 0], at_tgt(0, d))
        else:
            remote(asum.at[i, zi[4], pl.ds(0, 16)], zfar.at[i, 0], zs_sem.at[i], zr_sem.at[i, 0, 0], zr)
            remote(asum.at[i, zi[4], pl.ds(16, 16)], zfar.at[i, 1], zs_sem.at[i], zr_sem.at[i, 1, 0], zl)

    def a_direct(i, ch):
        n = DIRECT.index(ch)
        arrive(zall.at[n], zr_sem.at[i, 0, 0])
        total = asum[i, z]
        for d in range(7):
            total = total + zall[n, d]
        finish(ch, total)

    def h_mid(n, ch):
        arrive(hrecv.at[n], hr_sem.at[n])
        asum[NA + n] = asum[NA + n] + hrecv[n]
        z_start(NA + n, ch)

    def q_start():
        for d in (2, 1, 3):
            remote(tmp4.at[xi[d]], qbuf.at[d - 1], qs_sem.at[0], qr_sem.at[0], at_tgt(d, 0))

    def q_mid():
        arrive(qbuf.at[pl.ds(0, 3)], qr_sem.at[0])
        tmp4[x] = tmp4[x] + qbuf[0] + qbuf[1] + qbuf[2]
        for d in (4, 3, 5, 2, 6, 1, 7):
            remote(tmp4.at[x], qbuf.at[2 + d], qs_sem.at[1], qr_sem.at[1], at_tgt(0, d))

    def q_end():
        arrive(qbuf.at[pl.ds(3, 7)], qr_sem.at[1])
        total = tmp4[x]
        for d in range(7):
            total = total + qbuf[3 + d]
        rcol[0] = col_form(1.0 / total[0:1, :])
        rcol[1] = col_form(1.0 / total[1:2, :])

    steps = dict(ad=a_direct, hm=h_mid, ap=a_pass, am=a_mid, ar=a_ring, ae=a_end, br=b_ring, bm=b_mid, be=b_end)
    ready = set()
    q_start()
    for name, ch, *rest in SCHEDULE:
        if name == "qm":
            q_mid()
        elif name == "qe":
            q_end()
        elif name == "hw":
            mate_weights()
        elif name == "hf":
            gather_share(6 + 2 * ch, 7 + 2 * ch)
        elif name == "ht":
            take(4 + 2 * ch)
            take(5 + 2 * ch)
        elif name == "ao":
            a_own(KINDS[:ch].count("A"), ch)
        elif name == "bo":
            b_own(KINDS[:ch].count("B"), ch)
        elif name == "s" and KINDS[ch] == "H":
            h_start(KINDS[:ch].count("H"), ch)
        elif name == "s":
            if ch < 2:
                project_one(ch)
            elif ch // 2 not in ready:
                ready.add(ch // 2)
                project(ch // 2 * 2)
            (a_start if KINDS[ch] == "A" else b_start)(KINDS[:ch].count(KINDS[ch]), ch)
        elif KINDS[ch] == "H" and name in ("ar", "ae", "ad"):
            steps[name](NA + KINDS[:ch].count("H"), ch, *rest)
        else:
            steps[name](KINDS[:ch].count(KINDS[ch]), ch, *rest)

    for e in range(3):
        arrive(rbuf.at[e, pl.ds(0, 31)], rs_sem.at[e])
        arrive(cbuf.at[e, pl.ds(0, 7)], cs_sem.at[e])
    arrive(qbuf.at[pl.ds(0, 3)], qs_sem.at[0])
    arrive(qbuf.at[pl.ds(3, 7)], qs_sem.at[1])
    for i, ch in enumerate(chunks_of("A")):
        arrive(part.at[ch, pl.ds(0, 3)], as_sem.at[i])
    for i in range(NA + NH):
        arrive(asum.at[i, pl.ds(0, 7)], zs_sem.at[i])
    for n in range(NH):
        arrive(hsend.at[n], hs_sem.at[n])
    for u in range(2 + NH):
        if shared(u):
            arrive(stage.at[u, 0], gs_sem.at[u])
            arrive(gath.at[u, 0, pl.ds(0, 3)], ys_sem.at[u])
        else:
            arrive(stage.at[u], gs_sem.at[u])
        arrive(stage.at[u], ds_sem.at[u])
    for kind in range(4):
        arrive(kvec.at[0], ks_sem.at[kind])
    for i, ch in enumerate(chunks_of("B")):
        arrive(part.at[ch, :, pl.ds(0, 7)], bs_sem.at[i])
        arrive(bx.at[i], bxs_sem.at[i])


def settle(*refs):
    sem = refs[-1]
    copies = [pltpu.make_async_copy(refs[n], refs[3 + n], sem.at[n]) for n in range(3)]
    for copy in copies:
        copy.start()
    for copy in copies:
        copy.wait()


def body(source_features, target_features, source_logmass, target_logmass, teacher_rows):
    na, nb, nz = NA, KINDS.count("B"), NA + NH
    f32 = jnp.float32
    vmem = pl.BlockSpec(memory_space=pltpu.VMEM)
    dma = pltpu.SemaphoreType.DMA
    projected, f, g = pl.pallas_call(
        functools.partial(kernel, source_features.shape[1]),
        out_shape=(
            jax.ShapeDtypeStruct((ROWS, CHUNKS * LANES), jnp.bfloat16),
            jax.ShapeDtypeStruct((BLK, LANES), f32),
            jax.ShapeDtypeStruct((BLK, LANES), f32),
        ),
        in_specs=[pl.BlockSpec(memory_space=pltpu.HBM)] * 5,
        out_specs=(vmem, vmem, vmem),
        scratch_shapes=[
            pltpu.VMEM(source_features.shape, source_features.dtype),
            pltpu.VMEM(target_features.shape, target_features.dtype),
            pltpu.VMEM((BLK, LANES), f32),
            pltpu.VMEM((BLK, LANES), f32),
            pltpu.VMEM((BLK, LANES, TILE), f32),
            pltpu.VMEM((BLK, LANES, LANES), f32),
            pltpu.VMEM((TILE, TILE), jnp.bfloat16),
            pltpu.VMEM((TILE, CHUNKS * LANES), jnp.bfloat16),
            pltpu.VMEM((CHUNKS, NX, NZ, ROWS, LANES), f32),
            pltpu.VMEM((3, 32, BLK, LANES), f32),
            pltpu.VMEM((3, 8, BLK, LANES), f32),
            pltpu.VMEM((7, BLK, LANES), f32),
            pltpu.VMEM((NX, 2, LANES), f32),
            pltpu.VMEM((10, 2, LANES), f32),
            pltpu.VMEM((na, 2, 4, ROWS, LANES), f32),
            pltpu.VMEM((na, 2, NZ, ROWS, LANES), f32),
            pltpu.VMEM((nz, NZ, ROWS, LANES), f32),
            pltpu.VMEM((nz, 2, ROWS // 2, LANES), f32),
            pltpu.VMEM((nz, 2, 3, ROWS, LANES), f32),
            pltpu.VMEM((nb, 2, 2, ROWS, LANES), f32),
            pltpu.VMEM((nb, 2, 3, NX, ROWS, LANES), f32),
            pltpu.VMEM((nb, NX, ROWS, LANES), f32),
            pltpu.VMEM((nb, 3, ROWS, LANES), f32),
            pltpu.VMEM((2, LANES, LANES), f32),
            dma, dma((4,)), dma((3,)), dma((3,)), dma((3,)), dma((3,)), dma((2,)), dma((2,)),
            dma((na,)), dma((na, 4)), dma((nz,)), dma((nz, 2, 4)),
            dma((nb,)), dma((nb, 2, 4)), dma((nb,)), dma((nb,)),
            pltpu.VMEM((max(1, len(DIRECT)), 7, ROWS, LANES), f32),
            pltpu.VMEM((2 + NH, 4, LANES, LANES), f32),
            pltpu.VMEM((2 + NH, 2, 4, LANES, LANES), f32),
            pltpu.VMEM((2, HALF, TILE), f32),
            pltpu.VMEM((2, HALF, TILE), jnp.bfloat16),
            pltpu.VMEM((NH, TILE, LANES), jnp.bfloat16),
            pltpu.VMEM((6, BLK, LANES), f32),
            pltpu.VMEM((NH, NZ, ROWS, LANES), f32),
            pltpu.VMEM((NH, NZ, ROWS, LANES), f32),
            dma((2 + NH,)), dma((2 + NH,)), dma((2 + NH,)), dma((2 + NH,)), dma((2 + NH,)), dma((2 + NH,)), dma((4,)), dma((4,)), dma((NH,)), dma((NH,)),
        ],
        compiler_params=pltpu.CompilerParams(
            collective_id=0, has_side_effects=True, vmem_limit_bytes=(64 * 1024 - 192) * 1024),
    )(source_features, target_features, source_logmass.reshape(BLK, LANES),
      target_logmass.reshape(BLK, LANES), teacher_rows)
    return pl.pallas_call(
        settle,
        out_shape=(
            jax.ShapeDtypeStruct(projected.shape, jnp.bfloat16),
            jax.ShapeDtypeStruct((TILE,), f32),
            jax.ShapeDtypeStruct((TILE,), f32),
        ),
        in_specs=[vmem] * 3,
        out_specs=(pl.BlockSpec(memory_space=pl.ANY),) * 3,
        scratch_shapes=[dma((3,))],
    )(projected, f.reshape(TILE), g.reshape(TILE))


def solution(mesh):
    in_specs = (P("src", None), P("tgt", None), P("src"), P("tgt"), P("tgt", None))
    out_specs = (P(("src", "tgt"), None), P("src"), P("tgt"))
    return jax.shard_map(body, mesh=mesh, in_specs=in_specs, out_specs=out_specs, check_vma=False)
```
